32 devices in a mesh: dp: 4 (over y, x), ctx: 2 (over core), wt: 4 (over z).
Axes of the slice: x: 2, y: 2, z: 4, core: 2. Of those that a mesh axis runs over, the one named last changes fastest.
Arguments:
- tokens: bfloat16 [16, 2048, 1600], P(('dp', 'wt'), 'ctx'), may hold values from -6 to 6
- cotangent: bfloat16 [16, 2048, 1600], P(('dp', 'wt'), 'ctx'), may hold values from -6 to 6
- doc_lengths: int32 [16, 4], P(('dp', 'wt')), may hold values from 1 to 2045, as said below
- adapter_ids: int32 [16, 1], P(('dp', 'wt')), may hold values from 0 to 7
- first_gain: bfloat16 [1600], P('wt'), may hold values from 0.5 to 1.5
- first_shift: bfloat16 [1600], P('wt'), may hold values from -1 to 1
- qkv_weight: bfloat16 [1600, 4800], P('wt'), may hold values from -0.21875 to 0.21875
- qkv_bias: bfloat16 [4800], P('wt'), may hold values from -1 to 1
- out_weight: bfloat16 [1600, 1600], P('wt'), may hold values from -0.875 to 0.875
- out_bias: bfloat16 [1600], P('wt'), may hold values from -1 to 1
- second_gain: bfloat16 [1600], P('wt'), may hold values from 0.5 to 1.5
- second_shift: bfloat16 [1600], P('wt'), may hold values from -1 to 1
- up_weight: bfloat16 [1600, 6400], P('wt'), may hold values from -0.15625 to 0.15625
- up_bias: bfloat16 [6400], P('wt'), may hold values from -1 to 1
- down_weight: bfloat16 [6400, 1600], P('wt'), may hold values from -0.078125 to 0.078125
- down_bias: bfloat16 [1600], P('wt'), may hold values from -1 to 1
- qkv_adapt_in: bfloat16 [8, 16, 1600], replicated, may hold values from -0.15625 to 0.15625
- qkv_adapt_out: bfloat16 [8, 16, 4800], replicated, may hold values from -0.75 to 0.75
- out_adapt_in: bfloat16 [8, 16, 1600], replicated, may hold values from -0.875 to 0.875
- out_adapt_out: bfloat16 [8, 16, 1600], replicated, may hold values from -0.75 to 0.75
- up_adapt_in: bfloat16 [8, 16, 1600], replicated, may hold values from -0.15625 to 0.15625
- up_adapt_out: bfloat16 [8, 16, 6400], replicated, may hold values from -0.75 to 0.75
- down_adapt_in: bfloat16 [8, 16, 6400], replicated, may hold values from -0.078125 to 0.078125
- down_adapt_out: bfloat16 [8, 16, 1600], replicated, may hold values from -0.75 to 0.75
Outputs:
- output: bfloat16 [16, 2048, 1600], P(('dp', 'wt'), 'ctx')
- grad_tokens: float32 [16, 2048, 1600], P(('dp', 'wt'), 'ctx')
- grad_qkv_in: float32 [8, 16, 1600], replicated
- grad_qkv_out: float32 [8, 16, 4800], replicated
- grad_out_in: float32 [8, 16, 1600], replicated
- grad_out_out: float32 [8, 16, 1600], replicated
- grad_up_in: float32 [8, 16, 1600], replicated
- grad_up_out: float32 [8, 16, 6400], replicated
- grad_down_in: float32 [8, 16, 6400], replicated
- grad_down_out: float32 [8, 16, 1600], replicated
The draws below stay inside these ranges and needn't reach their ends.
Inputs may be any that keep to these rules, and one draw needn't show every extreme that they name: `doc_lengths`: each row sums to 2048. `adapter_ids`: every adapter is the adapter of some sequence.
All inputs are finite; a program needn't handle non-finite values.
Results may differ from the reference program's by a relative error of at most 0.015.
The reference program's roundings to bfloat16 on the way count: a program that leaves them out, or rounds other values in their place, can miss the bound.
Values may be sent and summed in bfloat16 or wider, within the bound.
No kernel may reach another device: no remote copies, remote signals or barrier semaphores. Data moves between devices by JAX's collectives and lax.ppermute only.
A program may use at most 320 MiB of HBM per device.

```python
import jax
import jax.numpy as jnp
from jax import lax

D = 1600
HEADS = 25
HEAD_DIM = 64
FF = 6400
RANK = 16
ADAPTERS = 8
WINDOW = 1024
LENGTH = 2048
TOK_DEV = 1024
NSEQ = 16


def draw_doc_lengths(key, part):
    key = jax.random.fold_in(key, 17)
    first_key, second_key, third_key, fourth_key = jax.random.split(key, 4)
    leading = jax.random.randint(first_key, (NSEQ,), 1, TOK_DEV // 2 + 1)
    trailing = jax.random.randint(second_key, (NSEQ,), 2, TOK_DEV // 2 + 1)
    spread = jax.random.randint(third_key, (NSEQ,), 0, 1 << 20)
    special = jax.random.randint(fourth_key, (), 0, NSEQ)
    marked = jnp.arange(NSEQ, dtype=jnp.int32) == special
    leading = jnp.where(marked, 1, leading)
    trailing = jnp.where(marked, 2, trailing)
    before_last = spread % (trailing - 1) + 1
    last_piece = trailing - before_last
    middle = LENGTH - leading - trailing
    return jnp.stack([leading, middle, before_last, last_piece], axis=1).astype(jnp.int32)


def shard_levels(stream_key, shape, pieces, low, top_value):
    loudness, own = 1.0, jax.random.fold_in(stream_key, 6)
    for position, shards_of in pieces:
        heights = jnp.exp(jax.random.uniform(jax.random.fold_in(own, position), (shards_of,), jnp.float32, low / len(pieces), top_value / len(pieces)))
        loudness = loudness * jnp.repeat(heights, shape[position] // shards_of).reshape([-1 if axis == position else 1 for axis in range(len(shape))])
    return loudness


def different_ones(rng, rows, count, top, lift):
    sequence = jax.random.permutation(jax.random.fold_in(rng, 1), count)
    boost = sequence
    for power in range(3):
        boost = boost * boost // count
    boost = boost * lift // count
    tickets = jax.random.randint(jax.random.fold_in(rng, 2), (rows, count), 0, 4096) + boost
    fixed_rows = jax.random.permutation(jax.random.fold_in(rng, 3), rows)[jnp.arange(count) % rows]
    tickets = jnp.where(jnp.arange(rows)[:, None] == fixed_rows[None, :], 1 << 14, tickets)
    merit = tickets * count + jnp.arange(count)
    return lax.top_k(merit.astype(jnp.int32), top)[1].astype(jnp.int32)


def normal_values(key, dims, width, bound, cuts=(), kind=jnp.bfloat16):
    factor_of = shard_levels(key, dims, cuts, -0.22, 0.18) if cuts else 1.0
    drawn = jax.random.normal(key, dims, jnp.float32) * width * factor_of
    return jnp.minimum(jnp.maximum(drawn, -bound), bound).astype(kind)


def setup_inputs(seed: int = 0) -> dict:
    arg_keys = jax.random.split(jax.random.key(seed), 25)
    tokens = normal_values(arg_keys[0], (NSEQ, LENGTH, D), 1.0, 6.0, ((0, 16), (1, 2)))
    cotangent = normal_values(arg_keys[1], (NSEQ, LENGTH, D), 1.0, 6.0, ((0, 16), (1, 2)))
    doc_lengths = draw_doc_lengths(jax.random.fold_in(arg_keys[24], 71), 0)
    adapter_ids = different_ones(arg_keys[3], NSEQ, ADAPTERS, 1, 0)
    first_gain = jnp.clip(1.0 + 0.1 * jax.random.normal(arg_keys[4], (D,), jnp.float32), 0.5, 1.5).astype(jnp.bfloat16)
    first_shift = normal_values(arg_keys[5], (D,), 0.2, 1.0, ((0, 4),))
    qkv_weight = normal_values(arg_keys[6], (D, 3 * D), (D // 2) ** -0.5, 0.21875, ((0, 4),))
    qkv_bias = normal_values(arg_keys[7], (3 * D,), 0.2, 1.0, ((0, 4),))
    out_weight = normal_values(arg_keys[8], (D, D), (D // 32) ** -0.5, 0.875, ((0, 4),))
    out_bias = normal_values(arg_keys[9], (D,), 0.2, 1.0, ((0, 4),))
    second_gain = jnp.clip(1.0 + 0.1 * jax.random.normal(arg_keys[10], (D,), jnp.float32), 0.5, 1.5).astype(jnp.bfloat16)
    second_shift = normal_values(arg_keys[11], (D,), 0.2, 1.0, ((0, 4),))
    up_weight = normal_values(arg_keys[12], (D, FF), D ** -0.5, 0.15625, ((0, 4),))
    up_bias = normal_values(arg_keys[13], (FF,), 0.2, 1.0, ((0, 4),))
    down_weight = normal_values(arg_keys[14], (FF, D), FF ** -0.5, 0.078125, ((0, 4),))
    down_bias = normal_values(arg_keys[15], (D,), 0.2, 1.0, ((0, 4),))
    qkv_adapt_in = normal_values(arg_keys[16], (ADAPTERS, RANK, D), D ** -0.5, 0.15625)
    qkv_adapt_out = normal_values(arg_keys[17], (ADAPTERS, RANK, 3 * D), (4 * RANK) ** -0.5, 0.75)
    out_adapt_in = normal_values(arg_keys[18], (ADAPTERS, RANK, D), (D // 32) ** -0.5, 0.875)
    out_adapt_out = normal_values(arg_keys[19], (ADAPTERS, RANK, D), (4 * RANK) ** -0.5, 0.75)
    up_adapt_in = normal_values(arg_keys[20], (ADAPTERS, RANK, D), D ** -0.5, 0.15625)
    up_adapt_out = normal_values(arg_keys[21], (ADAPTERS, RANK, FF), (4 * RANK) ** -0.5, 0.75)
    down_adapt_in = normal_values(arg_keys[22], (ADAPTERS, RANK, FF), FF ** -0.5, 0.078125)
    down_adapt_out = normal_values(arg_keys[23], (ADAPTERS, RANK, D), (4 * RANK) ** -0.5, 0.75)
    return dict(tokens=tokens, cotangent=cotangent, doc_lengths=doc_lengths, adapter_ids=adapter_ids, first_gain=first_gain, first_shift=first_shift, qkv_weight=qkv_weight, qkv_bias=qkv_bias, out_weight=out_weight, out_bias=out_bias, second_gain=second_gain, second_shift=second_shift, up_weight=up_weight, up_bias=up_bias, down_weight=down_weight, down_bias=down_bias, qkv_adapt_in=qkv_adapt_in, qkv_adapt_out=qkv_adapt_out, out_adapt_in=out_adapt_in, out_adapt_out=out_adapt_out, up_adapt_in=up_adapt_in, up_adapt_out=up_adapt_out, down_adapt_in=down_adapt_in, down_adapt_out=down_adapt_out)


EPSILON = 1e-05
HIGHEST = lax.Precision.HIGHEST

@jax.custom_vjp
def low(v):
    return lax.optimization_barrier(v.astype(jnp.bfloat16)).astype(jnp.float32)

@jax.custom_vjp
def low_back(v):
    return v

def low_keep(v):
    return (low(v), None)

def low_pass(kept, grad):
    return (grad,)

def back_keep(v):
    return (v, None)

def back_low(kept, grad):
    return (low(grad),)
low.defvjp(low_keep, low_pass)
low_back.defvjp(back_keep, back_low)

def rounded(values):
    return low(low_back(values))

def matmul(left_side, right_side):
    return jnp.dot(left_side, right_side, precision=HIGHEST)

def matmul_transposed(left_side, right_side):
    return lax.dot_general(left_side, right_side, (((1,), (1,)), ((), ())), precision=HIGHEST)

def layer_norm(values, norm_gain, norm_shift):
    center = values - lax.optimization_barrier(jnp.mean(values, axis=-1, keepdims=True))
    inverse = lax.rsqrt(lax.optimization_barrier(jnp.mean(center * center, axis=-1, keepdims=True)) + EPSILON)
    return center * inverse * norm_gain + norm_shift

def document_index(positions, lengths):
    bounds = jnp.cumsum(lengths).astype(jnp.int32)[:-1]
    return lax.optimization_barrier(jnp.sum((positions[:, None] >= bounds[None, :]).astype(jnp.int32), axis=1)).astype(jnp.int32)

def block_mask(query_pos, key_pos, lengths):
    query_doc = document_index(query_pos, lengths)
    key_doc = document_index(key_pos, lengths)
    distance = query_pos[:, None] - key_pos[None, :]
    same_doc = query_doc[:, None] == key_doc[None, :]
    return (key_pos[None, :] >= 0) & same_doc & (distance >= 0) & (distance < WINDOW)

def attention(qkv, lengths):
    row_count = qkv.shape[0]
    block_rows = min(512, row_count)
    key_rows = WINDOW + block_rows
    queries = qkv[:, :D]
    key_all = jnp.pad(qkv[:, D:2 * D], ((WINDOW, 0), (0, 0)))
    value_all = jnp.pad(qkv[:, 2 * D:], ((WINDOW, 0), (0, 0)))
    factor = HEAD_DIM ** (-0.5)

    def one_block(block_index):
        row_start = (block_index * block_rows).astype(jnp.int32)
        query_part = lax.dynamic_slice_in_dim(queries, row_start, block_rows, 0).reshape(block_rows, HEADS, HEAD_DIM)
        key_part = lax.dynamic_slice_in_dim(key_all, row_start, key_rows, 0).reshape(key_rows, HEADS, HEAD_DIM)
        value_part = lax.dynamic_slice_in_dim(value_all, row_start, key_rows, 0).reshape(key_rows, HEADS, HEAD_DIM)
        query_pos = row_start + jnp.arange(block_rows, dtype=jnp.int32)
        key_pos = row_start - WINDOW + jnp.arange(key_rows, dtype=jnp.int32)
        allowed = block_mask(query_pos, key_pos, lengths)
        products = jnp.einsum('qhd,khd->hqk', query_part, key_part, precision=HIGHEST)
        scores = jnp.where(allowed[None], low_back(products) * factor, -1e+30)
        chances = jax.nn.softmax(scores, axis=-1)
        combined = jnp.einsum('hqk,khd->qhd', low(chances), value_part, precision=HIGHEST)
        return combined.reshape(block_rows, D)
    blocks = lax.map(jax.checkpoint(one_block), jnp.arange(row_count // block_rows, dtype=jnp.int32))
    return blocks.reshape(row_count, D)

def layer(values, lengths, frozen, adapters):
    first_gain, first_shift, qkv_weight, qkv_bias, out_weight, out_bias, second_gain, second_shift, up_weight, up_bias, down_weight, down_bias = frozen
    qkv_in, qkv_out, proj_in, proj_out, up_in, up_out, down_in, down_out = adapters
    first_in = low(layer_norm(values, first_gain, first_shift))
    qkv_low = rounded(matmul_transposed(first_in, qkv_in))
    qkv = rounded(matmul(first_in, qkv_weight) + qkv_bias + matmul(qkv_low, qkv_out))
    attended = rounded(attention(qkv, lengths))
    out_low = rounded(matmul_transposed(attended, proj_in))
    branch = low_back(matmul(attended, out_weight) + out_bias + matmul(out_low, proj_out))
    hidden = values + branch
    second_in = low(layer_norm(hidden, second_gain, second_shift))
    up_low = rounded(matmul_transposed(second_in, up_in))
    upper_sum = low_back(matmul(second_in, up_weight) + up_bias + matmul(up_low, up_out))
    active = rounded(jax.nn.gelu(upper_sum, approximate=True))
    down_low = rounded(matmul_transposed(active, down_in))
    return hidden + (matmul(active, down_weight) + down_bias + matmul(down_low, down_out))

def reference(tokens, cotangent, doc_lengths, adapter_ids, first_gain, first_shift, qkv_weight, qkv_bias, out_weight, out_bias, second_gain, second_shift, up_weight, up_bias, down_weight, down_bias, qkv_adapt_in, qkv_adapt_out, out_adapt_in, out_adapt_out, up_adapt_in, up_adapt_out, down_adapt_in, down_adapt_out):
    frozen = tuple((element.astype(jnp.float32) for element in (first_gain, first_shift, qkv_weight, qkv_bias, out_weight, out_bias, second_gain, second_shift, up_weight, up_bias, down_weight, down_bias)))
    stacks = tuple((element.astype(jnp.float32) for element in (qkv_adapt_in, qkv_adapt_out, out_adapt_in, out_adapt_out, up_adapt_in, up_adapt_out, down_adapt_in, down_adapt_out)))

    def one_sequence(totals, inputs):
        values, upstream, lengths, chosen = inputs
        picked = tuple((lax.dynamic_index_in_dim(stacked, chosen, 0, keepdims=False) for stacked in stacks))

        def forward(inner_values, inner_adapters):
            return layer(inner_values, lengths, frozen, inner_adapters)
        result, pullback = jax.vjp(forward, values.astype(jnp.float32), picked)
        grad_values, grad_adapters = pullback(upstream.astype(jnp.float32))
        totals = tuple((summed.at[chosen].add(gradient) for summed, gradient in zip(totals, grad_adapters)))
        return (totals, (result.astype(jnp.bfloat16), grad_values))
    starting = tuple((jnp.zeros(stacked.shape, jnp.float32) for stacked in stacks))
    totals, (output, grad_tokens) = lax.scan(one_sequence, starting, (tokens, cotangent, doc_lengths, adapter_ids[:, 0].astype(jnp.int32)))
    return (output, grad_tokens, totals[0], totals[1], totals[2], totals[3], totals[4], totals[5], totals[6], totals[7])
```

```python
from functools import partial

import jax
import jax.numpy as jnp
from jax import lax
from jax.experimental import pallas as pl
from jax.experimental.pallas import tpu as pltpu
from jax.sharding import PartitionSpec as P

HEADS = 25
HEAD_DIM = 64
ADAPTERS = 8
WINDOW = 1024


EPSILON = 1e-05
MASKED = -1e30


def shifted(array, axis, by):
    devices = lax.axis_size(axis)
    pairs = [(i, i + by) for i in range(devices) if 0 <= i + by < devices]
    return lax.ppermute(array, axis, pairs)


def product(left_side, right_side):
    return jnp.dot(left_side, right_side, preferred_element_type=jnp.float32)


def product_transposed(left_side, right_side):
    return lax.dot_general(
        left_side, right_side, (((1,), (1,)), ((), ())), preferred_element_type=jnp.float32
    )


def product_outer(left_side, right_side):
    return lax.dot_general(
        left_side, right_side, (((0,), (0,)), ((), ())), preferred_element_type=jnp.float32
    )


def norm_forward(values, norm_gain, norm_shift):
    center = values - jnp.mean(values, axis=-1, keepdims=True)
    inverse = lax.rsqrt(jnp.mean(center * center, axis=-1, keepdims=True) + EPSILON)
    normed = center * inverse
    return (normed * norm_gain + norm_shift, normed, inverse)


def norm_backward(upstream, normed, inverse, norm_gain):
    scaled = upstream * norm_gain
    return inverse * (
        scaled
        - jnp.mean(scaled, axis=-1, keepdims=True)
        - normed * jnp.mean(scaled * normed, axis=-1, keepdims=True)
    )


TILE = 256
REACH_TILES = WINDOW // TILE
SPAN_TILES = REACH_TILES + 1
PAIRS = (HEADS + 1) // 2
PADDED = PAIRS * 128
FACTOR = HEAD_DIM ** (-0.5)


def split_pair(pair):
    lane = lax.broadcasted_iota(jnp.int32, pair.shape, 1)
    zero = jnp.zeros_like(pair)
    return jnp.concatenate(
        [jnp.where(lane < HEAD_DIM, pair, zero), jnp.where(lane >= HEAD_DIM, pair, zero)], axis=0
    )


def join_pair(stacked):
    lane = lax.broadcasted_iota(jnp.int32, (TILE, 128), 1)
    return jnp.where(lane < HEAD_DIM, stacked[:TILE], stacked[TILE:])


def tile_bias(bounds, query_start, key_start):
    rows = query_start + lax.broadcasted_iota(jnp.int32, (TILE, 1), 0)
    columns = key_start + lax.broadcasted_iota(jnp.int32, (1, TILE), 1)
    row_doc = sum((rows >= bound).astype(jnp.int32) for bound in bounds)
    column_doc = sum((columns >= bound).astype(jnp.int32) for bound in bounds)
    shape = (TILE, TILE)
    distance = jnp.broadcast_to(rows, shape) - jnp.broadcast_to(columns, shape)
    same = jnp.broadcast_to(row_doc, shape) == jnp.broadcast_to(column_doc, shape)
    seen = jnp.broadcast_to(columns, shape) >= 0
    return jnp.where(same & seen & (distance >= 0) & (distance < WINDOW), 0.0, MASKED)


def fill_biases(meta, bias_scr, tiles):
    bounds = [meta[place] for place in range(3)]
    first = meta[3]

    def one(step, carry):
        tile = step // SPAN_TILES
        key_tile = tile + lax.rem(step, SPAN_TILES) - REACH_TILES
        bias_scr[step] = tile_bias(bounds, first + tile * TILE, first + key_tile * TILE)
        return carry

    lax.fori_loop(0, tiles * SPAN_TILES, one, 0)


def attend_forward_kernel(tiles, meta, q_ref, k_ref, v_ref, o_ref, lse_ref, bias_scr, acc_scr, va_scr):
    @pl.when(pl.program_id(0) == 0)
    def _():
        fill_biases(meta, bias_scr, tiles)
        va_scr[:, 128:] = jnp.ones((va_scr.shape[0], 128), jnp.bfloat16)

    va_scr[:, :128] = v_ref[...]
    chunk = TILE // 2
    for tile in range(tiles):
        stacked = split_pair(q_ref[pl.ds(tile * TILE, TILE), :] * FACTOR)
        window = pl.ds(tile * TILE, SPAN_TILES * TILE)
        keys = k_ref[window, :]
        values = va_scr[window, :]
        for part in range(2 * TILE // chunk):
            start = part * chunk
            bias_rows = pl.ds(start % TILE, chunk)
            bias = jnp.concatenate(
                [bias_scr[tile * SPAN_TILES + t, bias_rows, :] for t in range(SPAN_TILES)], axis=1
            )
            scores = product_transposed(stacked[start : start + chunk], keys) + bias
            highest = jnp.max(scores, axis=1, keepdims=True)
            mixed = product(jnp.exp(scores - highest).astype(jnp.bfloat16), values)
            summed = mixed[:, 128:]
            acc_scr[pl.ds(start, chunk), :] = mixed[:, :128] / summed
            lse_ref[pl.ds(tile * 2 * TILE + start, chunk), :] = highest + jnp.log(summed)
        o_ref[pl.ds(tile * TILE, TILE), :] = join_pair(acc_scr[...]).astype(jnp.bfloat16)


def attend_forward(meta, queries, keys, values):
    rows, key_rows = queries.shape[0], keys.shape[0]
    tiles = rows // TILE
    column = lambda count: pl.BlockSpec((count, 128), lambda j, m: (0, j))
    return pl.pallas_call(
        partial(attend_forward_kernel, tiles),
        grid_spec=pltpu.PrefetchScalarGridSpec(
            num_scalar_prefetch=1,
            grid=(PAIRS,),
            in_specs=[column(rows), column(key_rows), column(key_rows)],
            out_specs=[column(rows), pl.BlockSpec((None, 2 * rows, 128), lambda j, m: (j, 0, 0))],
            scratch_shapes=[
                pltpu.VMEM((tiles * SPAN_TILES, TILE, TILE), jnp.float32),
                pltpu.VMEM((2 * TILE, 128), jnp.float32),
                pltpu.VMEM((key_rows, 256), jnp.bfloat16),
            ],
        ),
        out_shape=[
            jax.ShapeDtypeStruct((rows, PADDED), jnp.bfloat16),
            jax.ShapeDtypeStruct((PAIRS, 2 * rows, 128), jnp.float32),
        ],
        compiler_params=pltpu.CompilerParams(vmem_limit_bytes=56 << 20),
        name="attend_forward",
    )(meta, queries, keys, values)


def attend_backward_kernel(
    tiles, meta, q_ref, k_ref, v_ref, g_ref, o_ref, lse_ref,
    dq_ref, dk_far_ref, dk_ref, dv_far_ref, dv_ref, bias_scr, dq_scr, dkt, dvt,
):
    @pl.when(pl.program_id(0) == 0)
    def _():
        fill_biases(meta, bias_scr, tiles)

    dkt[...] = jnp.zeros_like(dkt)
    dvt[...] = jnp.zeros_like(dvt)
    for tile in range(tiles):
        rows = pl.ds(tile * TILE, TILE)
        queries = split_pair(q_ref[rows, :] * FACTOR)
        grads = split_pair(g_ref[rows, :])
        mixed = o_ref[rows, :].astype(jnp.float32)
        centered = jnp.sum(
            grads.astype(jnp.float32) * jnp.concatenate([mixed, mixed], axis=0), axis=1, keepdims=True
        )
        lse = lse_ref[pl.ds(tile * 2 * TILE, 2 * TILE), :]
        lse = jnp.concatenate([lse, lse], axis=1)
        queries_t = queries.T
        grads_t = grads.T
        dq_scr[...] = jnp.zeros_like(dq_scr)
        for t in range(SPAN_TILES):
            at = pl.ds((tile + t) * TILE, TILE)
            keys = k_ref[at, :]
            bias = bias_scr[tile * SPAN_TILES + t]
            scores = product_transposed(queries, keys)
            chances = jnp.exp(scores + jnp.concatenate([bias, bias], axis=0) - lse)
            grad_chances = product_transposed(grads, v_ref[at, :])
            grad_scores = (chances * (grad_chances - centered)).astype(jnp.bfloat16)
            dvt[tile + t] += product(grads_t, chances.astype(jnp.bfloat16))
            dkt[tile + t] += product(queries_t, grad_scores)
            dq_scr[...] += product(grad_scores, keys)
        dq_ref[rows, :] = (join_pair(dq_scr[...]) * FACTOR).astype(jnp.bfloat16)
    for t in range(tiles + REACH_TILES):
        if t < REACH_TILES:
            at = pl.ds(t * TILE, TILE)
            dk_far_ref[at, :] = dkt[t].T.astype(jnp.bfloat16)
            dv_far_ref[at, :] = dvt[t].T.astype(jnp.bfloat16)
        else:
            at = pl.ds((t - REACH_TILES) * TILE, TILE)
            dk_ref[at, :] = dkt[t].T
            dv_ref[at, :] = dvt[t].T


def attend_backward(meta, queries, keys, values, grad_mixed, mixed, lse):
    rows, key_rows = queries.shape[0], keys.shape[0]
    tiles = rows // TILE
    column = lambda count: pl.BlockSpec((count, 128), lambda j, m: (0, j))
    out = lambda count, kind: jax.ShapeDtypeStruct((count, PADDED), kind)
    return pl.pallas_call(
        partial(attend_backward_kernel, tiles),
        grid_spec=pltpu.PrefetchScalarGridSpec(
            num_scalar_prefetch=1,
            grid=(PAIRS,),
            in_specs=[
                column(rows), column(key_rows), column(key_rows), column(rows), column(rows),
                pl.BlockSpec((None, 2 * rows, 128), lambda j, m: (j, 0, 0)),
            ],
            out_specs=[column(rows), column(WINDOW), column(rows), column(WINDOW), column(rows)],
            scratch_shapes=[
                pltpu.VMEM((tiles * SPAN_TILES, TILE, TILE), jnp.float32),
                pltpu.VMEM((2 * TILE, 128), jnp.float32),
                pltpu.VMEM((key_rows // TILE, 128, TILE), jnp.float32),
                pltpu.VMEM((key_rows // TILE, 128, TILE), jnp.float32),
            ],
        ),
        out_shape=[
            out(rows, jnp.bfloat16), out(WINDOW, jnp.bfloat16), out(rows, jnp.float32),
            out(WINDOW, jnp.bfloat16), out(rows, jnp.float32),
        ],
        compiler_params=pltpu.CompilerParams(vmem_limit_bytes=56 << 20),
        name="attend_backward",
    )(meta, queries, keys, values, grad_mixed, mixed, lse)


def shards(
    tokens,
    cotangent,
    doc_lengths,
    adapter_ids,
    first_gain,
    first_shift,
    qkv_weight,
    qkv_bias,
    out_weight,
    out_bias,
    second_gain,
    second_shift,
    up_weight,
    up_bias,
    down_weight,
    down_bias,
    qkv_adapt_in,
    qkv_adapt_out,
    out_adapt_in,
    out_adapt_out,
    up_adapt_in,
    up_adapt_out,
    down_adapt_in,
    down_adapt_out,
):
    gathered = (
        lax.all_gather(first_gain, "wt", axis=0, tiled=True),
        lax.all_gather(first_shift, "wt", axis=0, tiled=True),
        lax.all_gather(qkv_weight, "wt", axis=0, tiled=True),
        lax.all_gather(qkv_bias, "wt", axis=0, tiled=True),
        lax.all_gather(out_weight, "wt", axis=0, tiled=True),
        lax.all_gather(out_bias, "wt", axis=0, tiled=True),
        lax.all_gather(second_gain, "wt", axis=0, tiled=True),
        lax.all_gather(second_shift, "wt", axis=0, tiled=True),
        lax.all_gather(up_weight, "wt", axis=0, tiled=True),
        lax.all_gather(up_bias, "wt", axis=0, tiled=True),
        lax.all_gather(down_weight, "wt", axis=0, tiled=True),
        lax.all_gather(down_bias, "wt", axis=0, tiled=True),
    )
    (
        gain_one,
        shift_one,
        weight_qkv,
        bias_qkv,
        weight_out,
        bias_out,
        gain_two,
        shift_two,
        weight_up,
        bias_up,
        weight_down,
        bias_down,
    ) = gathered
    lengths = doc_lengths[0]
    chosen = adapter_ids[0, 0]

    def select(stacked):
        return lax.dynamic_index_in_dim(stacked, chosen, 0, keepdims=False)

    adapter_qkv_in = select(qkv_adapt_in)
    adapter_qkv_out = select(qkv_adapt_out)
    adapter_out_in = select(out_adapt_in)
    adapter_out_out = select(out_adapt_out)
    adapter_up_in = select(up_adapt_in)
    adapter_up_out = select(up_adapt_out)
    adapter_down_in = select(down_adapt_in)
    adapter_down_out = select(down_adapt_out)
    values = tokens[0].astype(jnp.float32)
    row_count, feature_count = values.shape
    first_query = lax.axis_index("ctx") * row_count
    reach = -(-WINDOW // row_count)
    normed_in, normed_one, inverse_one = norm_forward(
        values, gain_one.astype(jnp.float32), shift_one.astype(jnp.float32)
    )
    first_in = normed_in.astype(jnp.bfloat16)
    qkv_low = product_transposed(first_in, adapter_qkv_in).astype(jnp.bfloat16)
    qkv_all = (
        product(first_in, weight_qkv)
        + bias_qkv.astype(jnp.float32)
        + product(qkv_low, adapter_qkv_out)
    ).astype(jnp.bfloat16)
    padding = ((0, 0), (0, PADDED - feature_count))
    queries = jnp.pad(qkv_all[:, :feature_count], padding)
    key_value = jnp.stack(
        [
            jnp.pad(qkv_all[:, feature_count : 2 * feature_count], padding),
            jnp.pad(qkv_all[:, 2 * feature_count :], padding),
        ]
    )
    pieces = []
    for offset in range(reach, 0, -1):
        pieces.append(shifted(key_value, "ctx", offset))
    pieces.append(key_value)
    buffer = jnp.concatenate(pieces, axis=1)
    key_buffer = buffer[0]
    value_buffer = buffer[1]
    meta = jnp.concatenate([jnp.cumsum(lengths)[:3], first_query[None]]).astype(jnp.int32)
    mixed_padded, logsums = attend_forward(meta, queries, key_buffer, value_buffer)
    mixed_low = mixed_padded[:, :feature_count]
    out_low = product_transposed(mixed_low, adapter_out_in).astype(jnp.bfloat16)
    branch = (
        product(mixed_low, weight_out)
        + bias_out.astype(jnp.float32)
        + product(out_low, adapter_out_out)
    )
    hidden = values + branch
    normed_mid, normed_two, inverse_two = norm_forward(
        hidden, gain_two.astype(jnp.float32), shift_two.astype(jnp.float32)
    )
    second_in = normed_mid.astype(jnp.bfloat16)
    up_low = product_transposed(second_in, adapter_up_in).astype(jnp.bfloat16)
    upper_sum = (
        product(second_in, weight_up)
        + bias_up.astype(jnp.float32)
        + product(up_low, adapter_up_out)
    )
    active = jax.nn.gelu(upper_sum, approximate=True).astype(jnp.bfloat16)
    down_low = product_transposed(active, adapter_down_in).astype(jnp.bfloat16)
    output = (
        hidden
        + (
            product(active, weight_down)
            + bias_down.astype(jnp.float32)
            + product(down_low, adapter_down_out)
        )
    ).astype(jnp.bfloat16)
    gain_one, weight_qkv, weight_out, gain_two, weight_up, weight_down = (
        lax.all_gather(first_gain, "wt", axis=0, tiled=True),
        lax.all_gather(qkv_weight, "wt", axis=0, tiled=True),
        lax.all_gather(out_weight, "wt", axis=0, tiled=True),
        lax.all_gather(second_gain, "wt", axis=0, tiled=True),
        lax.all_gather(up_weight, "wt", axis=0, tiled=True),
        lax.all_gather(down_weight, "wt", axis=0, tiled=True),
    )
    upstream = cotangent[0]
    grad_down_out = product_outer(down_low, upstream)
    grad_down_low = product_transposed(upstream, adapter_down_out).astype(jnp.bfloat16)
    grad_down_in = product_outer(grad_down_low, active)
    grad_active = (
        product_transposed(upstream, weight_down) + product(grad_down_low, adapter_down_in)
    ).astype(jnp.bfloat16)
    gelu_pull = jax.vjp(partial(jax.nn.gelu, approximate=True), upper_sum)[1]
    grad_upper = gelu_pull(grad_active.astype(jnp.float32))[0].astype(jnp.bfloat16)
    grad_up_out = product_outer(up_low, grad_upper)
    grad_up_low = product_transposed(grad_upper, adapter_up_out).astype(jnp.bfloat16)
    grad_up_in = product_outer(grad_up_low, second_in)
    grad_second = product_transposed(grad_upper, weight_up) + product(grad_up_low, adapter_up_in)
    grad_hidden = upstream.astype(jnp.float32) + norm_backward(
        grad_second, normed_two, inverse_two, gain_two.astype(jnp.float32)
    )
    grad_branch = grad_hidden.astype(jnp.bfloat16)
    grad_out_out = product_outer(out_low, grad_branch)
    grad_out_low = product_transposed(grad_branch, adapter_out_out).astype(jnp.bfloat16)
    grad_out_in = product_outer(grad_out_low, mixed_low)
    grad_mixed = (
        product_transposed(grad_branch, weight_out) + product(grad_out_low, adapter_out_in)
    ).astype(jnp.bfloat16)
    grad_queries, far_keys, near_keys, far_values, near_values = attend_backward(
        meta, queries, key_buffer, value_buffer, jnp.pad(grad_mixed, padding), mixed_padded, logsums
    )
    far_pair = jnp.stack([far_keys, far_values])
    owned_keys, owned_values = near_keys, near_values
    for offset in range(reach, 0, -1):
        first_row = (reach - offset) * row_count
        moved = shifted(far_pair[:, first_row : first_row + row_count], "ctx", -offset)
        owned_keys = owned_keys + moved[0].astype(jnp.float32)
        owned_values = owned_values + moved[1].astype(jnp.float32)
    grad_qkv = jnp.concatenate(
        [
            grad_queries[:, :feature_count],
            owned_keys[:, :feature_count].astype(jnp.bfloat16),
            owned_values[:, :feature_count].astype(jnp.bfloat16),
        ],
        axis=1,
    )
    grad_qkv_out = product_outer(qkv_low, grad_qkv)
    grad_qkv_low = product_transposed(grad_qkv, adapter_qkv_out).astype(jnp.bfloat16)
    grad_qkv_in = product_outer(grad_qkv_low, first_in)
    grad_first = product_transposed(grad_qkv, weight_qkv) + product(grad_qkv_low, adapter_qkv_in)
    grad_input = grad_hidden + norm_backward(
        grad_first, normed_one, inverse_one, gain_one.astype(jnp.float32)
    )
    selector = (jnp.arange(ADAPTERS, dtype=jnp.int32) == chosen).astype(jnp.float32)

    def spread_out(single):
        return selector[:, None, None] * single[None]

    stacked_qkv_in = spread_out(grad_qkv_in)
    stacked_qkv_out = spread_out(grad_qkv_out)
    stacked_out_in = spread_out(grad_out_in)
    stacked_out_out = spread_out(grad_out_out)
    stacked_up_in = spread_out(grad_up_in)
    stacked_up_out = spread_out(grad_up_out)
    stacked_down_in = spread_out(grad_down_in)
    stacked_down_out = spread_out(grad_down_out)
    totals = lax.psum(
        (
            stacked_qkv_in,
            stacked_qkv_out,
            stacked_out_in,
            stacked_out_out,
            stacked_up_in,
            stacked_up_out,
            stacked_down_in,
            stacked_down_out,
        ),
        ("dp", "ctx", "wt"),
    )
    return (
        output[None],
        grad_input[None],
        totals[0],
        totals[1],
        totals[2],
        totals[3],
        totals[4],
        totals[5],
        totals[6],
        totals[7],
    )


def solution(mesh):
    return jax.shard_map(
        shards,
        mesh=mesh,
        in_specs=(
            P(("dp", "wt"), "ctx", None),
            P(("dp", "wt"), "ctx", None),
            P(("dp", "wt"), None),
            P(("dp", "wt"), None),
            P("wt"),
            P("wt"),
            P("wt", None),
            P("wt"),
            P("wt", None),
            P("wt"),
            P("wt"),
            P("wt"),
            P("wt", None),
            P("wt"),
            P("wt", None),
            P("wt"),
            P(),
            P(),
            P(),
            P(),
            P(),
            P(),
            P(),
            P(),
        ),
        out_specs=(
            P(("dp", "wt"), "ctx", None),
            P(("dp", "wt"), "ctx", None),
            P(),
            P(),
            P(),
            P(),
            P(),
            P(),
            P(),
            P(),
        ),
        check_vma=False,
    )
```

```python
from functools import partial

import jax
import jax.numpy as jnp
from jax import lax
from jax.experimental import pallas as pl
from jax.experimental.pallas import tpu as pltpu
from jax.sharding import PartitionSpec as P

HEADS = 25
HEAD_DIM = 64
ADAPTERS = 8
WINDOW = 1024
RANK = 16
EPSILON = 1e-05
MASKED = -1e30

PAIRS = (HEADS + 1) // 2
PADDED = PAIRS * 128
FACTOR = HEAD_DIM ** (-0.5)
SHARDS = 4
PARTS = 8
BLOCK = 256
FF_CHUNK = 1280
VMEM_LIMIT = 60 << 20

def product(left_side, right_side):
    return lax.dot_general(left_side, right_side, (((1,), (0,)), ((), ())), preferred_element_type=jnp.float32)


def product_transposed(left_side, right_side):
    return lax.dot_general(left_side, right_side, (((1,), (1,)), ((), ())), preferred_element_type=jnp.float32)


def product_outer(left_side, right_side):
    return lax.dot_general(left_side, right_side, (((0,), (0,)), ((), ())), preferred_element_type=jnp.float32)


def norm_forward(values, norm_gain, norm_shift):
    center = values - jnp.mean(values, axis=-1, keepdims=True)
    inverse = lax.rsqrt(jnp.mean(center * center, axis=-1, keepdims=True) + EPSILON)
    normed = center * inverse
    return (normed * norm_gain + norm_shift, normed, inverse)


def norm_backward(upstream, normed, inverse, norm_gain):
    scaled = upstream * norm_gain
    return inverse * (
        scaled
        - jnp.mean(scaled, axis=-1, keepdims=True)
        - normed * jnp.mean(scaled * normed, axis=-1, keepdims=True)
    )


def copy_piece(source, target, row, columns, sem):
    start = pl.multiple_of(row, 16)
    pltpu.make_async_copy(source, target.at[pl.ds(start, source.shape[0]), columns], sem).start()


def start_shard(pieces, place, distance, target, source_columns, columns, sem):
    own, rest, parts = pieces[0], pieces[1], pieces[2:]
    base = place[distance] * own.shape[0]
    if distance == 0:
        copy_piece(own.at[:, source_columns], target, base, columns, sem)
        return
    part_rows = parts[0].shape[1]
    for source in range(PARTS):
        row = base + place[SHARDS + source] * part_rows
        copy_piece(parts[source].at[distance - 1, :, source_columns], target, row, columns, sem)
    row = base + PARTS * part_rows
    copy_piece(rest.at[distance - 1, :, source_columns], target, row, columns, sem)


def start_columns(pieces, place, target, source_columns, columns, sem):
    for distance in range(SHARDS):
        start_shard(pieces, place, distance, target, source_columns, columns, sem)


def wait_rows(target, start, rows, columns, sem):
    whole = target.at[pl.ds(start, rows), columns]
    pltpu.make_async_copy(whole, whole, sem).wait()


def widen(wide, low):
    rows = wide.shape[0]
    fill = jnp.zeros((rows, PADDED - wide.shape[1] - low.shape[1]), jnp.bfloat16)
    return jnp.concatenate([wide, low, fill], axis=1)


def blocks_of(rows):
    return [pl.ds(start, BLOCK) for start in range(0, rows, BLOCK)]


HBM = pl.BlockSpec(memory_space=pl.ANY)


def whole_of(array):
    shape = array.shape
    return pl.BlockSpec(shape, lambda *_: (0,) * len(shape))


def call(kernel, name, grid, place, inputs, pieces, in_specs, outs, out_specs, scratch):
    return pl.pallas_call(
        kernel,
        grid_spec=pltpu.PrefetchScalarGridSpec(
            num_scalar_prefetch=1,
            grid=grid,
            in_specs=in_specs + [HBM] * len(pieces),
            out_specs=out_specs,
            scratch_shapes=scratch,
        ),
        out_shape=outs,
        compiler_params=pltpu.CompilerParams(vmem_limit_bytes=VMEM_LIMIT),
        name=name,
    )(place, *inputs, *pieces)


def out_of(shape, kind):
    return jax.ShapeDtypeStruct(shape, kind)


def column_block(rows, width):
    return pl.BlockSpec((rows, width), lambda c, *_: (0, c))


def row_block(width):
    return pl.BlockSpec((BLOCK, width), lambda r, *_: (r, 0))


def qkv_kernel(place, x_ref, gain, shift, bias, a_in, a_out, *more):
    pieces, (first_ref, low_ref, q_ref, kv_ref, w, wide, sems) = more[:-7], more[-7:]
    rows, features = x_ref.shape
    step, steps = pl.program_id(0), pl.num_programs(0)
    width = w.shape[2]

    def fetch(c):
        columns = pl.ds(pl.multiple_of(c * width, 128), width)
        start_columns(pieces, place, w.at[c % 2], columns, pl.ds(0, width), sems.at[c % 2])

    @pl.when(step == 0)
    def _():
        fetch(0)
        for slot in range(2):
            w[slot, pl.ds(features + RANK, PADDED - features - RANK), :] = jnp.zeros(
                (PADDED - features - RANK, width), jnp.bfloat16
            )
        for block in blocks_of(rows):
            normed_in, _, _ = norm_forward(x_ref[block, :].astype(jnp.float32), gain[...], shift[...])
            first = normed_in.astype(jnp.bfloat16)
            low = product_transposed(first, a_in[...]).astype(jnp.bfloat16)
            first_ref[block, :] = first
            low_ref[block, :] = low
            wide[block, :] = widen(first, low)

    @pl.when(step + 1 < steps)
    def _():
        fetch(step + 1)

    slot = lax.rem(step, 2)
    wait_rows(w.at[slot], 0, features, pl.ds(0, width), sems.at[slot])
    w[slot, pl.ds(features, RANK), :] = a_out[...]
    for block in blocks_of(rows):
        part = (product(wide[block, :], w[slot]) + bias[...]).astype(jnp.bfloat16)

        @pl.when(step == 0)
        def _():
            q_ref[block, :] = part

        @pl.when(step > 0)
        def _():
            kv_ref[block, :] = part


def qkv_call(place, x, gain, shift, bias, a_in, a_out, pieces):
    rows, features = x.shape
    steps = 3
    width = PADDED
    return call(
        qkv_kernel, "qkv", (steps,), place, [x, gain, shift, bias, a_in, a_out], pieces,
        [whole_of(x), whole_of(gain), whole_of(shift), column_block(1, width), whole_of(a_in), column_block(RANK, width)],
        [out_of((rows, features), jnp.bfloat16), out_of((rows, RANK), jnp.bfloat16), out_of((rows, width), jnp.bfloat16), out_of((rows, 2 * width), jnp.bfloat16)],
        [whole_of(x), pl.BlockSpec((rows, RANK), lambda *_: (0, 0)), pl.BlockSpec((rows, width), lambda *_: (0, 0)),
         pl.BlockSpec((rows, width), lambda c, *_: (0, jnp.maximum(c - 1, 0)))],
        [pltpu.VMEM((2, PADDED, width), jnp.bfloat16), pltpu.VMEM((rows, PADDED), jnp.bfloat16), pltpu.SemaphoreType.DMA((2,))],
    )


def out_kernel(place, x_ref, mixed_ref, gain, shift, bias, a_in, a_out, u_in, *more):
    pieces, (hidden_ref, second_ref, low_ref, up_low_ref, w, sem) = more[:-6], more[-6:]
    features = x_ref.shape[1]

    @pl.when(pl.program_id(0) == 0)
    def _():
        start_columns(pieces, place, w, pl.ds(0, features), pl.ds(0, features), sem)
        w[pl.ds(features, RANK), :] = a_out[...]
        w[pl.ds(features + RANK, PADDED - features - RANK), :] = jnp.zeros(
            (PADDED - features - RANK, features), jnp.bfloat16
        )
        wait_rows(w, 0, features, pl.ds(0, features), sem)

    mixed = mixed_ref[:, :features]
    low = product_transposed(mixed, a_in[...]).astype(jnp.bfloat16)
    hidden = x_ref[...].astype(jnp.float32) + (product(widen(mixed, low), w[...]) + bias[...])
    normed_mid, _, _ = norm_forward(hidden, gain[...], shift[...])
    second = normed_mid.astype(jnp.bfloat16)
    hidden_ref[...] = hidden
    second_ref[...] = second
    low_ref[...] = low
    up_low_ref[...] = product_transposed(second, u_in[...]).astype(jnp.bfloat16)


def out_call(place, x, mixed, gain, shift, bias, a_in, a_out, u_in, pieces):
    rows, features = x.shape
    return call(
        out_kernel, "out", (rows // BLOCK,), place, [x, mixed, gain, shift, bias, a_in, a_out, u_in], pieces,
        [row_block(features), row_block(PADDED)] + [whole_of(a) for a in (gain, shift, bias, a_in, a_out, u_in)],
        [out_of((rows, features), jnp.float32), out_of((rows, features), jnp.bfloat16), out_of((rows, RANK), jnp.bfloat16), out_of((rows, RANK), jnp.bfloat16)],
        [row_block(features), row_block(features), row_block(RANK), row_block(RANK)],
        [pltpu.VMEM((PADDED, features), jnp.bfloat16), pltpu.SemaphoreType.DMA(())],
    )


def fetch_down(pieces, place, w, sems):
    width = w.shape[1]
    for distance in range(SHARDS):
        start_shard(pieces, place, distance, w, pl.ds(0, width), pl.ds(0, width), sems.at[place[distance]])


def wait_down(step, w, sems):
    shard_rows = w.shape[0] // SHARDS
    for shard in range(SHARDS):
        first_step = max(0, -(-(shard * shard_rows - FF_CHUNK + 1) // FF_CHUNK))

        @pl.when(step == first_step)
        def _():
            wait_rows(w, shard * shard_rows, shard_rows, pl.ds(0, w.shape[1]), sems.at[shard])


def active_grad_kernel(place, cot_ref, a_in, a_out, *more):
    pieces, (g_ref, low_ref, w, sems) = more[:-4], more[-4:]
    rows, features = cot_ref.shape
    step = pl.program_id(0)

    @pl.when(step == 0)
    def _():
        fetch_down(pieces, place, w, sems)
        for block in blocks_of(rows):
            low_ref[block, :] = product_transposed(cot_ref[block, :], a_out[...]).astype(jnp.bfloat16)

    wait_down(step, w, sems)
    weight = w[pl.ds(pl.multiple_of(step * FF_CHUNK, FF_CHUNK), FF_CHUNK), :]
    for block in blocks_of(rows):
        g_ref[block, :] = (
            product_transposed(cot_ref[block, :], weight) + product(low_ref[block, :], a_in[...])
        ).astype(jnp.bfloat16)


def active_grad_call(place, cot, a_in, a_out, pieces):
    rows, features = cot.shape
    units = a_in.shape[1]
    return call(
        active_grad_kernel, "active_grad", (units // FF_CHUNK,), place, [cot, a_in, a_out], pieces,
        [whole_of(cot), column_block(RANK, FF_CHUNK), whole_of(a_out)],
        [out_of((rows, units), jnp.bfloat16), out_of((rows, RANK), jnp.bfloat16)],
        [column_block(rows, FF_CHUNK), pl.BlockSpec((rows, RANK), lambda *_: (0, 0))],
        [pltpu.VMEM((units, features), jnp.bfloat16), pltpu.SemaphoreType.DMA((SHARDS,))],
    )


GELU_A = 0.7978845608
GELU_B = 0.044715


def up_kernel(place, second_ref, up_low_ref, g_active_ref, g_low_ref, bias, u_out, d_in, *more):
    pieces, (active_ref, acc_ref, down_low_ref, g_up_out_ref, g_down_in_ref, w, wide, low_scr, sems) = more[:-9], more[-9:]
    rows, features = second_ref.shape
    step, steps = pl.program_id(0), pl.num_programs(0)
    width = w.shape[2]

    def fetch(c):
        columns = pl.ds(pl.multiple_of(c * width, 128), width)
        start_columns(pieces, place, w.at[c % 2], columns, pl.ds(0, width), sems.at[c % 2])

    @pl.when(step == 0)
    def _():
        fetch(0)
        for slot in range(2):
            w[slot, pl.ds(features + RANK, PADDED - features - RANK), :] = jnp.zeros(
                (PADDED - features - RANK, width), jnp.bfloat16
            )
        for block in blocks_of(rows):
            wide[block, :] = widen(second_ref[block, :], up_low_ref[block, :])

    @pl.when(step + 1 < steps)
    def _():
        fetch(step + 1)

    slot = lax.rem(step, 2)
    wait_rows(w.at[slot], 0, features, pl.ds(0, width), sems.at[slot])
    w[slot, pl.ds(features, RANK), :] = u_out[...]
    up_out_sum, down_in_sum = None, None
    for block in blocks_of(rows):
        upper = product(wide[block, :], w[slot]) + bias[...]
        square = upper * upper
        inner = jnp.tanh((GELU_A * upper) * (1.0 + GELU_B * square))
        half = 0.5 * (1.0 + inner)
        active = (upper * half).astype(jnp.bfloat16)
        slope = half + (0.5 * GELU_A) * upper * (1.0 - inner * inner) * (1.0 + (3.0 * GELU_B) * square)
        g_upper = (g_active_ref[block, :].astype(jnp.float32) * slope).astype(jnp.bfloat16)
        active_ref[block, :] = active
        acc = product_transposed(g_upper, w[slot])
        low = product_transposed(active, d_in[...])

        @pl.when(step == 0)
        def _():
            acc_ref[block, :] = acc
            low_scr[block, :] = low

        @pl.when(step > 0)
        def _():
            acc_ref[block, :] += acc
            low_scr[block, :] += low

        up_out = product_outer(up_low_ref[block, :], g_upper)
        down_in = product_outer(g_low_ref[block, :], active)
        up_out_sum = up_out if up_out_sum is None else up_out_sum + up_out
        down_in_sum = down_in if down_in_sum is None else down_in_sum + down_in
    g_up_out_ref[...] = up_out_sum
    g_down_in_ref[...] = down_in_sum

    @pl.when(step == steps - 1)
    def _():
        down_low_ref[...] = low_scr[...].astype(jnp.bfloat16)


def up_call(place, second, up_low, g_active, g_low, bias, u_out, d_in, pieces):
    rows, features = second.shape
    units = bias.shape[1]
    low_block = pl.BlockSpec((rows, RANK), lambda *_: (0, 0))
    return call(
        up_kernel, "up", (units // FF_CHUNK,), place, [second, up_low, g_active, g_low, bias, u_out, d_in], pieces,
        [whole_of(second), low_block, column_block(rows, FF_CHUNK), low_block,
         column_block(1, FF_CHUNK), column_block(RANK, FF_CHUNK), column_block(RANK, FF_CHUNK)],
        [out_of((rows, units), jnp.bfloat16), out_of((rows, PADDED), jnp.float32), out_of((rows, RANK), jnp.bfloat16),
         out_of((RANK, units), jnp.float32), out_of((RANK, units), jnp.float32)],
        [column_block(rows, FF_CHUNK), pl.BlockSpec((rows, PADDED), lambda *_: (0, 0)), low_block,
         column_block(RANK, FF_CHUNK), column_block(RANK, FF_CHUNK)],
        [pltpu.VMEM((2, PADDED, FF_CHUNK), jnp.bfloat16), pltpu.VMEM((rows, PADDED), jnp.bfloat16), pltpu.VMEM((rows, RANK), jnp.float32),
         pltpu.SemaphoreType.DMA((2,))],
    )


def out_grad_kernel(place, acc_ref, hidden_ref, second_ref, cot_ref, mixed_ref, low_ref, down_low_ref, gain, u_in, a_in, a_out, *more):
    pieces, (g_hidden_ref, g_mixed_ref, g_up_in, g_out_out, g_out_in, g_down_out, w, sem) = more[:-8], more[-8:]
    features = hidden_ref.shape[1]
    step = pl.program_id(0)

    @pl.when(step == 0)
    def _():
        start_columns(pieces, place, w, pl.ds(0, features), pl.ds(0, features), sem)
        w[pl.ds(features, RANK), :] = a_out[...]
        w[pl.ds(features + RANK, PADDED - features - RANK), :] = jnp.zeros(
            (PADDED - features - RANK, features), jnp.bfloat16
        )

    g_up_low = acc_ref[:, features : features + RANK].astype(jnp.bfloat16)
    g_second = acc_ref[:, :features] + product(g_up_low, u_in[...])
    _, normed, inverse = norm_forward(hidden_ref[...], gain[...], 0.0)
    cot = cot_ref[...]
    g_hidden = cot.astype(jnp.float32) + norm_backward(g_second, normed, inverse, gain[...])
    g_branch = g_hidden.astype(jnp.bfloat16)
    g_hidden_ref[...] = g_hidden

    @pl.when(step == 0)
    def _():
        wait_rows(w, 0, features, pl.ds(0, features), sem)

    back = product_transposed(g_branch, w[...])
    g_low = back[:, features : features + RANK].astype(jnp.bfloat16)
    g_mixed = back[:, :features] + product(g_low, a_in[...])
    g_mixed_ref[:, :features] = g_mixed.astype(jnp.bfloat16)
    g_mixed_ref[:, features:] = jnp.zeros((BLOCK, PADDED - features), jnp.bfloat16)
    sums = (
        product_outer(g_up_low, second_ref[...]),
        product_outer(low_ref[...], g_branch),
        product_outer(g_low, mixed_ref[:, :features]),
        product_outer(down_low_ref[...], cot),
    )
    for total, term in zip((g_up_in, g_out_out, g_out_in, g_down_out), sums):
        @pl.when(step == 0)
        def _():
            total[...] = term

        @pl.when(step > 0)
        def _():
            total[...] += term


def out_grad_call(place, acc, hidden, second, cot, mixed, low, down_low, gain, u_in, a_in, a_out, pieces):
    rows, features = hidden.shape
    small = pl.BlockSpec((RANK, features), lambda *_: (0, 0))
    return call(
        out_grad_kernel, "out_grad", (rows // BLOCK,), place,
        [acc, hidden, second, cot, mixed, low, down_low, gain, u_in, a_in, a_out], pieces,
        [row_block(PADDED), row_block(features), row_block(features), row_block(features), row_block(PADDED),
         row_block(RANK), row_block(RANK)] + [whole_of(a) for a in (gain, u_in, a_in, a_out)],
        [out_of((rows, features), jnp.float32), out_of((rows, PADDED), jnp.bfloat16)] + [out_of((RANK, features), jnp.float32)] * 4,
        [row_block(features), row_block(PADDED)] + [small] * 4,
        [pltpu.VMEM((PADDED, features), jnp.bfloat16), pltpu.SemaphoreType.DMA(())],
    )


def down_kernel(place, active_ref, hidden_ref, down_low_ref, bias, a_out, *more):
    pieces, (out_ref, w, acc, sems) = more[:-4], more[-4:]
    rows, features = hidden_ref.shape
    step, steps = pl.program_id(0), pl.num_programs(0)

    @pl.when(step == 0)
    def _():
        fetch_down(pieces, place, w, sems)
        for block in blocks_of(rows):
            acc[block, :] = product(down_low_ref[block, :], a_out[...]) + bias[...]

    wait_down(step, w, sems)
    weight = w[pl.ds(pl.multiple_of(step * FF_CHUNK, FF_CHUNK), FF_CHUNK), :]
    for block in blocks_of(rows):
        acc[block, :] += product(active_ref[block, :], weight)

    @pl.when(step == steps - 1)
    def _():
        for block in blocks_of(rows):
            out_ref[block, :] = (hidden_ref[block, :] + acc[block, :]).astype(jnp.bfloat16)


def down_call(place, active, hidden, down_low, bias, a_out, pieces):
    rows, features = hidden.shape
    units = active.shape[1]
    return call(
        down_kernel, "down", (units // FF_CHUNK,), place, [active, hidden, down_low, bias, a_out], pieces,
        [column_block(rows, FF_CHUNK), whole_of(hidden), pl.BlockSpec((rows, RANK), lambda *_: (0, 0)),
         whole_of(bias), whole_of(a_out)],
        out_of((rows, features), jnp.bfloat16),
        pl.BlockSpec((rows, features), lambda *_: (0, 0)),
        [pltpu.VMEM((units, features), jnp.bfloat16), pltpu.VMEM((rows, features), jnp.float32), pltpu.SemaphoreType.DMA((SHARDS,))],
    )


def tokens_grad_kernel(place, x_ref, first_ref, low_ref, g_hidden_ref, gain, a_in, a_out, near_ref, far_ref, *more):
    pieces, (out_ref, g_qkv_out, g_qkv_in, w, acc, sems) = more[:-6], more[-6:]
    rows, features = x_ref.shape
    step, steps = pl.program_id(0), pl.num_programs(0)
    width = w.shape[2]

    def fetch(c):
        columns = pl.ds(pl.multiple_of(c * width, 128), width)
        start_columns(pieces, place, w.at[c % 2], columns, pl.ds(0, width), sems.at[c % 2])

    @pl.when(step == 0)
    def _():
        fetch(0)
        for slot in range(2):
            w[slot, pl.ds(features + RANK, PADDED - features - RANK), :] = jnp.zeros(
                (PADDED - features - RANK, width), jnp.bfloat16
            )

    @pl.when(step + 1 < steps)
    def _():
        fetch(step + 1)

    slot = lax.rem(step, 2)
    wait_rows(w.at[slot], 0, features, pl.ds(0, width), sems.at[slot])
    w[slot, pl.ds(features, RANK), :] = a_out[...]
    qkv_out_sum = None
    for block in blocks_of(rows):
        far = jnp.where(step > 0, far_ref[block, :].astype(jnp.float32), 0.0)
        g = (near_ref[block, :].astype(jnp.float32) + far).astype(jnp.bfloat16)
        back = product_transposed(g, w[slot])

        @pl.when(step == 0)
        def _():
            acc[block, :] = back

        @pl.when(step > 0)
        def _():
            acc[block, :] += back

        term = product_outer(low_ref[block, :], g)
        qkv_out_sum = term if qkv_out_sum is None else qkv_out_sum + term
    g_qkv_out[...] = qkv_out_sum

    @pl.when(step == steps - 1)
    def _():
        qkv_in_sum = None
        for block in blocks_of(rows):
            g_low = acc[block, pl.ds(features, RANK)].astype(jnp.bfloat16)
            g_first = acc[block, pl.ds(0, features)] + product(g_low, a_in[...])
            _, normed, inverse = norm_forward(x_ref[block, :].astype(jnp.float32), gain[...], 0.0)
            out_ref[block, :] = g_hidden_ref[block, :] + norm_backward(g_first, normed, inverse, gain[...])
            term = product_outer(g_low, first_ref[block, :])
            qkv_in_sum = term if qkv_in_sum is None else qkv_in_sum + term
        g_qkv_in[...] = qkv_in_sum


def tokens_grad_call(place, x, first, low, g_hidden, gain, a_in, a_out, near, far, pieces):
    rows, features = x.shape
    steps = 3
    near_block = pl.BlockSpec((None, rows, PADDED), lambda c, *_: (c, 0, 0))
    far_block = pl.BlockSpec((None, rows, PADDED), lambda c, *_: (jnp.maximum(c - 1, 0), 0, 0))
    return call(
        tokens_grad_kernel, "tokens_grad", (steps,), place, [x, first, low, g_hidden, gain, a_in, a_out, near, far], pieces,
        [whole_of(x), whole_of(first), whole_of(low), whole_of(g_hidden), whole_of(gain), whole_of(a_in),
         column_block(RANK, PADDED), near_block, far_block],
        [out_of((rows, features), jnp.float32), out_of((RANK, steps * PADDED), jnp.float32), out_of((RANK, features), jnp.float32)],
        [pl.BlockSpec((rows, features), lambda *_: (0, 0)), column_block(RANK, PADDED),
         pl.BlockSpec((RANK, features), lambda *_: (0, 0))],
        [pltpu.VMEM((2, PADDED, PADDED), jnp.bfloat16), pltpu.VMEM((rows, PADDED), jnp.float32), pltpu.SemaphoreType.DMA((2,))],
    )


TILE = 256
REACH_TILES = WINDOW // TILE
SPAN_TILES = REACH_TILES + 1


def split_pair(pair):
    lane = lax.broadcasted_iota(jnp.int32, pair.shape, 1)
    zero = jnp.zeros_like(pair)
    return jnp.concatenate(
        [jnp.where(lane < HEAD_DIM, pair, zero), jnp.where(lane >= HEAD_DIM, pair, zero)], axis=0
    )


def join_pair(stacked):
    lane = lax.broadcasted_iota(jnp.int32, (TILE, 128), 1)
    return jnp.where(lane < HEAD_DIM, stacked[:TILE], stacked[TILE:])


def tile_bias(bounds, query_start, key_start):
    rows = query_start + lax.broadcasted_iota(jnp.int32, (TILE, 1), 0)
    columns = key_start + lax.broadcasted_iota(jnp.int32, (1, TILE), 1)
    row_doc = sum((rows >= bound).astype(jnp.int32) for bound in bounds)
    column_doc = sum((columns >= bound).astype(jnp.int32) for bound in bounds)
    shape = (TILE, TILE)
    distance = jnp.broadcast_to(rows, shape) - jnp.broadcast_to(columns, shape)
    same = jnp.broadcast_to(row_doc, shape) == jnp.broadcast_to(column_doc, shape)
    seen = jnp.broadcast_to(columns, shape) >= 0
    return jnp.where(same & seen & (distance >= 0) & (distance < WINDOW), 0.0, MASKED)


def fill_biases(meta, bias_scr, tiles):
    bounds = [meta[place] for place in range(3)]
    first = meta[3]

    def one(step, carry):
        tile = step // SPAN_TILES
        key_tile = tile + lax.rem(step, SPAN_TILES) - REACH_TILES
        bias_scr[step] = tile_bias(bounds, first + tile * TILE, first + key_tile * TILE)
        return carry

    lax.fori_loop(0, tiles * SPAN_TILES, one, 0)


def key_tile(far_ref, near_ref, tile):
    if tile < REACH_TILES:
        return far_ref[pl.ds(tile * TILE, TILE), :]
    return near_ref[pl.ds((tile - REACH_TILES) * TILE, TILE), :]


def attend_forward_kernel(tiles, meta, q_ref, k_far, v_far, k_near, v_near, o_ref, lse_ref, bias_scr, acc_scr):
    @pl.when(pl.program_id(0) == 0)
    def _():
        fill_biases(meta, bias_scr, tiles)

    ones = jnp.ones((TILE, 128), jnp.bfloat16)
    chunk = TILE // 2
    for tile in range(tiles):
        stacked = split_pair(q_ref[pl.ds(tile * TILE, TILE), :] * FACTOR)
        span = range(tile, tile + SPAN_TILES)
        keys = jnp.concatenate([key_tile(k_far, k_near, t) for t in span], axis=0)
        values = jnp.concatenate(
            [jnp.concatenate([key_tile(v_far, v_near, t), ones], axis=1) for t in span], axis=0
        )
        for part in range(2 * TILE // chunk):
            start = part * chunk
            bias_rows = pl.ds(start % TILE, chunk)
            bias = jnp.concatenate(
                [bias_scr[tile * SPAN_TILES + t, bias_rows, :] for t in range(SPAN_TILES)], axis=1
            )
            scores = product_transposed(stacked[start : start + chunk], keys) + bias
            highest = jnp.max(scores, axis=1, keepdims=True)
            mixed = product(jnp.exp(scores - highest).astype(jnp.bfloat16), values)
            summed = mixed[:, 128:]
            acc_scr[pl.ds(start, chunk), :] = mixed[:, :128] / summed
            lse_ref[pl.ds(tile * 2 * TILE + start, chunk), :] = highest + jnp.log(summed)
        o_ref[pl.ds(tile * TILE, TILE), :] = join_pair(acc_scr[...]).astype(jnp.bfloat16)


def pair_columns(rows, offset=0):
    return pl.BlockSpec((rows, 128), lambda j, *_: (0, offset + j))


def attend_forward(meta, queries, far, near):
    rows = queries.shape[0]
    tiles = rows // TILE
    return pl.pallas_call(
        partial(attend_forward_kernel, tiles),
        grid_spec=pltpu.PrefetchScalarGridSpec(
            num_scalar_prefetch=1,
            grid=(PAIRS,),
            in_specs=[
                pair_columns(rows), pair_columns(WINDOW), pair_columns(WINDOW, PAIRS),
                pair_columns(rows), pair_columns(rows, PAIRS),
            ],
            out_specs=[pair_columns(rows), pl.BlockSpec((None, 2 * rows, 128), lambda j, *_: (j, 0, 0))],
            scratch_shapes=[
                pltpu.VMEM((tiles * SPAN_TILES, TILE, TILE), jnp.float32),
                pltpu.VMEM((2 * TILE, 128), jnp.float32),
            ],
        ),
        out_shape=[
            jax.ShapeDtypeStruct((rows, PADDED), jnp.bfloat16),
            jax.ShapeDtypeStruct((PAIRS, 2 * rows, 128), jnp.float32),
        ],
        compiler_params=pltpu.CompilerParams(vmem_limit_bytes=VMEM_LIMIT),
        name="attend_forward",
    )(meta, queries, far, far, near, near)


def attend_backward_kernel(
    tiles, meta, q_ref, k_far, v_far, k_near, v_near, g_ref, o_ref, lse_ref,
    near_ref, far_ref, bias_scr, dq_scr, dkt, dvt,
):
    @pl.when(pl.program_id(0) == 0)
    def _():
        fill_biases(meta, bias_scr, tiles)

    dkt[...] = jnp.zeros_like(dkt)
    dvt[...] = jnp.zeros_like(dvt)
    for tile in range(tiles):
        rows = pl.ds(tile * TILE, TILE)
        queries = split_pair(q_ref[rows, :] * FACTOR)
        grads = split_pair(g_ref[rows, :])
        mixed = o_ref[rows, :].astype(jnp.float32)
        centered = jnp.sum(
            grads.astype(jnp.float32) * jnp.concatenate([mixed, mixed], axis=0), axis=1, keepdims=True
        )
        lse = lse_ref[pl.ds(tile * 2 * TILE, 2 * TILE), :]
        lse = jnp.concatenate([lse, lse], axis=1)
        queries_t = queries.T
        grads_t = grads.T
        dq_scr[...] = jnp.zeros_like(dq_scr)
        for t in range(SPAN_TILES):
            keys = key_tile(k_far, k_near, tile + t)
            bias = bias_scr[tile * SPAN_TILES + t]
            scores = product_transposed(queries, keys)
            chances = jnp.exp(scores + jnp.concatenate([bias, bias], axis=0) - lse)
            grad_chances = product_transposed(grads, key_tile(v_far, v_near, tile + t))
            grad_scores = (chances * (grad_chances - centered)).astype(jnp.bfloat16)
            dvt[tile + t] += product(grads_t, chances.astype(jnp.bfloat16))
            dkt[tile + t] += product(queries_t, grad_scores)
            dq_scr[...] += product(grad_scores, keys)
        near_ref[0, rows, :] = (join_pair(dq_scr[...]) * FACTOR).astype(jnp.bfloat16)
    for t in range(tiles + REACH_TILES):
        target, first = (far_ref, 0) if t < REACH_TILES else (near_ref, 1)
        rows = pl.ds((t if t < REACH_TILES else t - REACH_TILES) * TILE, TILE)
        target[first, rows, :] = dkt[t].T.astype(jnp.bfloat16)
        target[first + 1, rows, :] = dvt[t].T.astype(jnp.bfloat16)


def attend_backward(meta, queries, far, near, grad_mixed, mixed, lse):
    rows = queries.shape[0]
    tiles = rows // TILE
    return pl.pallas_call(
        partial(attend_backward_kernel, tiles),
        grid_spec=pltpu.PrefetchScalarGridSpec(
            num_scalar_prefetch=1,
            grid=(PAIRS,),
            in_specs=[
                pair_columns(rows), pair_columns(WINDOW), pair_columns(WINDOW, PAIRS),
                pair_columns(rows), pair_columns(rows, PAIRS), pair_columns(rows), pair_columns(rows),
                pl.BlockSpec((None, 2 * rows, 128), lambda j, *_: (j, 0, 0)),
            ],
            out_specs=[
                pl.BlockSpec((3, rows, 128), lambda j, *_: (0, 0, j)),
                pl.BlockSpec((2, WINDOW, 128), lambda j, *_: (0, 0, j)),
            ],
            scratch_shapes=[
                pltpu.VMEM((tiles * SPAN_TILES, TILE, TILE), jnp.float32),
                pltpu.VMEM((2 * TILE, 128), jnp.float32),
                pltpu.VMEM((tiles + REACH_TILES, 128, TILE), jnp.float32),
                pltpu.VMEM((tiles + REACH_TILES, 128, TILE), jnp.float32),
            ],
        ),
        out_shape=[
            jax.ShapeDtypeStruct((3, rows, PADDED), jnp.bfloat16),
            jax.ShapeDtypeStruct((2, WINDOW, PADDED), jnp.bfloat16),
        ],
        compiler_params=pltpu.CompilerParams(vmem_limit_bytes=VMEM_LIMIT),
        name="attend_backward",
    )(meta, queries, far, far, near, near, grad_mixed, mixed, lse)


def ring_pairs(size):
    return [(i, (i + 1) % size) for i in range(size)]


def plane_pairs(sizes):
    first, second = [], []
    cores = sizes["ctx"]
    for chip in range(sizes["dp"]):
        for core in range(cores):
            steps = (chip ^ 1, chip ^ 2) if core % 2 == 0 else (chip ^ 2, chip ^ 1)
            here = chip * cores + core
            first.append((here, steps[0] * cores + core))
            second.append((here, steps[1] * cores + core))
    return first, second


def swap_pairs(size):
    return [(i, i ^ 1) for i in range(size)]


def shifted(array, size, by):
    pairs = [(i, i + by) for i in range(size) if 0 <= i + by < size]
    return lax.ppermute(array, "ctx", pairs)


def place_of():
    chip, core, shard = lax.axis_index("dp"), lax.axis_index("ctx") % 2, lax.axis_index("wt")
    places = [(shard - distance) % SHARDS for distance in range(SHARDS)]
    for side in (core, 1 - core):
        near = jnp.where(side == 0, chip ^ 1, chip ^ 2)
        for where in (chip, near, near ^ 3, chip ^ 3):
            places.append(where * 2 + side)
    return jnp.stack(places).astype(jnp.int32)


def gather_shards(sizes, own, extra):
    rows = own.shape[0] // (PARTS * 16) * 16
    index = lax.axis_index("dp") * 2 + lax.axis_index("ctx") % 2
    moved = lax.dynamic_slice_in_dim(own, index * rows, rows, 0)
    moved = jnp.concatenate([moved, own[PARTS * rows :]] + extra, axis=0)
    steps = []
    for _ in range(SHARDS - 1):
        moved = lax.ppermute(moved, "wt", ring_pairs(sizes["wt"]))
        steps.append(moved)
    return rows, steps


def spread_parts(sizes, own, rows, steps):
    first, second = plane_pairs(sizes)
    swap = swap_pairs(sizes["ctx"])
    mine = jnp.stack([step[:rows] for step in steps])
    one = lax.ppermute(mine, ("dp", "ctx"), first)
    two = lax.ppermute(mine, ("dp", "ctx"), second)
    both = lax.ppermute(one, ("dp", "ctx"), second)
    parts = [mine, one, two, both]
    parts += [lax.ppermute(part, "ctx", swap) for part in parts]
    left = own.shape[0] - PARTS * rows
    rest = jnp.stack([step[rows : rows + left] for step in steps])
    return [own, rest, *parts]


def pad_thirds(array, features):
    pieces = []
    for third in range(3):
        piece = array[..., third * features : (third + 1) * features]
        pieces.append(jnp.pad(piece, [(0, 0)] * (array.ndim - 1) + [(0, PADDED - features)]))
    return jnp.concatenate(pieces, axis=-1)


def summed_adapters(sizes, terms, chosen):
    widths = [term.shape[1] for term in terms]
    flat = jnp.concatenate(terms, axis=1)
    if sizes["ctx"] == 2:
        flat = flat + lax.ppermute(flat, "ctx", swap_pairs(2))
    else:
        flat = lax.psum(flat, "ctx")
    ids = jnp.broadcast_to(chosen.astype(jnp.bfloat16), (RANK, 128))
    sent = jnp.concatenate([flat.astype(jnp.bfloat16), ids], axis=1)
    everyone = lax.all_gather(sent, ("dp", "wt"), axis=0)
    numbers = everyone[:, 0, sum(widths)].astype(jnp.int32)
    selector = (jnp.arange(ADAPTERS, dtype=jnp.int32)[:, None] == numbers[None, :]).astype(jnp.bfloat16)
    totals, start = [], 0
    for width in widths:
        part = everyone[:, :, start : start + width]
        totals.append(jnp.einsum("as,srn->arn", selector, part, preferred_element_type=jnp.float32))
        start += width
    return totals


def shards(
    sizes,
    tokens,
    cotangent,
    doc_lengths,
    adapter_ids,
    first_gain,
    first_shift,
    qkv_weight,
    qkv_bias,
    out_weight,
    out_bias,
    second_gain,
    second_shift,
    up_weight,
    up_bias,
    down_weight,
    down_bias,
    qkv_adapt_in,
    qkv_adapt_out,
    out_adapt_in,
    out_adapt_out,
    up_adapt_in,
    up_adapt_out,
    down_adapt_in,
    down_adapt_out,
):
    values, upstream = tokens[0], cotangent[0]
    row_count, feature_count = values.shape
    ctx = sizes["ctx"]
    place = place_of()

    vectors = [first_gain, first_shift, qkv_bias, out_bias, second_gain, second_shift, up_bias, down_bias]
    lengths = [vector.shape[0] for vector in vectors]
    own_qkv = pad_thirds(qkv_weight, feature_count)
    flat = jnp.concatenate(vectors)
    extra_rows = 16
    flat = jnp.pad(flat, (0, extra_rows * own_qkv.shape[1] - flat.shape[0])).reshape(extra_rows, -1)

    rows_qkv, steps_qkv = gather_shards(sizes, own_qkv, [flat])
    pieces_qkv = spread_parts(sizes, own_qkv, rows_qkv, steps_qkv)
    later = lax.optimization_barrier((out_weight, down_weight, up_weight, steps_qkv[-1]))
    out_own, down_own, up_own = later[:3]
    gathered = [gather_shards(sizes, out_own, [])]
    down_own, _ = lax.optimization_barrier((down_own, gathered[-1][1][-1]))
    gathered.append(gather_shards(sizes, down_own, []))
    up_own, _ = lax.optimization_barrier((up_own, gathered[-1][1][-1]))
    gathered.append(gather_shards(sizes, up_own, []))
    pieces_out = spread_parts(sizes, out_own, *gathered[0])
    pieces_down = spread_parts(sizes, down_own, *gathered[1])
    pieces_up = spread_parts(sizes, up_own, *gathered[2])

    extra_start = own_qkv.shape[0] - (PARTS - 1) * rows_qkv
    by_distance = jnp.stack([flat] + [step[extra_start:] for step in steps_qkv])
    order = (lax.axis_index("wt") - jnp.arange(SHARDS)) % SHARDS
    by_shard = jnp.take(by_distance, order, axis=0).reshape(SHARDS, -1).astype(jnp.float32)
    vectors, start = [], 0
    for length in lengths:
        vectors.append(by_shard[:, start : start + length].reshape(1, -1))
        start += length
    gain_one, shift_one, bias_qkv, bias_out, gain_two, shift_two, bias_up, bias_down = vectors
    bias_qkv = pad_thirds(bias_qkv, feature_count)

    chosen = adapter_ids[0, 0]

    def select(stacked):
        return lax.dynamic_index_in_dim(stacked, chosen, 0, keepdims=False)

    adapter_qkv_in = select(qkv_adapt_in)
    adapter_qkv_out = pad_thirds(select(qkv_adapt_out), feature_count)
    adapter_out_in = select(out_adapt_in)
    adapter_out_out = select(out_adapt_out)
    adapter_up_in = select(up_adapt_in)
    adapter_up_out = select(up_adapt_out)
    adapter_down_in = select(down_adapt_in)
    adapter_down_out = select(down_adapt_out)

    first_query = lax.axis_index("ctx") * row_count
    meta = jnp.concatenate([jnp.cumsum(doc_lengths[0])[:3], first_query[None]]).astype(jnp.int32)
    reach = -(-WINDOW // row_count)

    first_in, qkv_low, queries, near = qkv_call(
        place, values, gain_one, shift_one, bias_qkv, adapter_qkv_in, adapter_qkv_out, pieces_qkv
    )
    far = jnp.concatenate([shifted(near, ctx, offset) for offset in range(reach, 0, -1)], axis=0)
    mixed, logsums = attend_forward(meta, queries, far, near)
    hidden, second_in, out_low, up_low = out_call(
        place, values, mixed, gain_two, shift_two, bias_out, adapter_out_in, adapter_out_out, adapter_up_in, pieces_out
    )
    grad_active, grad_down_low = active_grad_call(place, upstream, adapter_down_in, adapter_down_out, pieces_down)
    active, grad_second, down_low, grad_up_out, grad_down_in = up_call(
        place, second_in, up_low, grad_active, grad_down_low, bias_up, adapter_up_out, adapter_down_in, pieces_up
    )
    grad_hidden, grad_mixed, grad_up_in, grad_out_out, grad_out_in, grad_down_out = out_grad_call(
        place, grad_second, hidden, second_in, upstream, mixed, out_low, down_low, gain_two,
        adapter_up_in, adapter_out_in, adapter_out_out, pieces_out,
    )
    total_up_out, total_down_in, total_up_in, total_out_out, total_out_in, total_down_out = summed_adapters(
        sizes, [grad_up_out, grad_down_in, grad_up_in, grad_out_out, grad_out_in, grad_down_out], chosen
    )
    near_grads, far_grads = attend_backward(meta, queries, far, near, grad_mixed, mixed, logsums)
    output = down_call(place, active, hidden, down_low, bias_down, adapter_down_out, pieces_down)
    moved = 0
    for offset in range(reach, 0, -1):
        first_row = (reach - offset) * row_count
        moved += shifted(far_grads[:, first_row : first_row + row_count], ctx, -offset)
    grad_input, grad_qkv_out, grad_qkv_in = tokens_grad_call(
        place, values, first_in, qkv_low, grad_hidden, gain_one, adapter_qkv_in, adapter_qkv_out,
        near_grads, moved, pieces_qkv,
    )
    total_qkv_out, total_qkv_in = summed_adapters(sizes, [grad_qkv_out, grad_qkv_in], chosen)
    total_qkv_out = jnp.concatenate(
        [total_qkv_out[..., third * PADDED : third * PADDED + feature_count] for third in range(3)], axis=-1
    )
    return (
        output[None],
        grad_input[None],
        total_qkv_in,
        total_qkv_out,
        total_out_in,
        total_out_out,
        total_up_in,
        total_up_out,
        total_down_in,
        total_down_out,
    )


def solution(mesh):
    return jax.shard_map(
        partial(shards, dict(mesh.shape)),
        mesh=mesh,
        in_specs=(
            P(("dp", "wt"), "ctx", None),
            P(("dp", "wt"), "ctx", None),
            P(("dp", "wt"), None),
            P(("dp", "wt"), None),
            P("wt"),
            P("wt"),
            P("wt", None),
            P("wt"),
            P("wt", None),
            P("wt"),
            P("wt"),
            P("wt"),
            P("wt", None),
            P("wt"),
            P("wt", None),
            P("wt"),
            P(),
            P(),
            P(),
            P(),
            P(),
            P(),
            P(),
            P(),
        ),
        out_specs=(
            P(("dp", "wt"), "ctx", None),
            P(("dp", "wt"), "ctx", None),
            P(),
            P(),
            P(),
            P(),
            P(),
            P(),
            P(),
            P(),
        ),
        check_vma=False,
    )
```

```python
from functools import partial

import jax
import jax.numpy as jnp
from jax import lax
from jax.experimental import pallas as pl
from jax.experimental.pallas import tpu as pltpu
from jax.sharding import PartitionSpec as P

HEADS = 25
HEAD_DIM = 64
ADAPTERS = 8
WINDOW = 1024
RANK = 16
EPSILON = 1e-05
MASKED = -1e30

PAIRS = (HEADS + 1) // 2
PADDED = PAIRS * 128
FACTOR = HEAD_DIM ** (-0.5)
SHARDS = 4
PARTS = 8
BLOCK = 256
FF_CHUNK = 1280
VMEM_LIMIT = 60 << 20

def product(left_side, right_side):
    return lax.dot_general(left_side, right_side, (((1,), (0,)), ((), ())), preferred_element_type=jnp.float32)


def product_transposed(left_side, right_side):
    return lax.dot_general(left_side, right_side, (((1,), (1,)), ((), ())), preferred_element_type=jnp.float32)


def product_outer(left_side, right_side):
    return lax.dot_general(left_side, right_side, (((0,), (0,)), ((), ())), preferred_element_type=jnp.float32)


def norm_forward(values, norm_gain, norm_shift):
    center = values - jnp.mean(values, axis=-1, keepdims=True)
    inverse = lax.rsqrt(jnp.mean(center * center, axis=-1, keepdims=True) + EPSILON)
    normed = center * inverse
    return (normed * norm_gain + norm_shift, normed, inverse)


def norm_backward(upstream, normed, inverse, norm_gain):
    scaled = upstream * norm_gain
    return inverse * (
        scaled
        - jnp.mean(scaled, axis=-1, keepdims=True)
        - normed * jnp.mean(scaled * normed, axis=-1, keepdims=True)
    )


def copy_piece(source, target, row, columns, sem):
    start = pl.multiple_of(row, 16)
    pltpu.make_async_copy(source, target.at[pl.ds(start, source.shape[0]), columns], sem).start()


def start_shard(pieces, place, distance, target, source_columns, columns, sem):
    own, steps = pieces[0], pieces[1:SHARDS]
    together = len(steps[0].shape) == 3
    parts = pieces[2:] if together else pieces[SHARDS:]
    base = place[distance] * own.shape[0]
    if distance == 0:
        copy_piece(own.at[:, source_columns], target, base, columns, sem)
        return
    part_rows = own.shape[0] // (PARTS * 16) * 16
    for source in range(PARTS):
        if len(parts) == PARTS:
            part = parts[source].at[distance - 1, pl.ds(0, part_rows), source_columns]
        else:
            part = parts[(distance - 1) * PARTS + source].at[:, source_columns]
        row = base + place[SHARDS + source] * part_rows
        copy_piece(part, target, row, columns, sem)
    left = own.shape[0] - PARTS * part_rows
    base += PARTS * part_rows
    if left > RANK:
        left //= SHARDS
        for source in range(SHARDS):
            rest = parts[source].at[distance - 1, pl.ds(part_rows, left), source_columns]
            copy_piece(rest, target, base + place[SHARDS + source] // 2 * left, columns, sem)
        return
    step = steps[0].at[place[distance]] if together else steps[distance - 1]
    copy_piece(step.at[pl.ds(part_rows, left), source_columns], target, base, columns, sem)


def start_columns(pieces, place, target, source_columns, columns, sem):
    for distance in range(SHARDS):
        start_shard(pieces, place, distance, target, source_columns, columns, sem)


def wait_rows(target, start, rows, columns, sem):
    whole = target.at[pl.ds(start, rows), columns]
    pltpu.make_async_copy(whole, whole, sem).wait()


def widen(wide, low):
    rows = wide.shape[0]
    fill = jnp.zeros((rows, PADDED - wide.shape[1] - low.shape[1]), jnp.bfloat16)
    return jnp.concatenate([wide, low, fill], axis=1)


def blocks_of(rows):
    return [pl.ds(start, BLOCK) for start in range(0, rows, BLOCK)]


HBM = pl.BlockSpec(memory_space=pl.ANY)


def whole_of(array):
    shape = array.shape
    return pl.BlockSpec(shape, lambda *_: (0,) * len(shape))


def call(kernel, name, grid, place, inputs, pieces, in_specs, outs, out_specs, scratch, macs, aliases={}):
    return pl.pallas_call(
        kernel,
        grid_spec=pltpu.PrefetchScalarGridSpec(
            num_scalar_prefetch=1,
            grid=grid,
            in_specs=in_specs + [HBM] * len(pieces),
            out_specs=out_specs,
            scratch_shapes=scratch,
        ),
        out_shape=outs,
        input_output_aliases=aliases,
        compiler_params=pltpu.CompilerParams(vmem_limit_bytes=VMEM_LIMIT),
        cost_estimate=pl.CostEstimate(flops=2 * macs, bytes_accessed=1 << 22, transcendentals=0),
        name=name,
    )(place, *inputs, *pieces)


def out_of(shape, kind):
    return jax.ShapeDtypeStruct(shape, kind)


def picked(width, column=lambda *grid: 0):
    return pl.BlockSpec((None, RANK, width), lambda c, place: (place[SHARDS + PARTS], 0, column(c)))


def column_block(rows, width):
    return pl.BlockSpec((rows, width), lambda c, *_: (0, c))


def row_block(width):
    return pl.BlockSpec((BLOCK, width), lambda r, *_: (r, 0))


def keys_kernel(place, x_ref, gain, shift, bias, a_in, a_out, *more):
    pieces, (first_ref, low_ref, kv_ref, w, wide, sems) = more[:-6], more[-6:]
    rows, features = x_ref.shape

    @pl.when(pl.program_id(0) == 0)
    def _():
        fetch_columns(pieces, place, w, sems, 0, 1)
        for slot in range(2):
            clear_tail(w.at[slot], features)
        for block in blocks_of(rows):
            normed_in, _, _ = norm_forward(x_ref[block, :].astype(jnp.float32), gain[...], shift[...])
            first = normed_in.astype(jnp.bfloat16)
            low = product_transposed(first, a_in[...]).astype(jnp.bfloat16)
            first_ref[block, :] = first
            low_ref[block, :] = low
            wide[block, :] = widen(first, low)

    slot = next_columns(pieces, place, w, sems, features, 1)
    w[slot, pl.ds(features, RANK), :] = a_out[...]
    for block in blocks_of(rows):
        kv_ref[block, :] = (product(wide[block, :], w[slot]) + bias[...]).astype(jnp.bfloat16)


def fetch_columns(pieces, place, w, sems, c, offset=0):
    width = w.shape[2]
    columns = pl.ds(pl.multiple_of((c + offset) * width, 128), width)
    start_columns(pieces, place, w.at[c % 2], columns, pl.ds(0, width), sems.at[c % 2])


def next_columns(pieces, place, w, sems, features, offset=0):
    step, steps = pl.program_id(0), pl.num_programs(0)

    @pl.when(step + 1 < steps)
    def _():
        fetch_columns(pieces, place, w, sems, step + 1, offset)

    slot = lax.rem(step, 2)
    wait_rows(w.at[slot], 0, features, pl.ds(0, w.shape[2]), sems.at[slot])
    return slot


def clear_tail(w, features):
    count = w.shape[0] - features - RANK
    w[pl.ds(features + RANK, count), :] = jnp.zeros((count, w.shape[1]), jnp.bfloat16)


def keys_call(place, x, gain, shift, bias, a_in, a_out, pieces):
    rows, features = x.shape
    width = PADDED
    third = lambda height: pl.BlockSpec((height, width), lambda c, *_: (0, c + 1))
    return call(
        keys_kernel, "keys", (2,), place, [x, gain, shift, bias, a_in, a_out], pieces,
        [whole_of(x), whole_of(gain), whole_of(shift), third(1), picked(features), third(RANK)],
        [out_of((rows, features), jnp.bfloat16), out_of((rows, RANK), jnp.bfloat16), out_of((rows, 2 * width), jnp.bfloat16)],
        [whole_of(x), pl.BlockSpec((rows, RANK), lambda *_: (0, 0)), column_block(rows, width)],
        [pltpu.VMEM((2, PADDED, width), jnp.bfloat16), pltpu.VMEM((rows, PADDED), jnp.bfloat16), pltpu.SemaphoreType.DMA((2,))],
        rows * features * 2 * width,
    )


def queries_kernel(place, first_ref, low_ref, bias, a_out, *more):
    pieces, (q_ref, w, sems) = more[:-3], more[-3:]
    rows, features = first_ref.shape
    width = w.shape[1]
    halves = [pl.ds(0, width // 256 * 128), pl.ds(width // 256 * 128, width - width // 256 * 128)]
    for half, columns in enumerate(halves):
        start_columns(pieces, place, w, columns, columns, sems.at[half])
    clear_tail(w, features)
    w[pl.ds(features, RANK), :] = a_out[...]
    for half, columns in enumerate(halves):
        wait_rows(w, 0, features, columns, sems.at[half])
        for block in blocks_of(rows):
            wide = widen(first_ref[block, :], low_ref[block, :])
            q_ref[block, columns] = (product(wide, w[:, columns]) + bias[:, columns]).astype(jnp.bfloat16)


def queries_call(place, first, low, bias, a_out, pieces):
    rows, features = first.shape
    width = PADDED
    return call(
        queries_kernel, "queries", (1,), place, [first, low, bias, a_out], pieces,
        [whole_of(first), whole_of(low), column_block(1, width), column_block(RANK, width)],
        out_of((rows, width), jnp.bfloat16),
        column_block(rows, width),
        [pltpu.VMEM((PADDED, width), jnp.bfloat16), pltpu.SemaphoreType.DMA((2,))],
        rows * features * width,
    )


def out_kernel(place, x_ref, mixed_ref, gain, shift, bias, a_in, a_out, u_in, *more):
    pieces, (hidden_ref, second_ref, low_ref, up_low_ref, w, sem) = more[:-6], more[-6:]
    features = x_ref.shape[1]

    @pl.when(pl.program_id(0) == 0)
    def _():
        start_columns(pieces, place, w, pl.ds(0, features), pl.ds(0, features), sem)
        w[pl.ds(features, RANK), :] = a_out[...]
        w[pl.ds(features + RANK, PADDED - features - RANK), :] = jnp.zeros(
            (PADDED - features - RANK, features), jnp.bfloat16
        )
        wait_rows(w, 0, features, pl.ds(0, features), sem)

    mixed = mixed_ref[:, :features]
    low = product_transposed(mixed, a_in[...]).astype(jnp.bfloat16)
    hidden = x_ref[...].astype(jnp.float32) + (product(widen(mixed, low), w[...]) + bias[...])
    normed_mid, _, _ = norm_forward(hidden, gain[...], shift[...])
    second = normed_mid.astype(jnp.bfloat16)
    hidden_ref[...] = hidden
    second_ref[...] = second
    low_ref[...] = low
    up_low_ref[...] = product_transposed(second, u_in[...]).astype(jnp.bfloat16)


def out_call(place, x, mixed, gain, shift, bias, a_in, a_out, u_in, pieces):
    rows, features = x.shape
    return call(
        out_kernel, "out", (rows // BLOCK,), place, [x, mixed, gain, shift, bias, a_in, a_out, u_in], pieces,
        [row_block(features), row_block(PADDED)] + [whole_of(a) for a in (gain, shift, bias)] + [picked(features)] * 3,
        [out_of((rows, features), jnp.float32), out_of((rows, features), jnp.bfloat16), out_of((rows, RANK), jnp.bfloat16), out_of((rows, RANK), jnp.bfloat16)],
        [row_block(features), row_block(features), row_block(RANK), row_block(RANK)],
        [pltpu.VMEM((PADDED, features), jnp.bfloat16), pltpu.SemaphoreType.DMA(())],
        rows * features * features,
    )


def fetch_down(pieces, place, w, sems):
    width = w.shape[1]
    for distance in range(SHARDS):
        start_shard(pieces, place, distance, w, pl.ds(0, width), pl.ds(0, width), sems.at[place[distance]])


def wait_down(step, w, sems, first=0, last=None):
    shard_rows = w.shape[0] // SHARDS
    last = w.shape[0] // FF_CHUNK if last is None else last
    for shard in range(SHARDS):
        first_step = max(0, -(-(shard * shard_rows - FF_CHUNK + 1) // FF_CHUNK))
        first_step = min(max(first_step, first), last - 1)

        @pl.when(step == first_step)
        def _():
            wait_rows(w, shard * shard_rows, shard_rows, pl.ds(0, w.shape[1]), sems.at[shard])


def active_grad_kernel(first, last, place, cot_ref, a_in, a_out, *more):
    pieces, (g_ref, low_ref, w, sems) = more[:-4], more[-4:]
    pieces = pieces[: len(pieces) - (2 if first else 0)]
    rows, features = cot_ref.shape
    step = pl.program_id(0) + first

    @pl.when(step == first)
    def _():
        fetch_down(pieces, place, w, sems)
        for block in blocks_of(rows):
            low_ref[block, :] = product_transposed(cot_ref[block, :], a_out[...]).astype(jnp.bfloat16)

    wait_down(step, w, sems, first, last)
    weight = w[pl.ds(pl.multiple_of(step * FF_CHUNK, FF_CHUNK), FF_CHUNK), :]
    for block in blocks_of(rows):
        g_ref[block, :] = (
            product_transposed(cot_ref[block, :], weight) + product(low_ref[block, :], a_in[...])
        ).astype(jnp.bfloat16)


def active_grad_call(place, cot, a_in, a_out, pieces, first, last, written=()):
    rows, features = cot.shape
    units = a_in.shape[2]
    chunk = lambda height: pl.BlockSpec((height, FF_CHUNK), lambda c, *_: (0, c + first))
    return call(
        partial(active_grad_kernel, first, last), "active_grad", (last - first,), place, [cot, a_in, a_out],
        [*pieces, *written],
        [whole_of(cot), picked(FF_CHUNK, lambda c: c + first), picked(features)],
        [out_of((rows, units), jnp.bfloat16), out_of((rows, RANK), jnp.bfloat16)],
        [chunk(rows), pl.BlockSpec((rows, RANK), lambda *_: (0, 0))],
        [pltpu.VMEM((units, features), jnp.bfloat16), pltpu.SemaphoreType.DMA((SHARDS,))],
        rows * features * FF_CHUNK * (last - first),
        {4 + len(pieces) + place: place for place in range(len(written))},
    )


GELU_A = 0.7978845608
GELU_B = 0.044715


def up_kernel(place, second_ref, up_low_ref, g_active_ref, g_low_ref, bias, u_out, d_in, *more):
    pieces, (active_ref, acc_ref, down_low_ref, g_up_out_ref, g_down_in_ref, w, wide, low_scr, sems) = more[:-9], more[-9:]
    rows, features = second_ref.shape
    step, steps = pl.program_id(0), pl.num_programs(0)
    width = w.shape[2]

    def fetch(c):
        columns = pl.ds(pl.multiple_of(c * width, 128), width)
        start_columns(pieces, place, w.at[c % 2], columns, pl.ds(0, width), sems.at[c % 2])

    @pl.when(step == 0)
    def _():
        fetch(0)
        for slot in range(2):
            w[slot, pl.ds(features + RANK, PADDED - features - RANK), :] = jnp.zeros(
                (PADDED - features - RANK, width), jnp.bfloat16
            )
        for block in blocks_of(rows):
            wide[block, :] = widen(second_ref[block, :], up_low_ref[block, :])

    @pl.when(step + 1 < steps)
    def _():
        fetch(step + 1)

    slot = lax.rem(step, 2)
    wait_rows(w.at[slot], 0, features, pl.ds(0, width), sems.at[slot])
    w[slot, pl.ds(features, RANK), :] = u_out[...]
    up_out_sum, down_in_sum = None, None
    for block in blocks_of(rows):
        upper = product(wide[block, :], w[slot]) + bias[...]
        square = upper * upper
        inner = jnp.tanh((GELU_A * upper) * (1.0 + GELU_B * square))
        half = 0.5 * (1.0 + inner)
        active = (upper * half).astype(jnp.bfloat16)
        slope = half + (0.5 * GELU_A) * upper * (1.0 - inner * inner) * (1.0 + (3.0 * GELU_B) * square)
        g_upper = (g_active_ref[block, :].astype(jnp.float32) * slope).astype(jnp.bfloat16)
        active_ref[block, :] = active
        acc = product_transposed(g_upper, w[slot])
        low = product_transposed(active, d_in[...])

        @pl.when(step == 0)
        def _():
            acc_ref[block, :] = acc
            low_scr[block, :] = low

        @pl.when(step > 0)
        def _():
            acc_ref[block, :] += acc
            low_scr[block, :] += low

        up_out = product_outer(up_low_ref[block, :], g_upper)
        down_in = product_outer(g_low_ref[block, :], active)
        up_out_sum = up_out if up_out_sum is None else up_out_sum + up_out
        down_in_sum = down_in if down_in_sum is None else down_in_sum + down_in
    g_up_out_ref[...] = up_out_sum
    g_down_in_ref[...] = down_in_sum

    @pl.when(step == steps - 1)
    def _():
        down_low_ref[...] = low_scr[...].astype(jnp.bfloat16)


def up_call(place, second, up_low, g_active, g_low, bias, u_out, d_in, pieces):
    rows, features = second.shape
    units = bias.shape[1]
    low_block = pl.BlockSpec((rows, RANK), lambda *_: (0, 0))
    return call(
        up_kernel, "up", (units // FF_CHUNK,), place, [second, up_low, g_active, g_low, bias, u_out, d_in], pieces,
        [whole_of(second), low_block, column_block(rows, FF_CHUNK), low_block,
         column_block(1, FF_CHUNK), picked(FF_CHUNK, lambda c: c), picked(FF_CHUNK, lambda c: c)],
        [out_of((rows, units), jnp.bfloat16), out_of((rows, PADDED), jnp.float32), out_of((rows, RANK), jnp.bfloat16),
         out_of((RANK, units), jnp.float32), out_of((RANK, units), jnp.float32)],
        [column_block(rows, FF_CHUNK), pl.BlockSpec((rows, PADDED), lambda *_: (0, 0)), low_block,
         column_block(RANK, FF_CHUNK), column_block(RANK, FF_CHUNK)],
        [pltpu.VMEM((2, PADDED, FF_CHUNK), jnp.bfloat16), pltpu.VMEM((rows, PADDED), jnp.bfloat16), pltpu.VMEM((rows, RANK), jnp.float32),
         pltpu.SemaphoreType.DMA((2,))],
        2 * rows * features * units,
    )


def out_grad_kernel(place, acc_ref, hidden_ref, second_ref, cot_ref, mixed_ref, low_ref, down_low_ref, gain, u_in, a_in, a_out, *more):
    pieces, (g_hidden_ref, g_mixed_ref, g_up_in, g_out_out, g_out_in, g_down_out, w, sem) = more[:-8], more[-8:]
    features = hidden_ref.shape[1]
    step = pl.program_id(0)

    @pl.when(step == 0)
    def _():
        start_columns(pieces, place, w, pl.ds(0, features), pl.ds(0, features), sem)
        w[pl.ds(features, RANK), :] = a_out[...]
        w[pl.ds(features + RANK, PADDED - features - RANK), :] = jnp.zeros(
            (PADDED - features - RANK, features), jnp.bfloat16
        )

    g_up_low = acc_ref[:, features : features + RANK].astype(jnp.bfloat16)
    g_second = acc_ref[:, :features] + product(g_up_low, u_in[...])
    _, normed, inverse = norm_forward(hidden_ref[...], gain[...], 0.0)
    cot = cot_ref[...]
    g_hidden = cot.astype(jnp.float32) + norm_backward(g_second, normed, inverse, gain[...])
    g_branch = g_hidden.astype(jnp.bfloat16)
    g_hidden_ref[...] = g_hidden

    @pl.when(step == 0)
    def _():
        wait_rows(w, 0, features, pl.ds(0, features), sem)

    back = product_transposed(g_branch, w[...])
    g_low = back[:, features : features + RANK].astype(jnp.bfloat16)
    g_mixed = back[:, :features] + product(g_low, a_in[...])
    g_mixed_ref[:, :features] = g_mixed.astype(jnp.bfloat16)
    g_mixed_ref[:, features:] = jnp.zeros((BLOCK, PADDED - features), jnp.bfloat16)
    sums = (
        product_outer(g_up_low, second_ref[...]),
        product_outer(low_ref[...], g_branch),
        product_outer(g_low, mixed_ref[:, :features]),
        product_outer(down_low_ref[...], cot),
    )
    for total, term in zip((g_up_in, g_out_out, g_out_in, g_down_out), sums):
        @pl.when(step == 0)
        def _():
            total[...] = term

        @pl.when(step > 0)
        def _():
            total[...] += term


def out_grad_call(place, acc, hidden, second, cot, mixed, low, down_low, gain, u_in, a_in, a_out, pieces):
    rows, features = hidden.shape
    small = pl.BlockSpec((RANK, features), lambda *_: (0, 0))
    return call(
        out_grad_kernel, "out_grad", (rows // BLOCK,), place,
        [acc, hidden, second, cot, mixed, low, down_low, gain, u_in, a_in, a_out], pieces,
        [row_block(PADDED), row_block(features), row_block(features), row_block(features), row_block(PADDED),
         row_block(RANK), row_block(RANK), whole_of(gain)] + [picked(features)] * 3,
        [out_of((rows, features), jnp.float32), out_of((rows, PADDED), jnp.bfloat16)] + [out_of((RANK, features), jnp.float32)] * 4,
        [row_block(features), row_block(PADDED)] + [small] * 4,
        [pltpu.VMEM((PADDED, features), jnp.bfloat16), pltpu.SemaphoreType.DMA(())],
        rows * features * features,
    )


def down_kernel(place, active_ref, hidden_ref, down_low_ref, bias, a_out, *more):
    pieces, (out_ref, w, acc, sems) = more[:-4], more[-4:]
    rows, features = hidden_ref.shape
    step, steps = pl.program_id(0), pl.num_programs(0)

    @pl.when(step == 0)
    def _():
        fetch_down(pieces, place, w, sems)
        for block in blocks_of(rows):
            acc[block, :] = product(down_low_ref[block, :], a_out[...]) + bias[...]

    wait_down(step, w, sems)
    weight = w[pl.ds(pl.multiple_of(step * FF_CHUNK, FF_CHUNK), FF_CHUNK), :]
    for block in blocks_of(rows):
        acc[block, :] += product(active_ref[block, :], weight)

    @pl.when(step == steps - 1)
    def _():
        for block in blocks_of(rows):
            out_ref[:, block] = (hidden_ref[block, :] + acc[block, :]).astype(jnp.bfloat16).T


def down_call(place, active, hidden, down_low, bias, a_out, pieces):
    rows, features = hidden.shape
    units = active.shape[1]
    return call(
        down_kernel, "down", (units // FF_CHUNK,), place, [active, hidden, down_low, bias, a_out], pieces,
        [column_block(rows, FF_CHUNK), whole_of(hidden), pl.BlockSpec((rows, RANK), lambda *_: (0, 0)),
         whole_of(bias), picked(features)],
        out_of((features, rows), jnp.bfloat16),
        pl.BlockSpec((features, rows), lambda *_: (0, 0)),
        [pltpu.VMEM((units, features), jnp.bfloat16), pltpu.VMEM((rows, features), jnp.float32), pltpu.SemaphoreType.DMA((SHARDS,))],
        rows * features * units,
    )


def tokens_grad_kernel(place, x_ref, first_ref, low_ref, g_hidden_ref, gain, a_in, a_out, near_ref, far_ref, *more):
    pieces, (out_ref, g_qkv_out, g_qkv_in, w, acc, sems) = more[:-6], more[-6:]
    rows, features = x_ref.shape
    step, steps = pl.program_id(0), pl.num_programs(0)
    width = w.shape[2]

    def fetch(c):
        columns = pl.ds(pl.multiple_of(c * width, 128), width)
        start_columns(pieces, place, w.at[c % 2], columns, pl.ds(0, width), sems.at[c % 2])

    @pl.when(step == 0)
    def _():
        fetch(0)
        for slot in range(2):
            w[slot, pl.ds(features + RANK, PADDED - features - RANK), :] = jnp.zeros(
                (PADDED - features - RANK, width), jnp.bfloat16
            )

    @pl.when(step + 1 < steps)
    def _():
        fetch(step + 1)

    slot = lax.rem(step, 2)
    wait_rows(w.at[slot], 0, features, pl.ds(0, width), sems.at[slot])
    w[slot, pl.ds(features, RANK), :] = a_out[...]
    qkv_out_sum = None
    for block in blocks_of(rows):
        far = jnp.where(step > 0, far_ref[block, :].astype(jnp.float32), 0.0)
        g = (near_ref[block, :].astype(jnp.float32) + far).astype(jnp.bfloat16)
        back = product_transposed(g, w[slot])

        @pl.when(step == 0)
        def _():
            acc[block, :] = back

        @pl.when(step > 0)
        def _():
            acc[block, :] += back

        term = product_outer(low_ref[block, :], g)
        qkv_out_sum = term if qkv_out_sum is None else qkv_out_sum + term
    g_qkv_out[...] = qkv_out_sum

    @pl.when(step == steps - 1)
    def _():
        qkv_in_sum = None
        for block in blocks_of(rows):
            g_low = acc[block, pl.ds(features, RANK)].astype(jnp.bfloat16)
            g_first = acc[block, pl.ds(0, features)] + product(g_low, a_in[...])
            _, normed, inverse = norm_forward(x_ref[block, :].astype(jnp.float32), gain[...], 0.0)
            out_ref[:, block] = (g_hidden_ref[block, :] + norm_backward(g_first, normed, inverse, gain[...])).T
            term = product_outer(g_low, first_ref[block, :])
            qkv_in_sum = term if qkv_in_sum is None else qkv_in_sum + term
        g_qkv_in[...] = qkv_in_sum


def tokens_grad_call(place, x, first, low, g_hidden, gain, a_in, a_out, near, far, pieces):
    rows, features = x.shape
    steps = 3
    near_block = pl.BlockSpec((None, rows, PADDED), lambda c, *_: (c, 0, 0))
    far_block = pl.BlockSpec((None, rows, PADDED), lambda c, *_: (jnp.maximum(c - 1, 0), 0, 0))
    return call(
        tokens_grad_kernel, "tokens_grad", (steps,), place, [x, first, low, g_hidden, gain, a_in, a_out, near, far], pieces,
        [whole_of(x), whole_of(first), whole_of(low), whole_of(g_hidden), whole_of(gain), picked(features),
         column_block(RANK, PADDED), near_block, far_block],
        [out_of((features, rows), jnp.float32), out_of((RANK, steps * PADDED), jnp.float32), out_of((RANK, features), jnp.float32)],
        [pl.BlockSpec((features, rows), lambda *_: (0, 0)), column_block(RANK, PADDED),
         pl.BlockSpec((RANK, features), lambda *_: (0, 0))],
        [pltpu.VMEM((2, PADDED, PADDED), jnp.bfloat16), pltpu.VMEM((rows, PADDED), jnp.float32), pltpu.SemaphoreType.DMA((2,))],
        rows * features * steps * PADDED,
    )


def combine_kernel(widths, numbers, *refs):
    parts, totals = refs[: -len(widths)], refs[-len(widths) :]
    sequences, _, part_width = parts[0].shape
    half_width = part_width - 128

    def add(halves):
        start = 0
        for total, spans in zip(totals, widths):
            into = 0
            for width in spans:
                done = 0
                while done < width:
                    half, at = divmod(start + done, half_width)
                    size = min(width - done, half_width - at)
                    for sequence in range(sequences):
                        target = (numbers[sequence], slice(None), pl.ds(into + done, size))
                        total[target] += halves[half][sequence, :, pl.ds(at, size)].astype(jnp.float32)
                    done += size
                into += width
                start += -(-width // 128) * 128

    for total in totals:
        total[...] = jnp.zeros_like(total)
    turned = numbers[sequences]

    @pl.when(turned == 0)
    def _():
        add(parts)

    if len(parts) == 2:
        @pl.when(turned == 1)
        def _():
            add(parts[::-1])


def combine_call(numbers, parts, widths):
    shapes = [(ADAPTERS, RANK, sum(spans)) for spans in widths]
    return pl.pallas_call(
        partial(combine_kernel, widths),
        grid_spec=pltpu.PrefetchScalarGridSpec(
            num_scalar_prefetch=1,
            grid=(1,),
            in_specs=[whole_of(part) for part in parts],
            out_specs=[pl.BlockSpec(shape, lambda *_: (0, 0, 0)) for shape in shapes],
        ),
        out_shape=[out_of(shape, jnp.float32) for shape in shapes],
        compiler_params=pltpu.CompilerParams(vmem_limit_bytes=VMEM_LIMIT),
        cost_estimate=pl.CostEstimate(flops=1 << 30, bytes_accessed=1 << 22, transcendentals=0),
        name="combine",
    )(numbers, *parts)


TILE = 256
REACH_TILES = WINDOW // TILE
SPAN_TILES = REACH_TILES + 1


def split_pair(pair):
    lane = lax.broadcasted_iota(jnp.int32, pair.shape, 1)
    zero = jnp.zeros_like(pair)
    return jnp.concatenate(
        [jnp.where(lane < HEAD_DIM, pair, zero), jnp.where(lane >= HEAD_DIM, pair, zero)], axis=0
    )


def join_pair(stacked):
    lane = lax.broadcasted_iota(jnp.int32, (TILE, 128), 1)
    return jnp.where(lane < HEAD_DIM, stacked[:TILE], stacked[TILE:])


def tile_bias(bounds, query_start, key_start):
    rows = query_start + lax.broadcasted_iota(jnp.int32, (TILE, 1), 0)
    columns = key_start + lax.broadcasted_iota(jnp.int32, (1, TILE), 1)
    row_doc = sum((rows >= bound).astype(jnp.int32) for bound in bounds)
    column_doc = sum((columns >= bound).astype(jnp.int32) for bound in bounds)
    shape = (TILE, TILE)
    distance = jnp.broadcast_to(rows, shape) - jnp.broadcast_to(columns, shape)
    same = jnp.broadcast_to(row_doc, shape) == jnp.broadcast_to(column_doc, shape)
    seen = jnp.broadcast_to(columns, shape) >= 0
    return jnp.where(same & seen & (distance >= 0) & (distance < WINDOW), 0.0, MASKED)


def fill_biases(meta, bias_scr, tiles):
    bounds = [meta[place] for place in range(3)]
    first = meta[3]

    def one(step, carry):
        tile = step // SPAN_TILES
        key_tile = tile + lax.rem(step, SPAN_TILES) - REACH_TILES
        bias_scr[step] = tile_bias(bounds, first + tile * TILE, first + key_tile * TILE)
        return carry

    lax.fori_loop(0, tiles * SPAN_TILES, one, 0)


def key_tile(far_ref, near_ref, tile):
    if tile < REACH_TILES:
        return far_ref[pl.ds(tile * TILE, TILE), :]
    return near_ref[pl.ds((tile - REACH_TILES) * TILE, TILE), :]


def attend_forward_kernel(tiles, meta, q_ref, k_far, v_far, k_near, v_near, *more):
    o_ref, lse_ref, bias_scr, acc_scr = more[-4:]

    @pl.when(pl.program_id(0) == 0)
    def _():
        fill_biases(meta, bias_scr, tiles)

    ones = jnp.ones((TILE, 128), jnp.bfloat16)
    chunk = TILE // 2
    for tile in range(tiles):
        stacked = split_pair(q_ref[pl.ds(tile * TILE, TILE), :] * FACTOR)
        span = range(tile, tile + SPAN_TILES)
        keys = jnp.concatenate([key_tile(k_far, k_near, t) for t in span], axis=0)
        values = jnp.concatenate(
            [jnp.concatenate([key_tile(v_far, v_near, t), ones], axis=1) for t in span], axis=0
        )
        for part in range(2 * TILE // chunk):
            start = part * chunk
            bias_rows = pl.ds(start % TILE, chunk)
            bias = jnp.concatenate(
                [bias_scr[tile * SPAN_TILES + t, bias_rows, :] for t in range(SPAN_TILES)], axis=1
            )
            scores = product_transposed(stacked[start : start + chunk], keys) + bias
            highest = jnp.max(scores, axis=1, keepdims=True)
            mixed = product(jnp.exp(scores - highest).astype(jnp.bfloat16), values)
            summed = mixed[:, 128:]
            acc_scr[pl.ds(start, chunk), :] = mixed[:, :128] / summed
            lse_ref[pl.ds(tile * 2 * TILE + start, chunk), :] = highest + jnp.log(summed)
        o_ref[pl.ds(tile * TILE, TILE), :] = join_pair(acc_scr[...]).astype(jnp.bfloat16)


def pair_columns(rows, offset=0):
    return pl.BlockSpec((rows, 128), lambda j, *_: (0, offset + j))


def attention_cost(products, pairs, rows):
    macs = products * pairs * 2 * rows * SPAN_TILES * TILE * 256
    return pl.CostEstimate(flops=2 * macs, bytes_accessed=1 << 24, transcendentals=0)


def attend_forward(meta, queries, far, near, start, pairs, written=()):
    rows = queries.shape[0]
    tiles = rows // TILE
    return pl.pallas_call(
        partial(attend_forward_kernel, tiles),
        grid_spec=pltpu.PrefetchScalarGridSpec(
            num_scalar_prefetch=1,
            grid=(pairs,),
            in_specs=[
                pair_columns(rows, start), pair_columns(WINDOW, start), pair_columns(WINDOW, PAIRS + start),
                pair_columns(rows, start), pair_columns(rows, PAIRS + start),
            ] + [pl.BlockSpec(memory_space=pl.ANY)] * len(written),
            out_specs=[
                pair_columns(rows, start),
                pl.BlockSpec((None, 2 * rows, 128), lambda j, *_: (start + j, 0, 0)),
            ],
            scratch_shapes=[
                pltpu.VMEM((tiles * SPAN_TILES, TILE, TILE), jnp.float32),
                pltpu.VMEM((2 * TILE, 128), jnp.float32),
            ],
        ),
        out_shape=[
            jax.ShapeDtypeStruct((rows, PADDED), jnp.bfloat16),
            jax.ShapeDtypeStruct((PAIRS, 2 * rows, 128), jnp.float32),
        ],
        input_output_aliases={6 + place: place for place in range(len(written))},
        compiler_params=pltpu.CompilerParams(vmem_limit_bytes=VMEM_LIMIT),
        cost_estimate=attention_cost(2, pairs, rows),
        name="attend_forward",
    )(meta, queries, far, far, near, near, *written)


def attend_backward_kernel(
    tiles, meta, q_ref, k_far, v_far, k_near, v_near, g_ref, o_ref, lse_ref,
    near_ref, far_ref, bias_scr, dq_scr, dkt, dvt,
):
    @pl.when(pl.program_id(0) == 0)
    def _():
        fill_biases(meta, bias_scr, tiles)

    dkt[...] = jnp.zeros_like(dkt)
    dvt[...] = jnp.zeros_like(dvt)
    for tile in range(tiles):
        rows = pl.ds(tile * TILE, TILE)
        queries = split_pair(q_ref[rows, :] * FACTOR)
        grads = split_pair(g_ref[rows, :])
        mixed = o_ref[rows, :].astype(jnp.float32)
        centered = jnp.sum(
            grads.astype(jnp.float32) * jnp.concatenate([mixed, mixed], axis=0), axis=1, keepdims=True
        )
        lse = lse_ref[pl.ds(tile * 2 * TILE, 2 * TILE), :]
        lse = jnp.concatenate([lse, lse], axis=1)
        queries_t = queries.T
        grads_t = grads.T
        dq_scr[...] = jnp.zeros_like(dq_scr)
        for t in range(SPAN_TILES):
            keys = key_tile(k_far, k_near, tile + t)
            bias = bias_scr[tile * SPAN_TILES + t]
            scores = product_transposed(queries, keys)
            chances = jnp.exp(scores + jnp.concatenate([bias, bias], axis=0) - lse)
            grad_chances = product_transposed(grads, key_tile(v_far, v_near, tile + t))
            grad_scores = (chances * (grad_chances - centered)).astype(jnp.bfloat16)
            dvt[tile + t] += product(grads_t, chances.astype(jnp.bfloat16))
            dkt[tile + t] += product(queries_t, grad_scores)
            dq_scr[...] += product(grad_scores, keys)
        near_ref[0, rows, :] = (join_pair(dq_scr[...]) * FACTOR).astype(jnp.bfloat16)
    for t in range(tiles + REACH_TILES):
        target, first = (far_ref, 0) if t < REACH_TILES else (near_ref, 1)
        rows = pl.ds((t if t < REACH_TILES else t - REACH_TILES) * TILE, TILE)
        target[first, rows, :] = dkt[t].T.astype(jnp.bfloat16)
        target[first + 1, rows, :] = dvt[t].T.astype(jnp.bfloat16)


def attend_backward(meta, queries, far, near, grad_mixed, mixed, lse):
    rows = queries.shape[0]
    tiles = rows // TILE
    return pl.pallas_call(
        partial(attend_backward_kernel, tiles),
        grid_spec=pltpu.PrefetchScalarGridSpec(
            num_scalar_prefetch=1,
            grid=(PAIRS,),
            in_specs=[
                pair_columns(rows), pair_columns(WINDOW), pair_columns(WINDOW, PAIRS),
                pair_columns(rows), pair_columns(rows, PAIRS), pair_columns(rows), pair_columns(rows),
                pl.BlockSpec((None, 2 * rows, 128), lambda j, *_: (j, 0, 0)),
            ],
            out_specs=[
                pl.BlockSpec((3, rows, 128), lambda j, *_: (0, 0, j)),
                pl.BlockSpec((2, WINDOW, 128), lambda j, *_: (0, 0, j)),
            ],
            scratch_shapes=[
                pltpu.VMEM((tiles * SPAN_TILES, TILE, TILE), jnp.float32),
                pltpu.VMEM((2 * TILE, 128), jnp.float32),
                pltpu.VMEM((tiles + REACH_TILES, 128, TILE), jnp.float32),
                pltpu.VMEM((tiles + REACH_TILES, 128, TILE), jnp.float32),
            ],
        ),
        out_shape=[
            jax.ShapeDtypeStruct((3, rows, PADDED), jnp.bfloat16),
            jax.ShapeDtypeStruct((2, WINDOW, PADDED), jnp.bfloat16),
        ],
        compiler_params=pltpu.CompilerParams(vmem_limit_bytes=VMEM_LIMIT),
        cost_estimate=attention_cost(5, PAIRS, rows),
        name="attend_backward",
    )(meta, queries, far, far, near, near, grad_mixed, mixed, lse)


def ring_pairs(size):
    return [(i, (i + 1) % size) for i in range(size)]


def plane_pairs(sizes):
    first, second = [], []
    cores = sizes["ctx"]
    for chip in range(sizes["dp"]):
        for core in range(cores):
            steps = (chip ^ 1, chip ^ 2) if core % 2 == 0 else (chip ^ 2, chip ^ 1)
            here = chip * cores + core
            first.append((here, steps[0] * cores + core))
            second.append((here, steps[1] * cores + core))
    return first, second


def swap_pairs(size):
    return [(i, i ^ 1) for i in range(size)]


def shifted(array, size, by):
    pairs = [(i, i + by) for i in range(size) if 0 <= i + by < size]
    return lax.ppermute(array, "ctx", pairs)


def place_of(chosen):
    chip, core, shard = lax.axis_index("dp"), lax.axis_index("ctx") % 2, lax.axis_index("wt")
    places = [(shard - distance) % SHARDS for distance in range(SHARDS)]
    for side in (core, 1 - core):
        near = jnp.where(side == 0, chip ^ 1, chip ^ 2)
        for where in (chip, near, near ^ 3, chip ^ 3):
            places.append(where * 2 + side)
    return jnp.stack([*places, chosen]).astype(jnp.int32)


def after(array, *others):
    return lax.optimization_barrier((array, *others))[0]


def after_all(arrays, *others):
    return lax.optimization_barrier((*arrays, *others))[: len(arrays)]


def own_part(own):
    rows = own.shape[0] // (PARTS * 16) * 16
    chip, core = lax.axis_index("dp"), lax.axis_index("ctx") % 2
    left = own.shape[0] - PARTS * rows
    first = PARTS * rows
    if left > RANK:
        left //= SHARDS
        first += chip * left
    mine = lax.dynamic_slice_in_dim(own, (chip * 2 + core) * rows, rows, 0)
    return jnp.concatenate([mine, lax.dynamic_slice_in_dim(own, first, left, 0)], axis=0)


def eighth(own, moved):
    rows = own.shape[0] // (PARTS * 16) * 16
    return moved if own.shape[0] - PARTS * rows > RANK else moved[:rows]


def ring(sizes, moved):
    steps = []
    for _ in range(SHARDS - 1):
        moved = lax.ppermute(moved, "wt", ring_pairs(sizes["wt"]))
        steps.append(moved)
    return steps


def direct(sizes, moved):
    size = sizes["wt"]
    return [
        lax.ppermute(moved, "wt", [(i, (i + distance) % size) for i in range(size)])
        for distance in range(1, SHARDS)
    ]


def plane_start(sizes, mine):
    first, second = plane_pairs(sizes)
    return [mine, lax.ppermute(mine, ("dp", "ctx"), first), lax.ppermute(mine, ("dp", "ctx"), second)]


def plane_end(sizes, parts):
    _, second = plane_pairs(sizes)
    return [*parts, lax.ppermute(parts[1], ("dp", "ctx"), second)]


def swap_cores(sizes, parts):
    swap = swap_pairs(sizes["ctx"])
    return [*parts, *[lax.ppermute(part, "ctx", swap) for part in parts]]


def pad_thirds(array, features):
    pieces = []
    for third in range(3):
        piece = array[..., third * features : (third + 1) * features]
        pieces.append(jnp.pad(piece, [(0, 0)] * (array.ndim - 1) + [(0, PADDED - features)]))
    return jnp.concatenate(pieces, axis=-1)


def send_adapters(sizes, terms, chosen):
    flat = jnp.concatenate(
        [jnp.pad(term, ((0, 0), (0, -term.shape[1] % 128))) for term in terms], axis=1
    )
    paired = sizes["ctx"] == 2
    if paired:
        half = flat.shape[1] // 2
        core = lax.axis_index("ctx")
        kept = lax.dynamic_slice_in_dim(flat, core * half, half, 1)
        given = lax.dynamic_slice_in_dim(flat, (1 - core) * half, half, 1)
        flat = kept + lax.ppermute(given, "ctx", swap_pairs(2))
    else:
        flat = lax.psum(flat, "ctx")
    ids = jnp.broadcast_to(chosen.astype(jnp.bfloat16), (RANK, 128))
    return jnp.concatenate([flat.astype(jnp.bfloat16), ids], axis=1)


def share_adapters(sent):
    return lax.all_gather(sent, ("dp", "wt"), axis=0)


def sequence_numbers(sizes, everyone):
    numbers = everyone[:, 0, -1].astype(jnp.int32)
    turned = lax.axis_index("ctx") if sizes["ctx"] == 2 else 0
    return jnp.concatenate([numbers, jnp.full((1,), turned, jnp.int32)])


def both_halves(sizes, everyone):
    if sizes["ctx"] != 2:
        return [everyone]
    return [everyone, lax.ppermute(everyone, "ctx", swap_pairs(2))]


def shards(
    sizes,
    tokens,
    cotangent,
    doc_lengths,
    adapter_ids,
    first_gain,
    first_shift,
    qkv_weight,
    qkv_bias,
    out_weight,
    out_bias,
    second_gain,
    second_shift,
    up_weight,
    up_bias,
    down_weight,
    down_bias,
    qkv_adapt_in,
    qkv_adapt_out,
    out_adapt_in,
    out_adapt_out,
    up_adapt_in,
    up_adapt_out,
    down_adapt_in,
    down_adapt_out,
):
    row_count, feature_count = tokens.shape[1:]
    ctx = sizes["ctx"]
    chosen = adapter_ids[0, 0]
    place = place_of(chosen)

    vectors = [first_gain, first_shift, qkv_bias, out_bias, second_gain, second_shift, up_bias, down_bias]
    lengths = [vector.shape[0] for vector in vectors]
    flat = jnp.concatenate(vectors)
    extra_rows = -(-flat.shape[0] // (3 * PADDED))
    flat = jnp.pad(flat, (0, extra_rows * 3 * PADDED - flat.shape[0])).reshape(extra_rows, -1)

    part_qkv = jnp.concatenate([pad_thirds(own_part(qkv_weight), feature_count), flat], axis=0)
    steps_qkv = ring(sizes, part_qkv)
    parts_qkv = []
    for step in steps_qkv:
        parts_qkv += swap_cores(sizes, plane_end(sizes, plane_start(sizes, eighth(qkv_weight, step))))
    own_qkv = pad_thirds(after(qkv_weight, steps_qkv[0]), feature_count)
    pieces_qkv = [own_qkv, *steps_qkv, *parts_qkv]
    values, adapter_qkv_out = after_all([tokens[0], qkv_adapt_out], steps_qkv[1])
    upstream = after(cotangent[0], steps_qkv[-1])
    adapter_qkv_out = pad_thirds(
        lax.dynamic_index_in_dim(adapter_qkv_out, chosen, 0, keepdims=False), feature_count
    )

    def stacked(own, steps):
        return jnp.stack([eighth(own, step) for step in steps])

    steps_out = direct(sizes, after(own_part(out_weight), steps_qkv[-1]))
    parts_out = plane_start(sizes, stacked(out_weight, steps_out))
    part_down = own_part(down_weight)
    folded = after(part_down.reshape(4, -1, feature_count), *steps_out)
    turn = partial(lax.ppermute, axis_name="wt", perm=ring_pairs(sizes["wt"]))

    by_distance = jnp.stack([flat] + [step[-extra_rows:] for step in steps_qkv])
    order = (lax.axis_index("wt") - jnp.arange(SHARDS)) % SHARDS
    by_shard = jnp.take(by_distance, order, axis=0).reshape(SHARDS, -1).astype(jnp.float32)
    vectors, start = [], 0
    for length in lengths:
        vectors.append(by_shard[:, start : start + length].reshape(1, -1))
        start += length
    gain_one, shift_one, bias_qkv, bias_out, gain_two, shift_two, bias_up, bias_down = vectors
    bias_qkv = pad_thirds(bias_qkv, feature_count)

    first_query = lax.axis_index("ctx") * row_count
    meta = jnp.concatenate([jnp.cumsum(doc_lengths[0])[:3], first_query[None]]).astype(jnp.int32)
    reach = -(-WINDOW // row_count)

    first_in, qkv_low, near = keys_call(
        place, after(values, upstream, *steps_out), gain_one, shift_one, bias_qkv, qkv_adapt_in, adapter_qkv_out, pieces_qkv
    )
    steps_down = [turn(folded)]
    *parts_out[1:], steps_down[0], near = after_all([*parts_out[1:], steps_down[0], near], near)

    far = jnp.concatenate([shifted(near, ctx, offset) for offset in range(reach, 0, -1)], axis=0)
    every_up = lax.all_gather(after(own_part(up_weight), steps_down[0]), "wt", axis=0)
    parts_out = plane_end(sizes, parts_out)
    steps_down.append(turn(steps_down[0]))
    queries = queries_call(
        place, after(first_in, parts_out[1], steps_down[0]), qkv_low, bias_qkv, adapter_qkv_out, pieces_qkv
    )
    *parts_out[3:], steps_down[1] = after_all([*parts_out[3:], steps_down[1]], queries)

    parts_out = swap_cores(sizes, parts_out)
    steps_down.append(turn(steps_down[1]))
    pairs = PAIRS // 2 + 1
    written = attend_forward(meta, after(queries, parts_out[3], steps_down[1]), far, near, 0, pairs)
    steps_down[2], *parts_out[4:] = after_all([steps_down[2], *parts_out[4:]], written[0])

    steps_down = [step.reshape(part_down.shape) for step in steps_down]
    parts_down = plane_start(sizes, stacked(down_weight, steps_down))
    mixed, logsums = attend_forward(
        meta, after(queries, steps_down[2]), far, near, pairs, PAIRS - pairs, written
    )
    *parts_down[1:], every_up = after_all([*parts_down[1:], every_up], mixed)

    parts_down = plane_end(sizes, parts_down)
    steps_up = [lax.dynamic_index_in_dim(every_up, place[k], 0, keepdims=False) for k in range(1, SHARDS)]
    parts_up = plane_start(sizes, stacked(up_weight, steps_up))
    pieces_out = [out_weight, *steps_out, *parts_out]
    hidden, second_in, out_low, up_low = out_call(
        place, values, after(mixed, *parts_down[1:3], every_up), gain_two, shift_two, bias_out, out_adapt_in,
        out_adapt_out, up_adapt_in, pieces_out,
    )
    parts_down[3] = after(parts_down[3], hidden)

    pieces_down = [down_weight, *steps_down, *swap_cores(sizes, parts_down)]
    written = active_grad_call(
        place, after(upstream, hidden), down_adapt_in, down_adapt_out, pieces_down, 0, 2
    )
    parts_up[1:] = after_all(parts_up[1:], written[0])
    parts_up = plane_end(sizes, parts_up)
    grad_active, grad_down_low = active_grad_call(
        place, after(upstream, *parts_up[1:3]), down_adapt_in, down_adapt_out, pieces_down, 2, 5, written
    )
    parts_up[3] = after(parts_up[3], grad_active)
    pieces_up = [up_weight, every_up, *swap_cores(sizes, parts_up)]
    active, grad_second, down_low, grad_up_out, grad_down_in = up_call(
        place, second_in, up_low, grad_active, grad_down_low, bias_up, up_adapt_out, down_adapt_in, pieces_up
    )
    grad_hidden, grad_mixed, grad_up_in, grad_out_out, grad_out_in, grad_down_out = out_grad_call(
        place, grad_second, hidden, second_in, upstream, mixed, out_low, down_low, gain_two,
        up_adapt_in, out_adapt_in, out_adapt_out, pieces_out,
    )
    terms = [grad_up_out, grad_down_in, grad_up_in, grad_out_out, grad_out_in, grad_down_out]
    widths = [(term.shape[1],) for term in terms]
    sent = send_adapters(sizes, terms, chosen)
    everyone = share_adapters(sent)
    near_grads, far_grads = attend_backward(meta, queries, far, near, after(grad_mixed, sent), mixed, logsums)
    everyone = after(everyone, near_grads)
    moved = 0
    for offset in range(reach, 0, -1):
        first_row = (reach - offset) * row_count
        moved += shifted(far_grads[:, first_row : first_row + row_count], ctx, -offset)
    halves = both_halves(sizes, everyone)
    numbers = sequence_numbers(sizes, everyone)
    grad_input, grad_qkv_out, grad_qkv_in = tokens_grad_call(
        place, values, first_in, qkv_low, grad_hidden, gain_one, qkv_adapt_in, adapter_qkv_out,
        after(near_grads, everyone), moved, pieces_qkv,
    )
    last_sent = send_adapters(sizes, [grad_qkv_out, grad_qkv_in], chosen)
    last_everyone = share_adapters(last_sent)
    numbers, active = after_all([numbers, active], last_sent)
    totals = combine_call(numbers, halves, widths)
    total_up_out, total_down_in, total_up_in, total_out_out, total_out_in, total_down_out = totals
    output = down_call(
        place, after(active, *totals), hidden, down_low, bias_down, down_adapt_out, pieces_down
    )
    last_halves = both_halves(sizes, after(last_everyone, output))
    total_qkv_out, total_qkv_in = combine_call(numbers, last_halves, [(feature_count,) * 3, (feature_count,)])
    return (
        output.T[None],
        grad_input.T[None],
        total_qkv_in,
        total_qkv_out,
        total_out_in,
        total_out_out,
        total_up_in,
        total_up_out,
        total_down_in,
        total_down_out,
    )


def solution(mesh):
    return jax.shard_map(
        partial(shards, dict(mesh.shape)),
        mesh=mesh,
        in_specs=(
            P(("dp", "wt"), "ctx", None),
            P(("dp", "wt"), "ctx", None),
            P(("dp", "wt"), None),
            P(("dp", "wt"), None),
            P("wt"),
            P("wt"),
            P("wt", None),
            P("wt"),
            P("wt", None),
            P("wt"),
            P("wt"),
            P("wt"),
            P("wt", None),
            P("wt"),
            P("wt", None),
            P("wt"),
            P(),
            P(),
            P(),
            P(),
            P(),
            P(),
            P(),
            P(),
        ),
        out_specs=(
            P(("dp", "wt"), "ctx", None),
            P(("dp", "wt"), "ctx", None),
            P(),
            P(),
            P(),
            P(),
            P(),
            P(),
            P(),
            P(),
        ),
        check_vma=False,
    )
```

```python
from functools import partial

import jax
import jax.numpy as jnp
from jax import lax
from jax.experimental import pallas as pl
from jax.experimental.pallas import tpu as pltpu
from jax.sharding import PartitionSpec as P

HEADS = 25
HEAD_DIM = 64
ADAPTERS = 8
WINDOW = 1024
RANK = 16
EPSILON = 1e-05
MASKED = -1e30

PAIRS = (HEADS + 1) // 2
PADDED = PAIRS * 128
FACTOR = HEAD_DIM ** (-0.5)
SHARDS = 4
PARTS = 8
BLOCK = 256
FF_CHUNK = 1280
VMEM_LIMIT = 60 << 20

def product(left_side, right_side):
    return lax.dot_general(left_side, right_side, (((1,), (0,)), ((), ())), preferred_element_type=jnp.float32)


def product_transposed(left_side, right_side):
    return lax.dot_general(left_side, right_side, (((1,), (1,)), ((), ())), preferred_element_type=jnp.float32)


def product_outer(left_side, right_side):
    return lax.dot_general(left_side, right_side, (((0,), (0,)), ((), ())), preferred_element_type=jnp.float32)


def norm_forward(values, norm_gain, norm_shift):
    center = values - jnp.mean(values, axis=-1, keepdims=True)
    inverse = lax.rsqrt(jnp.mean(center * center, axis=-1, keepdims=True) + EPSILON)
    normed = center * inverse
    return (normed * norm_gain + norm_shift, normed, inverse)


def norm_backward(upstream, normed, inverse, norm_gain):
    scaled = upstream * norm_gain
    return inverse * (
        scaled
        - jnp.mean(scaled, axis=-1, keepdims=True)
        - normed * jnp.mean(scaled * normed, axis=-1, keepdims=True)
    )


def copy_piece(source, target, row, columns, sem):
    start = pl.multiple_of(row, 16)
    pltpu.make_async_copy(source, target.at[pl.ds(start, source.shape[0]), columns], sem).start()


def start_shard(pieces, place, distance, target, source_columns, columns, sem):
    own, steps = pieces[0], pieces[1:SHARDS]
    together = len(steps[0].shape) == 3
    parts = pieces[2:] if together else pieces[SHARDS:]
    base = place[distance] * own.shape[0]
    if distance == 0:
        copy_piece(own.at[:, source_columns], target, base, columns, sem)
        return
    part_rows = own.shape[0] // (PARTS * 16) * 16
    for source in range(PARTS):
        if len(parts) == PARTS:
            part = parts[source].at[distance - 1, pl.ds(0, part_rows), source_columns]
        else:
            part = parts[(distance - 1) * PARTS + source].at[:, source_columns]
        row = base + place[SHARDS + source] * part_rows
        copy_piece(part, target, row, columns, sem)
    left = own.shape[0] - PARTS * part_rows
    base += PARTS * part_rows
    if left > RANK:
        left //= SHARDS
        for source in range(SHARDS):
            rest = parts[source].at[distance - 1, pl.ds(part_rows, left), source_columns]
            copy_piece(rest, target, base + place[SHARDS + source] // 2 * left, columns, sem)
        return
    step = steps[0].at[place[distance]] if together else steps[distance - 1]
    copy_piece(step.at[pl.ds(part_rows, left), source_columns], target, base, columns, sem)


def start_columns(pieces, place, target, source_columns, columns, sem):
    for distance in range(SHARDS):
        start_shard(pieces, place, distance, target, source_columns, columns, sem)


def wait_rows(target, start, rows, columns, sem):
    whole = target.at[pl.ds(start, rows), columns]
    pltpu.make_async_copy(whole, whole, sem).wait()


def widen(wide, low):
    rows = wide.shape[0]
    fill = jnp.zeros((rows, PADDED - wide.shape[1] - low.shape[1]), jnp.bfloat16)
    return jnp.concatenate([wide, low, fill], axis=1)


def blocks_of(rows):
    return [pl.ds(start, BLOCK) for start in range(0, rows, BLOCK)]


HBM = pl.BlockSpec(memory_space=pl.ANY)


def whole_of(array):
    shape = array.shape
    return pl.BlockSpec(shape, lambda *_: (0,) * len(shape))


def call(kernel, name, grid, place, inputs, pieces, in_specs, outs, out_specs, scratch, macs, aliases={}):
    return pl.pallas_call(
        kernel,
        grid_spec=pltpu.PrefetchScalarGridSpec(
            num_scalar_prefetch=1,
            grid=grid,
            in_specs=in_specs + [HBM] * len(pieces),
            out_specs=out_specs,
            scratch_shapes=scratch,
        ),
        out_shape=outs,
        input_output_aliases=aliases,
        compiler_params=pltpu.CompilerParams(vmem_limit_bytes=VMEM_LIMIT),
        cost_estimate=pl.CostEstimate(flops=2 * macs, bytes_accessed=1 << 22, transcendentals=0),
        name=name,
    )(place, *inputs, *pieces)


def out_of(shape, kind):
    return jax.ShapeDtypeStruct(shape, kind)


def picked(width, column=lambda *grid: 0):
    return pl.BlockSpec((None, RANK, width), lambda c, place: (place[SHARDS + PARTS], 0, column(c)))


def column_block(rows, width):
    return pl.BlockSpec((rows, width), lambda c, *_: (0, c))


def row_block(width):
    return pl.BlockSpec((BLOCK, width), lambda r, *_: (r, 0))


def keys_kernel(place, x_ref, gain, shift, bias, a_in, a_out, *more):
    pieces, (first_ref, low_ref, kv_ref, w, wide, sems) = more[:-6], more[-6:]
    rows, features = x_ref.shape

    @pl.when(pl.program_id(0) == 0)
    def _():
        fetch_columns(pieces, place, w, sems, 0, 1)
        for slot in range(2):
            clear_tail(w.at[slot], features)
        for block in blocks_of(rows):
            normed_in, _, _ = norm_forward(x_ref[block, :].astype(jnp.float32), gain[...], shift[...])
            first = normed_in.astype(jnp.bfloat16)
            low = product_transposed(first, a_in[...]).astype(jnp.bfloat16)
            first_ref[block, :] = first
            low_ref[block, :] = low
            wide[block, :] = widen(first, low)

    slot = next_columns(pieces, place, w, sems, features, 1)
    w[slot, pl.ds(features, RANK), :] = a_out[...]
    for block in blocks_of(rows):
        kv_ref[block, :] = (product(wide[block, :], w[slot]) + bias[...]).astype(jnp.bfloat16)


def fetch_columns(pieces, place, w, sems, c, offset=0):
    width = w.shape[2]
    columns = pl.ds(pl.multiple_of((c + offset) * width, 128), width)
    start_columns(pieces, place, w.at[c % 2], columns, pl.ds(0, width), sems.at[c % 2])


def next_columns(pieces, place, w, sems, features, offset=0):
    step, steps = pl.program_id(0), pl.num_programs(0)

    @pl.when(step + 1 < steps)
    def _():
        fetch_columns(pieces, place, w, sems, step + 1, offset)

    slot = lax.rem(step, 2)
    wait_rows(w.at[slot], 0, features, pl.ds(0, w.shape[2]), sems.at[slot])
    return slot


def clear_tail(w, features):
    count = w.shape[0] - features - RANK
    w[pl.ds(features + RANK, count), :] = jnp.zeros((count, w.shape[1]), jnp.bfloat16)


def keys_call(place, x, gain, shift, bias, a_in, a_out, pieces):
    rows, features = x.shape
    width = PADDED
    third = lambda height: pl.BlockSpec((height, width), lambda c, *_: (0, c + 1))
    return call(
        keys_kernel, "keys", (2,), place, [x, gain, shift, bias, a_in, a_out], pieces,
        [whole_of(x), whole_of(gain), whole_of(shift), third(1), picked(features), third(RANK)],
        [out_of((rows, features), jnp.bfloat16), out_of((rows, RANK), jnp.bfloat16), out_of((rows, 2 * width), jnp.bfloat16)],
        [whole_of(x), pl.BlockSpec((rows, RANK), lambda *_: (0, 0)), column_block(rows, width)],
        [pltpu.VMEM((2, PADDED, width), jnp.bfloat16), pltpu.VMEM((rows, PADDED), jnp.bfloat16), pltpu.SemaphoreType.DMA((2,))],
        rows * features * 2 * width,
    )


def queries_kernel(place, first_ref, low_ref, bias, a_out, *more):
    pieces, (q_ref, w, sems) = more[:-3], more[-3:]
    rows, features = first_ref.shape
    width = w.shape[1]
    halves = [pl.ds(0, width // 256 * 128), pl.ds(width // 256 * 128, width - width // 256 * 128)]
    for half, columns in enumerate(halves):
        start_columns(pieces, place, w, columns, columns, sems.at[half])
    clear_tail(w, features)
    w[pl.ds(features, RANK), :] = a_out[...]
    for half, columns in enumerate(halves):
        wait_rows(w, 0, features, columns, sems.at[half])
        for block in blocks_of(rows):
            wide = widen(first_ref[block, :], low_ref[block, :])
            q_ref[block, columns] = (product(wide, w[:, columns]) + bias[:, columns]).astype(jnp.bfloat16)


def queries_call(place, first, low, bias, a_out, pieces):
    rows, features = first.shape
    width = PADDED
    return call(
        queries_kernel, "queries", (1,), place, [first, low, bias, a_out], pieces,
        [whole_of(first), whole_of(low), column_block(1, width), column_block(RANK, width)],
        out_of((rows, width), jnp.bfloat16),
        column_block(rows, width),
        [pltpu.VMEM((PADDED, width), jnp.bfloat16), pltpu.SemaphoreType.DMA((2,))],
        rows * features * width,
    )


def out_kernel(place, x_ref, mixed_ref, gain, shift, bias, a_in, a_out, u_in, *more):
    pieces, (hidden_ref, second_ref, low_ref, up_low_ref, w, sem) = more[:-6], more[-6:]
    features = x_ref.shape[1]

    @pl.when(pl.program_id(0) == 0)
    def _():
        start_columns(pieces, place, w, pl.ds(0, features), pl.ds(0, features), sem)
        w[pl.ds(features, RANK), :] = a_out[...]
        w[pl.ds(features + RANK, PADDED - features - RANK), :] = jnp.zeros(
            (PADDED - features - RANK, features), jnp.bfloat16
        )
        wait_rows(w, 0, features, pl.ds(0, features), sem)

    mixed = mixed_ref[:, :features]
    low = product_transposed(mixed, a_in[...]).astype(jnp.bfloat16)
    hidden = x_ref[...].astype(jnp.float32) + (product(widen(mixed, low), w[...]) + bias[...])
    normed_mid, _, _ = norm_forward(hidden, gain[...], shift[...])
    second = normed_mid.astype(jnp.bfloat16)
    hidden_ref[...] = hidden
    second_ref[...] = second
    low_ref[...] = low
    up_low_ref[...] = product_transposed(second, u_in[...]).astype(jnp.bfloat16)


def out_call(place, x, mixed, gain, shift, bias, a_in, a_out, u_in, pieces):
    rows, features = x.shape
    return call(
        out_kernel, "out", (rows // BLOCK,), place, [x, mixed, gain, shift, bias, a_in, a_out, u_in], pieces,
        [row_block(features), row_block(PADDED)] + [whole_of(a) for a in (gain, shift, bias)] + [picked(features)] * 3,
        [out_of((rows, features), jnp.float32), out_of((rows, features), jnp.bfloat16), out_of((rows, RANK), jnp.bfloat16), out_of((rows, RANK), jnp.bfloat16)],
        [row_block(features), row_block(features), row_block(RANK), row_block(RANK)],
        [pltpu.VMEM((PADDED, features), jnp.bfloat16), pltpu.SemaphoreType.DMA(())],
        rows * features * features,
    )


def fetch_down(pieces, place, w, sems, first=0, last=None):
    width = w.shape[1]
    shard_rows = w.shape[0] // SHARDS
    last = w.shape[0] // FF_CHUNK if last is None else last
    for shard in range(SHARDS):
        if shard * shard_rows >= last * FF_CHUNK or (shard + 1) * shard_rows <= first * FF_CHUNK:
            continue
        for distance in range(SHARDS):
            @pl.when(place[distance] == shard)
            def _():
                start_shard(pieces, place, distance, w, pl.ds(0, width), pl.ds(0, width), sems.at[shard])


def wait_down(step, w, sems, first=0, last=None):
    shard_rows = w.shape[0] // SHARDS
    last = w.shape[0] // FF_CHUNK if last is None else last
    for shard in range(SHARDS):
        if shard * shard_rows >= last * FF_CHUNK or (shard + 1) * shard_rows <= first * FF_CHUNK:
            continue
        first_step = max(first, -(-(shard * shard_rows - FF_CHUNK + 1) // FF_CHUNK))

        @pl.when(step == first_step)
        def _():
            wait_rows(w, shard * shard_rows, shard_rows, pl.ds(0, w.shape[1]), sems.at[shard])


def active_grad_kernel(first, last, place, cot_ref, a_in, a_out, *more):
    pieces, (g_ref, low_ref, w, sems) = more[:-4], more[-4:]
    pieces = pieces[: len(pieces) - (2 if first else 0)]
    rows, features = cot_ref.shape
    step = pl.program_id(0) + first

    @pl.when(step == first)
    def _():
        fetch_down(pieces, place, w, sems, first, last)
        for block in blocks_of(rows):
            low_ref[block, :] = product_transposed(cot_ref[block, :], a_out[...]).astype(jnp.bfloat16)

    wait_down(step, w, sems, first, last)
    weight = w[pl.ds(pl.multiple_of(step * FF_CHUNK, FF_CHUNK), FF_CHUNK), :]
    for block in blocks_of(rows):
        g_ref[block, :] = (
            product_transposed(cot_ref[block, :], weight) + product(low_ref[block, :], a_in[...])
        ).astype(jnp.bfloat16)


def active_grad_call(place, cot, a_in, a_out, pieces, first, last, written=()):
    rows, features = cot.shape
    units = a_in.shape[2]
    chunk = lambda height: pl.BlockSpec((height, FF_CHUNK), lambda c, *_: (0, c + first))
    return call(
        partial(active_grad_kernel, first, last), "active_grad", (last - first,), place, [cot, a_in, a_out],
        [*pieces, *written],
        [whole_of(cot), picked(FF_CHUNK, lambda c: c + first), picked(features)],
        [out_of((rows, units), jnp.bfloat16), out_of((rows, RANK), jnp.bfloat16)],
        [chunk(rows), pl.BlockSpec((rows, RANK), lambda *_: (0, 0))],
        [pltpu.VMEM((units, features), jnp.bfloat16), pltpu.SemaphoreType.DMA((SHARDS,))],
        rows * features * FF_CHUNK * (last - first),
        {4 + len(pieces) + place: place for place in range(len(written))},
    )


GELU_A = 0.7978845608
GELU_B = 0.044715


def up_kernel(place, second_ref, up_low_ref, g_active_ref, g_low_ref, bias, u_out, d_in, *more):
    pieces, (active_ref, acc_ref, down_low_ref, g_up_out_ref, g_down_in_ref, w, wide, low_scr, g_scr, sems) = more[:-10], more[-10:]
    rows, features = second_ref.shape
    step, steps = pl.program_id(0), pl.num_programs(0)
    width = w.shape[2]

    def fetch(c):
        columns = pl.ds(pl.multiple_of(c * width, 128), width)
        start_columns(pieces, place, w.at[c % 2], columns, pl.ds(0, width), sems.at[c % 2])

    @pl.when(step == 0)
    def _():
        fetch(0)
        for slot in range(2):
            w[slot, pl.ds(features + RANK, PADDED - features - RANK), :] = jnp.zeros(
                (PADDED - features - RANK, width), jnp.bfloat16
            )
        acc_ref[...] = jnp.zeros_like(acc_ref)
        low_scr[...] = jnp.zeros_like(low_scr)
        for block in blocks_of(rows):
            wide[block, :] = widen(second_ref[block, :], up_low_ref[block, :])

    @pl.when(step + 1 < steps)
    def _():
        fetch(step + 1)

    slot = lax.rem(step, 2)
    wait_rows(w.at[slot], 0, features, pl.ds(0, width), sems.at[slot])
    w[slot, pl.ds(features, RANK), :] = u_out[...]
    blocks = blocks_of(rows)
    ahead = product(wide[blocks[0], :], w[slot])
    for number, block in enumerate(blocks):
        upper = ahead + bias[...]
        if number + 1 < len(blocks):
            ahead = product(wide[blocks[number + 1], :], w[slot])
        square = upper * upper
        inner = jnp.tanh(upper * (GELU_A + (GELU_A * GELU_B) * square))
        half = 0.5 + 0.5 * inner
        active = (upper * half).astype(jnp.bfloat16)
        slope = half + upper * (1.0 - inner * inner) * (0.5 * GELU_A + (1.5 * GELU_A * GELU_B) * square)
        g_upper = (g_active_ref[block, :].astype(jnp.float32) * slope).astype(jnp.bfloat16)
        active_ref[block, :] = active
        g_scr[block, :] = g_upper
        acc_ref[block, :] += product_transposed(g_upper, w[slot])
        low_scr[block, :] += product_transposed(active, d_in[...])
    g_up_out_ref[...] = product_outer(up_low_ref[...], g_scr[...])
    g_down_in_ref[...] = product_outer(g_low_ref[...], active_ref[...])

    @pl.when(step == steps - 1)
    def _():
        down_low_ref[...] = low_scr[...].astype(jnp.bfloat16)


def up_call(place, second, up_low, g_active, g_low, bias, u_out, d_in, pieces):
    rows, features = second.shape
    units = bias.shape[1]
    low_block = pl.BlockSpec((rows, RANK), lambda *_: (0, 0))
    return call(
        up_kernel, "up", (units // FF_CHUNK,), place, [second, up_low, g_active, g_low, bias, u_out, d_in], pieces,
        [whole_of(second), low_block, column_block(rows, FF_CHUNK), low_block,
         column_block(1, FF_CHUNK), picked(FF_CHUNK, lambda c: c), picked(FF_CHUNK, lambda c: c)],
        [out_of((rows, units), jnp.bfloat16), out_of((rows, PADDED), jnp.float32), out_of((rows, RANK), jnp.bfloat16),
         out_of((RANK, units), jnp.float32), out_of((RANK, units), jnp.float32)],
        [column_block(rows, FF_CHUNK), pl.BlockSpec((rows, PADDED), lambda *_: (0, 0)), low_block,
         column_block(RANK, FF_CHUNK), column_block(RANK, FF_CHUNK)],
        [pltpu.VMEM((2, PADDED, FF_CHUNK), jnp.bfloat16), pltpu.VMEM((rows, PADDED), jnp.bfloat16), pltpu.VMEM((rows, RANK), jnp.float32),
         pltpu.VMEM((rows, FF_CHUNK), jnp.bfloat16), pltpu.SemaphoreType.DMA((2,))],
        2 * rows * features * units,
    )


def out_grad_kernel(place, acc_ref, hidden_ref, second_ref, cot_ref, mixed_ref, low_ref, down_low_ref, gain, u_in, a_in, a_out, *more):
    pieces, (g_hidden_ref, g_mixed_ref, g_up_in, g_out_out, g_out_in, g_down_out, w, sem) = more[:-8], more[-8:]
    features = hidden_ref.shape[1]
    step = pl.program_id(0)

    @pl.when(step == 0)
    def _():
        start_columns(pieces, place, w, pl.ds(0, features), pl.ds(0, features), sem)
        w[pl.ds(features, RANK), :] = a_out[...]
        w[pl.ds(features + RANK, PADDED - features - RANK), :] = jnp.zeros(
            (PADDED - features - RANK, features), jnp.bfloat16
        )

    g_up_low = acc_ref[:, features : features + RANK].astype(jnp.bfloat16)
    g_second = acc_ref[:, :features] + product(g_up_low, u_in[...])
    _, normed, inverse = norm_forward(hidden_ref[...], gain[...], 0.0)
    cot = cot_ref[...]
    g_hidden = cot.astype(jnp.float32) + norm_backward(g_second, normed, inverse, gain[...])
    g_branch = g_hidden.astype(jnp.bfloat16)
    g_hidden_ref[...] = g_hidden

    @pl.when(step == 0)
    def _():
        wait_rows(w, 0, features, pl.ds(0, features), sem)

    back = product_transposed(g_branch, w[...])
    g_low = back[:, features : features + RANK].astype(jnp.bfloat16)
    g_mixed = back[:, :features] + product(g_low, a_in[...])
    g_mixed_ref[:, :features] = g_mixed.astype(jnp.bfloat16)
    g_mixed_ref[:, features:] = jnp.zeros((BLOCK, PADDED - features), jnp.bfloat16)
    sums = (
        product_outer(g_up_low, second_ref[...]),
        product_outer(low_ref[...], g_branch),
        product_outer(g_low, mixed_ref[:, :features]),
        product_outer(down_low_ref[...], cot),
    )
    for total, term in zip((g_up_in, g_out_out, g_out_in, g_down_out), sums):
        @pl.when(step == 0)
        def _():
            total[...] = term

        @pl.when(step > 0)
        def _():
            total[...] += term


def out_grad_call(place, acc, hidden, second, cot, mixed, low, down_low, gain, u_in, a_in, a_out, pieces):
    rows, features = hidden.shape
    small = pl.BlockSpec((RANK, features), lambda *_: (0, 0))
    return call(
        out_grad_kernel, "out_grad", (rows // BLOCK,), place,
        [acc, hidden, second, cot, mixed, low, down_low, gain, u_in, a_in, a_out], pieces,
        [row_block(PADDED), row_block(features), row_block(features), row_block(features), row_block(PADDED),
         row_block(RANK), row_block(RANK), whole_of(gain)] + [picked(features)] * 3,
        [out_of((rows, features), jnp.float32), out_of((rows, PADDED), jnp.bfloat16)] + [out_of((RANK, features), jnp.float32)] * 4,
        [row_block(features), row_block(PADDED)] + [small] * 4,
        [pltpu.VMEM((PADDED, features), jnp.bfloat16), pltpu.SemaphoreType.DMA(())],
        rows * features * features,
    )


def down_kernel(place, active_ref, hidden_ref, down_low_ref, bias, a_out, *more):
    pieces, (out_ref, w, acc, hidden, sems, late) = more[:-6], more[-6:]
    rows, features = hidden_ref.shape
    step, steps = pl.program_id(0), pl.num_programs(0)
    copy = pltpu.make_async_copy(hidden_ref, hidden, late)

    @pl.when(step == 0)
    def _():
        fetch_down(pieces, place, w, sems)
        copy.start()
        for block in blocks_of(rows):
            acc[block, :] = product(down_low_ref[block, :], a_out[...]) + bias[...]

    wait_down(step, w, sems)
    weight = w[pl.ds(pl.multiple_of(step * FF_CHUNK, FF_CHUNK), FF_CHUNK), :]
    for block in blocks_of(rows):
        acc[block, :] += product(active_ref[block, :], weight)

    @pl.when(step == steps - 1)
    def _():
        copy.wait()
        for block in blocks_of(rows):
            out_ref[:, block] = (hidden[block, :] + acc[block, :]).astype(jnp.bfloat16).T


def down_call(place, active, hidden, down_low, bias, a_out, pieces):
    rows, features = hidden.shape
    units = active.shape[1]
    return call(
        down_kernel, "down", (units // FF_CHUNK,), place, [active, hidden, down_low, bias, a_out], pieces,
        [column_block(rows, FF_CHUNK), HBM, pl.BlockSpec((rows, RANK), lambda *_: (0, 0)),
         whole_of(bias), picked(features)],
        out_of((features, rows), jnp.bfloat16),
        pl.BlockSpec((features, rows), lambda *_: (0, 0)),
        [pltpu.VMEM((units, features), jnp.bfloat16), pltpu.VMEM((rows, features), jnp.float32), pltpu.VMEM((rows, features), jnp.float32),
         pltpu.SemaphoreType.DMA((SHARDS,)), pltpu.SemaphoreType.DMA(())],
        rows * features * units,
    )


def tokens_grad_kernel(place, x_ref, first_ref, low_ref, g_hidden_ref, gain, a_in, a_out, near_ref, far_ref, *more):
    pieces, (out_ref, g_qkv_out, g_qkv_in, w, acc, x, first, g_hidden, sems, late) = more[:-10], more[-10:]
    rows, features = x_ref.shape
    step, steps = pl.program_id(0), pl.num_programs(0)
    pairs = ((x_ref, x), (first_ref, first), (g_hidden_ref, g_hidden))
    copies = [pltpu.make_async_copy(*pair, late.at[number]) for number, pair in enumerate(pairs)]

    @pl.when(step == 0)
    def _():
        fetch_columns(pieces, place, w, sems, 0)
        for slot in range(2):
            clear_tail(w.at[slot], features)
        acc[...] = jnp.zeros_like(acc)

    @pl.when(step == 1)
    def _():
        for copy in copies:
            copy.start()

    slot = next_columns(pieces, place, w, sems, features)
    w[slot, pl.ds(features, RANK), :] = a_out[...]
    scale = jnp.where(step > 0, 1.0, 0.0)
    qkv_out_sum = jnp.zeros(g_qkv_out.shape, jnp.float32)
    for block in blocks_of(rows):
        g = (near_ref[block, :].astype(jnp.float32) + scale * far_ref[block, :].astype(jnp.float32)).astype(jnp.bfloat16)
        acc[block, :] += product_transposed(g, w[slot])
        qkv_out_sum += product_outer(low_ref[block, :], g)
    g_qkv_out[...] = qkv_out_sum

    @pl.when(step == steps - 1)
    def _():
        for copy in copies:
            copy.wait()
        qkv_in_sum = jnp.zeros((RANK, features), jnp.float32)
        for block in blocks_of(rows):
            g_low = acc[block, pl.ds(features, RANK)].astype(jnp.bfloat16)
            g_first = acc[block, pl.ds(0, features)] + product(g_low, a_in[...])
            _, normed, inverse = norm_forward(x[block, :].astype(jnp.float32), gain[...], 0.0)
            out_ref[:, block] = (g_hidden[block, :] + norm_backward(g_first, normed, inverse, gain[...])).T
            qkv_in_sum += product_outer(g_low, first[block, :])
        g_qkv_in[...] = qkv_in_sum


def tokens_grad_call(place, x, first, low, g_hidden, gain, a_in, a_out, near, far, pieces):
    rows, features = x.shape
    steps = 3
    near_block = pl.BlockSpec((None, rows, PADDED), lambda c, *_: (c, 0, 0))
    far_block = pl.BlockSpec((None, rows, PADDED), lambda c, *_: (jnp.maximum(c - 1, 0), 0, 0))
    return call(
        tokens_grad_kernel, "tokens_grad", (steps,), place, [x, first, low, g_hidden, gain, a_in, a_out, near, far], pieces,
        [HBM, HBM, whole_of(low), HBM, whole_of(gain), picked(features),
         column_block(RANK, PADDED), near_block, far_block],
        [out_of((features, rows), jnp.float32), out_of((RANK, steps * PADDED), jnp.float32), out_of((RANK, features), jnp.float32)],
        [pl.BlockSpec((features, rows), lambda *_: (0, 0)), column_block(RANK, PADDED),
         pl.BlockSpec((RANK, features), lambda *_: (0, 0))],
        [pltpu.VMEM((2, PADDED, PADDED), jnp.bfloat16), pltpu.VMEM((rows, PADDED), jnp.float32),
         pltpu.VMEM((rows, features), jnp.bfloat16), pltpu.VMEM((rows, features), jnp.bfloat16), pltpu.VMEM((rows, features), jnp.float32),
         pltpu.SemaphoreType.DMA((2,)), pltpu.SemaphoreType.DMA((3,))],
        rows * features * steps * PADDED,
    )


def combine_kernel(widths, numbers, *refs):
    parts, totals = refs[: -len(widths)], refs[-len(widths) :]
    sequences, _, part_width = parts[0].shape
    half_width = part_width - 128

    def add(halves):
        start = 0
        for total, spans in zip(totals, widths):
            into = 0
            for width in spans:
                done = 0
                while done < width:
                    half, at = divmod(start + done, half_width)
                    size = min(width - done, half_width - at)
                    for sequence in range(sequences):
                        target = (numbers[sequence], slice(None), pl.ds(into + done, size))
                        total[target] += halves[half][sequence, :, pl.ds(at, size)].astype(jnp.float32)
                    done += size
                into += width
                start += -(-width // 128) * 128

    for total in totals:
        total[...] = jnp.zeros_like(total)
    turned = numbers[sequences]

    @pl.when(turned == 0)
    def _():
        add(parts)

    if len(parts) == 2:
        @pl.when(turned == 1)
        def _():
            add(parts[::-1])


def combine_call(numbers, parts, widths):
    shapes = [(ADAPTERS, RANK, sum(spans)) for spans in widths]
    return pl.pallas_call(
        partial(combine_kernel, widths),
        grid_spec=pltpu.PrefetchScalarGridSpec(
            num_scalar_prefetch=1,
            grid=(1,),
            in_specs=[whole_of(part) for part in parts],
            out_specs=[pl.BlockSpec(shape, lambda *_: (0, 0, 0)) for shape in shapes],
        ),
        out_shape=[out_of(shape, jnp.float32) for shape in shapes],
        compiler_params=pltpu.CompilerParams(vmem_limit_bytes=VMEM_LIMIT),
        cost_estimate=pl.CostEstimate(flops=1 << 30, bytes_accessed=1 << 22, transcendentals=0),
        name="combine",
    )(numbers, *parts)


TILE = 256
REACH_TILES = WINDOW // TILE
SPAN_TILES = REACH_TILES + 1


def split_pair(pair):
    lane = lax.broadcasted_iota(jnp.int32, pair.shape, 1)
    zero = jnp.zeros_like(pair)
    return jnp.concatenate(
        [jnp.where(lane < HEAD_DIM, pair, zero), jnp.where(lane >= HEAD_DIM, pair, zero)], axis=0
    )


def join_pair(stacked):
    lane = lax.broadcasted_iota(jnp.int32, (TILE, 128), 1)
    return jnp.where(lane < HEAD_DIM, stacked[:TILE], stacked[TILE:])


def tile_bias(bounds, query_start, key_start):
    rows = query_start + lax.broadcasted_iota(jnp.int32, (TILE, 1), 0)
    columns = key_start + lax.broadcasted_iota(jnp.int32, (1, TILE), 1)
    row_doc = sum((rows >= bound).astype(jnp.int32) for bound in bounds)
    column_doc = sum((columns >= bound).astype(jnp.int32) for bound in bounds)
    shape = (TILE, TILE)
    distance = jnp.broadcast_to(rows, shape) - jnp.broadcast_to(columns, shape)
    same = jnp.broadcast_to(row_doc, shape) == jnp.broadcast_to(column_doc, shape)
    seen = jnp.broadcast_to(columns, shape) >= 0
    return jnp.where(same & seen & (distance >= 0) & (distance < WINDOW), 0.0, MASKED)


def fill_biases(meta, bias_scr, tiles):
    bounds = [meta[place] for place in range(3)]
    first = meta[3]

    def one(step, carry):
        tile = step // SPAN_TILES
        key_tile = tile + lax.rem(step, SPAN_TILES) - REACH_TILES
        bias_scr[step] = tile_bias(bounds, first + tile * TILE, first + key_tile * TILE)
        return carry

    lax.fori_loop(0, tiles * SPAN_TILES, one, 0)


def key_tile(far_ref, near_ref, tile):
    if tile < REACH_TILES:
        return far_ref[pl.ds(tile * TILE, TILE), :]
    return near_ref[pl.ds((tile - REACH_TILES) * TILE, TILE), :]


def attend_forward_kernel(tiles, meta, q_ref, k_far, v_far, k_near, v_near, *more):
    o_ref, lse_ref, bias_scr, acc_scr = more[-4:]

    @pl.when(pl.program_id(0) == 0)
    def _():
        fill_biases(meta, bias_scr, tiles)

    ones = jnp.ones((TILE, 128), jnp.bfloat16)
    chunk = TILE // 2
    for tile in range(tiles):
        stacked = split_pair(q_ref[pl.ds(tile * TILE, TILE), :] * FACTOR)
        span = range(tile, tile + SPAN_TILES)
        keys = jnp.concatenate([key_tile(k_far, k_near, t) for t in span], axis=0)
        values = jnp.concatenate(
            [jnp.concatenate([key_tile(v_far, v_near, t), ones], axis=1) for t in span], axis=0
        )
        for part in range(2 * TILE // chunk):
            start = part * chunk
            bias_rows = pl.ds(start % TILE, chunk)
            bias = jnp.concatenate(
                [bias_scr[tile * SPAN_TILES + t, bias_rows, :] for t in range(SPAN_TILES)], axis=1
            )
            scores = product_transposed(stacked[start : start + chunk], keys) + bias
            highest = jnp.max(scores, axis=1, keepdims=True)
            mixed = product(jnp.exp(scores - highest).astype(jnp.bfloat16), values)
            summed = mixed[:, 128:]
            acc_scr[pl.ds(start, chunk), :] = mixed[:, :128] / summed
            lse_ref[pl.ds(tile * 2 * TILE + start, chunk), :] = highest + jnp.log(summed)
        o_ref[pl.ds(tile * TILE, TILE), :] = join_pair(acc_scr[...]).astype(jnp.bfloat16)


def pair_columns(rows, offset=0):
    return pl.BlockSpec((rows, 128), lambda j, *_: (0, offset + j))


def attention_cost(products, pairs, rows):
    macs = products * pairs * 2 * rows * SPAN_TILES * TILE * 256
    return pl.CostEstimate(flops=2 * macs, bytes_accessed=1 << 24, transcendentals=0)


def attend_forward(meta, queries, far, near, start, pairs, written=()):
    rows = queries.shape[0]
    tiles = rows // TILE
    return pl.pallas_call(
        partial(attend_forward_kernel, tiles),
        grid_spec=pltpu.PrefetchScalarGridSpec(
            num_scalar_prefetch=1,
            grid=(pairs,),
            in_specs=[
                pair_columns(rows, start), pair_columns(WINDOW, start), pair_columns(WINDOW, PAIRS + start),
                pair_columns(rows, start), pair_columns(rows, PAIRS + start),
            ] + [pl.BlockSpec(memory_space=pl.ANY)] * len(written),
            out_specs=[
                pair_columns(rows, start),
                pl.BlockSpec((None, 2 * rows, 128), lambda j, *_: (start + j, 0, 0)),
            ],
            scratch_shapes=[
                pltpu.VMEM((tiles * SPAN_TILES, TILE, TILE), jnp.float32),
                pltpu.VMEM((2 * TILE, 128), jnp.float32),
            ],
        ),
        out_shape=[
            jax.ShapeDtypeStruct((rows, PADDED), jnp.bfloat16),
            jax.ShapeDtypeStruct((PAIRS, 2 * rows, 128), jnp.float32),
        ],
        input_output_aliases={6 + place: place for place in range(len(written))},
        compiler_params=pltpu.CompilerParams(vmem_limit_bytes=VMEM_LIMIT),
        cost_estimate=attention_cost(2, pairs, rows),
        name="attend_forward",
    )(meta, queries, far, far, near, near, *written)


def attend_backward_kernel(
    tiles, meta, q_ref, k_far, v_far, k_near, v_near, g_ref, o_ref, lse_ref,
    near_ref, far_ref, bias_scr, dq_scr, dkt, dvt,
):
    @pl.when(pl.program_id(0) == 0)
    def _():
        fill_biases(meta, bias_scr, tiles)

    dkt[...] = jnp.zeros_like(dkt)
    dvt[...] = jnp.zeros_like(dvt)
    for tile in range(tiles):
        rows = pl.ds(tile * TILE, TILE)
        queries = split_pair(q_ref[rows, :] * FACTOR)
        grads = split_pair(g_ref[rows, :])
        mixed = o_ref[rows, :].astype(jnp.float32)
        centered = jnp.sum(
            grads.astype(jnp.float32) * jnp.concatenate([mixed, mixed], axis=0), axis=1, keepdims=True
        )
        lse = lse_ref[pl.ds(tile * 2 * TILE, 2 * TILE), :]
        lse = jnp.concatenate([lse, lse], axis=1)
        queries_t = queries.T
        grads_t = grads.T
        dq_scr[...] = jnp.zeros_like(dq_scr)
        for t in range(SPAN_TILES):
            keys = key_tile(k_far, k_near, tile + t)
            bias = bias_scr[tile * SPAN_TILES + t]
            scores = product_transposed(queries, keys)
            chances = jnp.exp(scores + jnp.concatenate([bias, bias], axis=0) - lse)
            grad_chances = product_transposed(grads, key_tile(v_far, v_near, tile + t))
            grad_scores = (chances * (grad_chances - centered)).astype(jnp.bfloat16)
            dvt[tile + t] += product(grads_t, chances.astype(jnp.bfloat16))
            dkt[tile + t] += product(queries_t, grad_scores)
            dq_scr[...] += product(grad_scores, keys)
        near_ref[0, rows, :] = (join_pair(dq_scr[...]) * FACTOR).astype(jnp.bfloat16)
    for t in range(tiles + REACH_TILES):
        target, first = (far_ref, 0) if t < REACH_TILES else (near_ref, 1)
        rows = pl.ds((t if t < REACH_TILES else t - REACH_TILES) * TILE, TILE)
        target[first, rows, :] = dkt[t].T.astype(jnp.bfloat16)
        target[first + 1, rows, :] = dvt[t].T.astype(jnp.bfloat16)


def attend_backward(meta, queries, far, near, grad_mixed, mixed, lse):
    rows = queries.shape[0]
    tiles = rows // TILE
    return pl.pallas_call(
        partial(attend_backward_kernel, tiles),
        grid_spec=pltpu.PrefetchScalarGridSpec(
            num_scalar_prefetch=1,
            grid=(PAIRS,),
            in_specs=[
                pair_columns(rows), pair_columns(WINDOW), pair_columns(WINDOW, PAIRS),
                pair_columns(rows), pair_columns(rows, PAIRS), pair_columns(rows), pair_columns(rows),
                pl.BlockSpec((None, 2 * rows, 128), lambda j, *_: (j, 0, 0)),
            ],
            out_specs=[
                pl.BlockSpec((3, rows, 128), lambda j, *_: (0, 0, j)),
                pl.BlockSpec((2, WINDOW, 128), lambda j, *_: (0, 0, j)),
            ],
            scratch_shapes=[
                pltpu.VMEM((tiles * SPAN_TILES, TILE, TILE), jnp.float32),
                pltpu.VMEM((2 * TILE, 128), jnp.float32),
                pltpu.VMEM((tiles + REACH_TILES, 128, TILE), jnp.float32),
                pltpu.VMEM((tiles + REACH_TILES, 128, TILE), jnp.float32),
            ],
        ),
        out_shape=[
            jax.ShapeDtypeStruct((3, rows, PADDED), jnp.bfloat16),
            jax.ShapeDtypeStruct((2, WINDOW, PADDED), jnp.bfloat16),
        ],
        compiler_params=pltpu.CompilerParams(vmem_limit_bytes=VMEM_LIMIT),
        cost_estimate=attention_cost(5, PAIRS, rows),
        name="attend_backward",
    )(meta, queries, far, far, near, near, grad_mixed, mixed, lse)


def ring_pairs(size):
    return [(i, (i + 1) % size) for i in range(size)]


def plane_pairs(sizes):
    first, second = [], []
    cores = sizes["ctx"]
    for chip in range(sizes["dp"]):
        for core in range(cores):
            steps = (chip ^ 1, chip ^ 2) if core % 2 == 0 else (chip ^ 2, chip ^ 1)
            here = chip * cores + core
            first.append((here, steps[0] * cores + core))
            second.append((here, steps[1] * cores + core))
    return first, second


def swap_pairs(size):
    return [(i, i ^ 1) for i in range(size)]


def shifted(array, size, by):
    pairs = [(i, i + by) for i in range(size) if 0 <= i + by < size]
    return lax.ppermute(array, "ctx", pairs)


def place_of(chosen):
    chip, core, shard = lax.axis_index("dp"), lax.axis_index("ctx") % 2, lax.axis_index("wt")
    places = [(shard - distance) % SHARDS for distance in range(SHARDS)]
    for side in (core, 1 - core):
        near = jnp.where(side == 0, chip ^ 1, chip ^ 2)
        for where in (chip, near, near ^ 3, chip ^ 3):
            places.append(where * 2 + side)
    return jnp.stack([*places, chosen]).astype(jnp.int32)


def after(array, *others):
    return lax.optimization_barrier((array, *others))[0]


def after_all(arrays, *others):
    return lax.optimization_barrier((*arrays, *others))[: len(arrays)]


def own_part(own):
    rows = own.shape[0] // (PARTS * 16) * 16
    chip, core = lax.axis_index("dp"), lax.axis_index("ctx") % 2
    left = own.shape[0] - PARTS * rows
    first = PARTS * rows
    if left > RANK:
        left //= SHARDS
        first += chip * left
    mine = lax.dynamic_slice_in_dim(own, (chip * 2 + core) * rows, rows, 0)
    return jnp.concatenate([mine, lax.dynamic_slice_in_dim(own, first, left, 0)], axis=0)


def eighth(own, moved):
    rows = own.shape[0] // (PARTS * 16) * 16
    return moved if own.shape[0] - PARTS * rows > RANK else moved[:rows]


def ring(sizes, moved):
    steps = []
    for _ in range(SHARDS - 1):
        moved = lax.ppermute(moved, "wt", ring_pairs(sizes["wt"]))
        steps.append(moved)
    return steps


def direct(sizes, moved):
    size = sizes["wt"]
    return [
        lax.ppermute(moved, "wt", [(i, (i + distance) % size) for i in range(size)])
        for distance in range(1, SHARDS)
    ]


def plane_start(sizes, mine):
    first, second = plane_pairs(sizes)
    return [mine, lax.ppermute(mine, ("dp", "ctx"), first), lax.ppermute(mine, ("dp", "ctx"), second)]


def plane_end(sizes, parts):
    _, second = plane_pairs(sizes)
    return [*parts, lax.ppermute(parts[1], ("dp", "ctx"), second)]


def swap_cores(sizes, parts):
    swap = swap_pairs(sizes["ctx"])
    return [*parts, *[lax.ppermute(part, "ctx", swap) for part in parts]]


def pad_thirds(array, features):
    pieces = []
    for third in range(3):
        piece = array[..., third * features : (third + 1) * features]
        pieces.append(jnp.pad(piece, [(0, 0)] * (array.ndim - 1) + [(0, PADDED - features)]))
    return jnp.concatenate(pieces, axis=-1)


def send_adapters(sizes, terms, chosen):
    flat = jnp.concatenate(
        [jnp.pad(term, ((0, 0), (0, -term.shape[1] % 128))) for term in terms], axis=1
    )
    paired = sizes["ctx"] == 2
    if paired:
        half = flat.shape[1] // 2
        core = lax.axis_index("ctx")
        kept = lax.dynamic_slice_in_dim(flat, core * half, half, 1)
        given = lax.dynamic_slice_in_dim(flat, (1 - core) * half, half, 1)
        flat = kept + lax.ppermute(given, "ctx", swap_pairs(2))
    else:
        flat = lax.psum(flat, "ctx")
    ids = jnp.broadcast_to(chosen.astype(jnp.bfloat16), (RANK, 128))
    return jnp.concatenate([flat.astype(jnp.bfloat16), ids], axis=1)


def share_adapters(sent):
    return lax.all_gather(sent, ("dp", "wt"), axis=0)


def sequence_numbers(sizes, everyone):
    numbers = everyone[:, 0, -1].astype(jnp.int32)
    turned = lax.axis_index("ctx") if sizes["ctx"] == 2 else 0
    return jnp.concatenate([numbers, jnp.full((1,), turned, jnp.int32)])


def both_halves(sizes, everyone):
    if sizes["ctx"] != 2:
        return [everyone]
    return [everyone, lax.ppermute(everyone, "ctx", swap_pairs(2))]


def shards(
    sizes,
    tokens,
    cotangent,
    doc_lengths,
    adapter_ids,
    first_gain,
    first_shift,
    qkv_weight,
    qkv_bias,
    out_weight,
    out_bias,
    second_gain,
    second_shift,
    up_weight,
    up_bias,
    down_weight,
    down_bias,
    qkv_adapt_in,
    qkv_adapt_out,
    out_adapt_in,
    out_adapt_out,
    up_adapt_in,
    up_adapt_out,
    down_adapt_in,
    down_adapt_out,
):
    row_count, feature_count = tokens.shape[1:]
    ctx = sizes["ctx"]
    chosen = adapter_ids[0, 0]
    place = place_of(chosen)

    vectors = [first_gain, first_shift, qkv_bias, out_bias, second_gain, second_shift, up_bias, down_bias]
    lengths = [vector.shape[0] for vector in vectors]
    flat = jnp.concatenate(vectors)
    extra_rows = -(-flat.shape[0] // (3 * PADDED))
    flat = jnp.pad(flat, (0, extra_rows * 3 * PADDED - flat.shape[0])).reshape(extra_rows, -1)

    part_qkv = jnp.concatenate([pad_thirds(own_part(qkv_weight), feature_count), flat], axis=0)
    steps_qkv = ring(sizes, part_qkv)
    parts_qkv = []
    for step in steps_qkv:
        parts_qkv += swap_cores(sizes, plane_end(sizes, plane_start(sizes, eighth(qkv_weight, step))))
    own_qkv = pad_thirds(after(qkv_weight, steps_qkv[0]), feature_count)
    pieces_qkv = [own_qkv, *steps_qkv, *parts_qkv]
    values, adapter_qkv_out = after_all([tokens[0], qkv_adapt_out], steps_qkv[1])
    upstream = after(cotangent[0], steps_qkv[-1])
    adapter_qkv_out = pad_thirds(
        lax.dynamic_index_in_dim(adapter_qkv_out, chosen, 0, keepdims=False), feature_count
    )

    def stacked(own, steps):
        return jnp.stack([eighth(own, step) for step in steps])

    steps_out = direct(sizes, after(own_part(out_weight), steps_qkv[-1]))
    parts_out = plane_start(sizes, stacked(out_weight, steps_out))
    part_down = own_part(down_weight)
    folded = after(part_down.reshape(4, -1, feature_count), *steps_out)
    turn = partial(lax.ppermute, axis_name="wt", perm=ring_pairs(sizes["wt"]))

    by_distance = jnp.stack([flat] + [step[-extra_rows:] for step in steps_qkv])
    order = (lax.axis_index("wt") - jnp.arange(SHARDS)) % SHARDS
    by_shard = jnp.take(by_distance, order, axis=0).reshape(SHARDS, -1).astype(jnp.float32)
    vectors, start = [], 0
    for length in lengths:
        vectors.append(by_shard[:, start : start + length].reshape(1, -1))
        start += length
    gain_one, shift_one, bias_qkv, bias_out, gain_two, shift_two, bias_up, bias_down = vectors
    bias_qkv = pad_thirds(bias_qkv, feature_count)

    first_query = lax.axis_index("ctx") * row_count
    meta = jnp.concatenate([jnp.cumsum(doc_lengths[0])[:3], first_query[None]]).astype(jnp.int32)
    reach = -(-WINDOW // row_count)

    first_in, qkv_low, near = keys_call(
        place, after(values, upstream, *steps_out), gain_one, shift_one, bias_qkv, qkv_adapt_in, adapter_qkv_out, pieces_qkv
    )
    steps_down = [turn(folded)]
    *parts_out[1:], steps_down[0], near = after_all([*parts_out[1:], steps_down[0], near], near)

    far = jnp.concatenate([shifted(near, ctx, offset) for offset in range(reach, 0, -1)], axis=0)
    every_up = lax.all_gather(after(own_part(up_weight), steps_down[0]), "wt", axis=0)
    parts_out = plane_end(sizes, parts_out)
    steps_down.append(turn(steps_down[0]))
    queries = queries_call(
        place, after(first_in, parts_out[1], steps_down[0]), qkv_low, bias_qkv, adapter_qkv_out, pieces_qkv
    )
    *parts_out[3:], steps_down[1] = after_all([*parts_out[3:], steps_down[1]], queries)

    parts_out = swap_cores(sizes, parts_out)
    steps_down.append(turn(steps_down[1]))
    pairs = PAIRS // 2 + 1
    written = attend_forward(meta, after(queries, parts_out[3], steps_down[1]), far, near, 0, pairs)
    steps_down[2], *parts_out[4:] = after_all([steps_down[2], *parts_out[4:]], written[0])

    steps_down = [step.reshape(part_down.shape) for step in steps_down]
    parts_down = plane_start(sizes, stacked(down_weight, steps_down))
    mixed, logsums = attend_forward(
        meta, after(queries, steps_down[2]), far, near, pairs, PAIRS - pairs, written
    )
    *parts_down[1:], every_up = after_all([*parts_down[1:], every_up], mixed)

    parts_down = plane_end(sizes, parts_down)
    steps_up = [lax.dynamic_index_in_dim(every_up, place[k], 0, keepdims=False) for k in range(1, SHARDS)]
    parts_up = plane_start(sizes, stacked(up_weight, steps_up))
    pieces_out = [out_weight, *steps_out, *parts_out]
    hidden, second_in, out_low, up_low = out_call(
        place, values, after(mixed, *parts_down[1:3], every_up), gain_two, shift_two, bias_out, out_adapt_in,
        out_adapt_out, up_adapt_in, pieces_out,
    )
    parts_down[3] = after(parts_down[3], hidden)

    pieces_down = [down_weight, *steps_down, *swap_cores(sizes, parts_down)]
    written = active_grad_call(
        place, after(upstream, hidden), down_adapt_in, down_adapt_out, pieces_down, 0, 2
    )
    parts_up[1:] = after_all(parts_up[1:], written[0])
    parts_up = plane_end(sizes, parts_up)
    grad_active, grad_down_low = active_grad_call(
        place, after(upstream, *parts_up[1:3]), down_adapt_in, down_adapt_out, pieces_down, 2, 5, written
    )
    parts_up[3] = after(parts_up[3], grad_active)
    pieces_up = [up_weight, every_up, *swap_cores(sizes, parts_up)]
    active, grad_second, down_low, grad_up_out, grad_down_in = up_call(
        place, second_in, up_low, grad_active, grad_down_low, bias_up, up_adapt_out, down_adapt_in, pieces_up
    )
    grad_hidden, grad_mixed, grad_up_in, grad_out_out, grad_out_in, grad_down_out = out_grad_call(
        place, grad_second, hidden, second_in, upstream, mixed, out_low, down_low, gain_two,
        up_adapt_in, out_adapt_in, out_adapt_out, pieces_out,
    )
    terms = [grad_up_out, grad_down_in, grad_up_in, grad_out_out, grad_out_in, grad_down_out]
    widths = [(term.shape[1],) for term in terms]
    sent = send_adapters(sizes, terms, chosen)
    everyone = share_adapters(sent)
    near_grads, far_grads = attend_backward(meta, queries, far, near, after(grad_mixed, sent), mixed, logsums)
    everyone = after(everyone, near_grads)
    moved = 0
    for offset in range(reach, 0, -1):
        first_row = (reach - offset) * row_count
        moved += shifted(far_grads[:, first_row : first_row + row_count], ctx, -offset)
    halves = both_halves(sizes, everyone)
    numbers = sequence_numbers(sizes, everyone)
    grad_input, grad_qkv_out, grad_qkv_in = tokens_grad_call(
        place, values, first_in, qkv_low, grad_hidden, gain_one, qkv_adapt_in, adapter_qkv_out,
        after(near_grads, everyone), moved, pieces_qkv,
    )
    last_sent = send_adapters(sizes, [grad_qkv_out, grad_qkv_in], chosen)
    last_everyone = share_adapters(last_sent)
    numbers, active = after_all([numbers, active], last_sent)
    totals = combine_call(numbers, halves, widths)
    total_up_out, total_down_in, total_up_in, total_out_out, total_out_in, total_down_out = totals
    output = down_call(
        place, after(active, *totals), hidden, down_low, bias_down, down_adapt_out, pieces_down
    )
    last_halves = both_halves(sizes, after(last_everyone, output))
    total_qkv_out, total_qkv_in = combine_call(numbers, last_halves, [(feature_count,) * 3, (feature_count,)])
    return (
        output.T[None],
        grad_input.T[None],
        total_qkv_in,
        total_qkv_out,
        total_out_in,
        total_out_out,
        total_up_in,
        total_up_out,
        total_down_in,
        total_down_out,
    )


def solution(mesh):
    return jax.shard_map(
        partial(shards, dict(mesh.shape)),
        mesh=mesh,
        in_specs=(
            P(("dp", "wt"), "ctx", None),
            P(("dp", "wt"), "ctx", None),
            P(("dp", "wt"), None),
            P(("dp", "wt"), None),
            P("wt"),
            P("wt"),
            P("wt", None),
            P("wt"),
            P("wt", None),
            P("wt"),
            P("wt"),
            P("wt"),
            P("wt", None),
            P("wt"),
            P("wt", None),
            P("wt"),
            P(),
            P(),
            P(),
            P(),
            P(),
            P(),
            P(),
            P(),
        ),
        out_specs=(
            P(("dp", "wt"), "ctx", None),
            P(("dp", "wt"), "ctx", None),
            P(),
            P(),
            P(),
            P(),
            P(),
            P(),
            P(),
            P(),
        ),
        check_vma=False,
    )
```

```python
from functools import partial

import jax
import jax.numpy as jnp
from jax import lax
from jax.experimental import pallas as pl
from jax.experimental.pallas import tpu as pltpu
from jax.sharding import PartitionSpec as P

HEADS = 25
HEAD_DIM = 64
ADAPTERS = 8
WINDOW = 1024
RANK = 16
EPSILON = 1e-05
MASKED = -1e30

PAIRS = (HEADS + 1) // 2
PADDED = PAIRS * 128
FACTOR = HEAD_DIM ** (-0.5)
SHARDS = 4
PARTS = 8
BLOCK = 256
FF_CHUNK = 1280
VMEM_LIMIT = 60 << 20

def product(left_side, right_side):
    return lax.dot_general(left_side, right_side, (((1,), (0,)), ((), ())), preferred_element_type=jnp.float32)


def product_transposed(left_side, right_side):
    return lax.dot_general(left_side, right_side, (((1,), (1,)), ((), ())), preferred_element_type=jnp.float32)


def product_outer(left_side, right_side):
    return lax.dot_general(left_side, right_side, (((0,), (0,)), ((), ())), preferred_element_type=jnp.float32)


def norm_forward(values, norm_gain, norm_shift):
    center = values - jnp.mean(values, axis=-1, keepdims=True)
    inverse = lax.rsqrt(jnp.mean(center * center, axis=-1, keepdims=True) + EPSILON)
    normed = center * inverse
    return (normed * norm_gain + norm_shift, normed, inverse)


def norm_backward(upstream, normed, inverse, norm_gain):
    scaled = upstream * norm_gain
    return inverse * (
        scaled
        - jnp.mean(scaled, axis=-1, keepdims=True)
        - normed * jnp.mean(scaled * normed, axis=-1, keepdims=True)
    )


def copy_piece(source, target, row, columns, sem):
    start = pl.multiple_of(row, 16)
    pltpu.make_async_copy(source, target.at[pl.ds(start, source.shape[0]), columns], sem).start()


def start_shard(pieces, place, distance, target, source_columns, columns, sem):
    own, steps = pieces[0], pieces[1:SHARDS]
    together = len(steps[0].shape) == 3
    parts = pieces[2:] if together else pieces[SHARDS:]
    base = place[distance] * own.shape[0]
    if distance == 0:
        copy_piece(own.at[:, source_columns], target, base, columns, sem)
        return
    part_rows = own.shape[0] // (PARTS * 16) * 16
    for source in range(PARTS):
        if len(parts) == PARTS:
            part = parts[source].at[distance - 1, pl.ds(0, part_rows), source_columns]
        else:
            part = parts[(distance - 1) * PARTS + source].at[:, source_columns]
        row = base + place[SHARDS + source] * part_rows
        copy_piece(part, target, row, columns, sem)
    left = own.shape[0] - PARTS * part_rows
    base += PARTS * part_rows
    if left > RANK:
        left //= SHARDS
        for source in range(SHARDS):
            rest = parts[source].at[distance - 1, pl.ds(part_rows, left), source_columns]
            copy_piece(rest, target, base + place[SHARDS + source] // 2 * left, columns, sem)
        return
    step = steps[0].at[place[distance]] if together else steps[distance - 1]
    copy_piece(step.at[pl.ds(part_rows, left), source_columns], target, base, columns, sem)


def start_columns(pieces, place, target, source_columns, columns, sem):
    for distance in range(SHARDS):
        start_shard(pieces, place, distance, target, source_columns, columns, sem)


def wait_rows(target, start, rows, columns, sem):
    whole = target.at[pl.ds(start, rows), columns]
    pltpu.make_async_copy(whole, whole, sem).wait()


def widen(wide, low):
    rows = wide.shape[0]
    fill = jnp.zeros((rows, PADDED - wide.shape[1] - low.shape[1]), jnp.bfloat16)
    return jnp.concatenate([wide, low, fill], axis=1)


def blocks_of(rows):
    return [pl.ds(start, BLOCK) for start in range(0, rows, BLOCK)]


HBM = pl.BlockSpec(memory_space=pl.ANY)


def whole_of(array):
    shape = array.shape
    return pl.BlockSpec(shape, lambda *_: (0,) * len(shape))


def call(kernel, name, grid, place, inputs, pieces, in_specs, outs, out_specs, scratch, macs, aliases={}):
    return pl.pallas_call(
        kernel,
        grid_spec=pltpu.PrefetchScalarGridSpec(
            num_scalar_prefetch=1,
            grid=grid,
            in_specs=in_specs + [HBM] * len(pieces),
            out_specs=out_specs,
            scratch_shapes=scratch,
        ),
        out_shape=outs,
        input_output_aliases=aliases,
        compiler_params=pltpu.CompilerParams(vmem_limit_bytes=VMEM_LIMIT),
        cost_estimate=pl.CostEstimate(flops=2 * macs, bytes_accessed=1 << 22, transcendentals=0),
        name=name,
    )(place, *inputs, *pieces)


def out_of(shape, kind):
    return jax.ShapeDtypeStruct(shape, kind)


def picked(width, column=lambda *grid: 0):
    return pl.BlockSpec((None, RANK, width), lambda c, place: (place[SHARDS + PARTS], 0, column(c)))


def column_block(rows, width):
    return pl.BlockSpec((rows, width), lambda c, *_: (0, c))


def row_block(width):
    return pl.BlockSpec((BLOCK, width), lambda r, *_: (r, 0))


def keys_kernel(place, x_ref, gain, shift, bias, a_in, a_out, *more):
    pieces, (first_ref, low_ref, kv_ref, w, wide, sems) = more[:-6], more[-6:]
    rows, features = x_ref.shape

    @pl.when(pl.program_id(0) == 0)
    def _():
        fetch_columns(pieces, place, w, sems, 0, 1)
        for slot in range(2):
            clear_tail(w.at[slot], features)
        for block in blocks_of(rows):
            normed_in, _, _ = norm_forward(x_ref[block, :].astype(jnp.float32), gain[...], shift[...])
            first = normed_in.astype(jnp.bfloat16)
            low = product_transposed(first, a_in[...]).astype(jnp.bfloat16)
            first_ref[block, :] = first
            low_ref[block, :] = low
            wide[block, :] = widen(first, low)

    slot = next_columns(pieces, place, w, sems, features, 1)
    w[slot, pl.ds(features, RANK), :] = a_out[...]
    for block in blocks_of(rows):
        kv_ref[block, :] = (product(wide[block, :], w[slot]) + bias[...]).astype(jnp.bfloat16)


def fetch_columns(pieces, place, w, sems, c, offset=0):
    width = w.shape[2]
    columns = pl.ds(pl.multiple_of((c + offset) * width, 128), width)
    start_columns(pieces, place, w.at[c % 2], columns, pl.ds(0, width), sems.at[c % 2])


def next_columns(pieces, place, w, sems, features, offset=0):
    step, steps = pl.program_id(0), pl.num_programs(0)

    @pl.when(step + 1 < steps)
    def _():
        fetch_columns(pieces, place, w, sems, step + 1, offset)

    slot = lax.rem(step, 2)
    wait_rows(w.at[slot], 0, features, pl.ds(0, w.shape[2]), sems.at[slot])
    return slot


def clear_tail(w, features):
    count = w.shape[0] - features - RANK
    w[pl.ds(features + RANK, count), :] = jnp.zeros((count, w.shape[1]), jnp.bfloat16)


def keys_call(place, x, gain, shift, bias, a_in, a_out, pieces):
    rows, features = x.shape
    width = PADDED
    third = lambda height: pl.BlockSpec((height, width), lambda c, *_: (0, c + 1))
    return call(
        keys_kernel, "keys", (2,), place, [x, gain, shift, bias, a_in, a_out], pieces,
        [whole_of(x), whole_of(gain), whole_of(shift), third(1), picked(features), third(RANK)],
        [out_of((rows, features), jnp.bfloat16), out_of((rows, RANK), jnp.bfloat16), out_of((rows, 2 * width), jnp.bfloat16)],
        [whole_of(x), pl.BlockSpec((rows, RANK), lambda *_: (0, 0)), column_block(rows, width)],
        [pltpu.VMEM((2, PADDED, width), jnp.bfloat16), pltpu.VMEM((rows, PADDED), jnp.bfloat16), pltpu.SemaphoreType.DMA((2,))],
        rows * features * 2 * width,
    )


def queries_kernel(place, first_ref, low_ref, bias, a_out, *more):
    pieces, (q_ref, w, sems) = more[:-3], more[-3:]
    rows, features = first_ref.shape
    width = w.shape[1]
    halves = [pl.ds(0, width // 256 * 128), pl.ds(width // 256 * 128, width - width // 256 * 128)]
    for half, columns in enumerate(halves):
        start_columns(pieces, place, w, columns, columns, sems.at[half])
    clear_tail(w, features)
    w[pl.ds(features, RANK), :] = a_out[...]
    for half, columns in enumerate(halves):
        wait_rows(w, 0, features, columns, sems.at[half])
        for block in blocks_of(rows):
            wide = widen(first_ref[block, :], low_ref[block, :])
            q_ref[block, columns] = (product(wide, w[:, columns]) + bias[:, columns]).astype(jnp.bfloat16)


def queries_call(place, first, low, bias, a_out, pieces):
    rows, features = first.shape
    width = PADDED
    return call(
        queries_kernel, "queries", (1,), place, [first, low, bias, a_out], pieces,
        [whole_of(first), whole_of(low), column_block(1, width), column_block(RANK, width)],
        out_of((rows, width), jnp.bfloat16),
        column_block(rows, width),
        [pltpu.VMEM((PADDED, width), jnp.bfloat16), pltpu.SemaphoreType.DMA((2,))],
        rows * features * width,
    )


def out_kernel(place, x_ref, mixed_ref, gain, shift, bias, a_in, a_out, u_in, *more):
    pieces, (hidden_ref, second_ref, low_ref, up_low_ref, w, sem) = more[:-6], more[-6:]
    features = x_ref.shape[1]

    @pl.when(pl.program_id(0) == 0)
    def _():
        start_columns(pieces, place, w, pl.ds(0, features), pl.ds(0, features), sem)
        w[pl.ds(features, RANK), :] = a_out[...]
        w[pl.ds(features + RANK, PADDED - features - RANK), :] = jnp.zeros(
            (PADDED - features - RANK, features), jnp.bfloat16
        )
        wait_rows(w, 0, features, pl.ds(0, features), sem)

    mixed = mixed_ref[:, :features]
    low = product_transposed(mixed, a_in[...]).astype(jnp.bfloat16)
    hidden = x_ref[...].astype(jnp.float32) + (product(widen(mixed, low), w[...]) + bias[...])
    normed_mid, _, _ = norm_forward(hidden, gain[...], shift[...])
    second = normed_mid.astype(jnp.bfloat16)
    hidden_ref[...] = hidden
    second_ref[...] = second
    low_ref[...] = low
    up_low_ref[...] = product_transposed(second, u_in[...]).astype(jnp.bfloat16)


def out_call(place, x, mixed, gain, shift, bias, a_in, a_out, u_in, pieces):
    rows, features = x.shape
    return call(
        out_kernel, "out", (rows // BLOCK,), place, [x, mixed, gain, shift, bias, a_in, a_out, u_in], pieces,
        [row_block(features), row_block(PADDED)] + [whole_of(a) for a in (gain, shift, bias)] + [picked(features)] * 3,
        [out_of((rows, features), jnp.float32), out_of((rows, features), jnp.bfloat16), out_of((rows, RANK), jnp.bfloat16), out_of((rows, RANK), jnp.bfloat16)],
        [row_block(features), row_block(features), row_block(RANK), row_block(RANK)],
        [pltpu.VMEM((PADDED, features), jnp.bfloat16), pltpu.SemaphoreType.DMA(())],
        rows * features * features,
    )


def fetch_down(pieces, place, w, sems, first=0, last=None):
    width = w.shape[1]
    shard_rows = w.shape[0] // SHARDS
    last = w.shape[0] // FF_CHUNK if last is None else last
    for shard in range(SHARDS):
        if shard * shard_rows >= last * FF_CHUNK or (shard + 1) * shard_rows <= first * FF_CHUNK:
            continue
        for distance in range(SHARDS):
            @pl.when(place[distance] == shard)
            def _():
                start_shard(pieces, place, distance, w, pl.ds(0, width), pl.ds(0, width), sems.at[shard])


def wait_down(step, w, sems, first=0, last=None):
    shard_rows = w.shape[0] // SHARDS
    last = w.shape[0] // FF_CHUNK if last is None else last
    for shard in range(SHARDS):
        if shard * shard_rows >= last * FF_CHUNK or (shard + 1) * shard_rows <= first * FF_CHUNK:
            continue
        first_step = max(first, -(-(shard * shard_rows - FF_CHUNK + 1) // FF_CHUNK))

        @pl.when(step == first_step)
        def _():
            wait_rows(w, shard * shard_rows, shard_rows, pl.ds(0, w.shape[1]), sems.at[shard])


def active_grad_kernel(first, last, place, cot_ref, a_in, a_out, *more):
    pieces, (g_ref, low_ref, w, sems) = more[:-4], more[-4:]
    pieces = pieces[: len(pieces) - (2 if first else 0)]
    rows, features = cot_ref.shape
    step = pl.program_id(0) + first

    @pl.when(step == first)
    def _():
        fetch_down(pieces, place, w, sems, first, last)
        for block in blocks_of(rows):
            low_ref[block, :] = product_transposed(cot_ref[block, :], a_out[...]).astype(jnp.bfloat16)

    wait_down(step, w, sems, first, last)
    weight = w[pl.ds(pl.multiple_of(step * FF_CHUNK, FF_CHUNK), FF_CHUNK), :]
    for block in blocks_of(rows):
        g_ref[block, :] = (
            product_transposed(cot_ref[block, :], weight) + product(low_ref[block, :], a_in[...])
        ).astype(jnp.bfloat16)


def active_grad_call(place, cot, a_in, a_out, pieces, first, last, written=()):
    rows, features = cot.shape
    units = a_in.shape[2]
    chunk = lambda height: pl.BlockSpec((height, FF_CHUNK), lambda c, *_: (0, c + first))
    return call(
        partial(active_grad_kernel, first, last), "active_grad", (last - first,), place, [cot, a_in, a_out],
        [*pieces, *written],
        [whole_of(cot), picked(FF_CHUNK, lambda c: c + first), picked(features)],
        [out_of((rows, units), jnp.bfloat16), out_of((rows, RANK), jnp.bfloat16)],
        [chunk(rows), pl.BlockSpec((rows, RANK), lambda *_: (0, 0))],
        [pltpu.VMEM((units, features), jnp.bfloat16), pltpu.SemaphoreType.DMA((SHARDS,))],
        rows * features * FF_CHUNK * (last - first) if first else RANK,
        {4 + len(pieces) + place: place for place in range(len(written))},
    )


GELU_A = 0.7978845608
GELU_B = 0.044715


def up_kernel(place, second_ref, up_low_ref, g_active_ref, g_low_ref, bias, u_out, d_in, *more):
    pieces, (active_ref, acc_ref, down_low_ref, g_up_out_ref, g_down_in_ref, w, wide, low_scr, g_scr, sems) = more[:-10], more[-10:]
    rows, features = second_ref.shape
    step, steps = pl.program_id(0), pl.num_programs(0)
    width = w.shape[2]

    def fetch(c):
        columns = pl.ds(pl.multiple_of(c * width, 128), width)
        start_columns(pieces, place, w.at[c % 2], columns, pl.ds(0, width), sems.at[c % 2])

    @pl.when(step == 0)
    def _():
        fetch(0)
        for slot in range(2):
            w[slot, pl.ds(features + RANK, PADDED - features - RANK), :] = jnp.zeros(
                (PADDED - features - RANK, width), jnp.bfloat16
            )
        acc_ref[...] = jnp.zeros_like(acc_ref)
        low_scr[...] = jnp.zeros_like(low_scr)
        for block in blocks_of(rows):
            wide[block, :] = widen(second_ref[block, :], up_low_ref[block, :])

    @pl.when(step + 1 < steps)
    def _():
        fetch(step + 1)

    slot = lax.rem(step, 2)
    wait_rows(w.at[slot], 0, features, pl.ds(0, width), sems.at[slot])
    w[slot, pl.ds(features, RANK), :] = u_out[...]
    blocks = blocks_of(rows)
    ahead = product(wide[blocks[0], :], w[slot])
    for number, block in enumerate(blocks):
        upper = ahead + bias[...]
        if number + 1 < len(blocks):
            ahead = product(wide[blocks[number + 1], :], w[slot])
        square = upper * upper
        inner = jnp.tanh(upper * (GELU_A + (GELU_A * GELU_B) * square))
        half = 0.5 + 0.5 * inner
        active = (upper * half).astype(jnp.bfloat16)
        slope = half + upper * (1.0 - inner * inner) * (0.5 * GELU_A + (1.5 * GELU_A * GELU_B) * square)
        g_upper = (g_active_ref[block, :].astype(jnp.float32) * slope).astype(jnp.bfloat16)
        active_ref[block, :] = active
        g_scr[block, :] = g_upper
        acc_ref[block, :] += product_transposed(g_upper, w[slot])
        low_scr[block, :] += product_transposed(active, d_in[...])
    g_up_out_ref[...] = product_outer(up_low_ref[...], g_scr[...])
    g_down_in_ref[...] = product_outer(g_low_ref[...], active_ref[...])

    @pl.when(step == steps - 1)
    def _():
        down_low_ref[...] = low_scr[...].astype(jnp.bfloat16)


def up_call(place, second, up_low, g_active, g_low, bias, u_out, d_in, pieces):
    rows, features = second.shape
    units = bias.shape[1]
    low_block = pl.BlockSpec((rows, RANK), lambda *_: (0, 0))
    return call(
        up_kernel, "up", (units // FF_CHUNK,), place, [second, up_low, g_active, g_low, bias, u_out, d_in], pieces,
        [whole_of(second), low_block, column_block(rows, FF_CHUNK), low_block,
         column_block(1, FF_CHUNK), picked(FF_CHUNK, lambda c: c), picked(FF_CHUNK, lambda c: c)],
        [out_of((rows, units), jnp.bfloat16), out_of((rows, PADDED), jnp.float32), out_of((rows, RANK), jnp.bfloat16),
         out_of((RANK, units), jnp.float32), out_of((RANK, units), jnp.float32)],
        [column_block(rows, FF_CHUNK), pl.BlockSpec((rows, PADDED), lambda *_: (0, 0)), low_block,
         column_block(RANK, FF_CHUNK), column_block(RANK, FF_CHUNK)],
        [pltpu.VMEM((2, PADDED, FF_CHUNK), jnp.bfloat16), pltpu.VMEM((rows, PADDED), jnp.bfloat16), pltpu.VMEM((rows, RANK), jnp.float32),
         pltpu.VMEM((rows, FF_CHUNK), jnp.bfloat16), pltpu.SemaphoreType.DMA((2,))],
        2 * rows * features * units,
    )


def out_grad_kernel(place, acc_ref, hidden_ref, second_ref, cot_ref, mixed_ref, low_ref, down_low_ref, gain, u_in, a_in, a_out, *more):
    pieces, (g_hidden_ref, g_mixed_ref, g_up_in, g_out_out, g_out_in, g_down_out, w, sem) = more[:-8], more[-8:]
    features = hidden_ref.shape[1]
    step = pl.program_id(0)

    @pl.when(step == 0)
    def _():
        start_columns(pieces, place, w, pl.ds(0, features), pl.ds(0, features), sem)
        w[pl.ds(features, RANK), :] = a_out[...]
        w[pl.ds(features + RANK, PADDED - features - RANK), :] = jnp.zeros(
            (PADDED - features - RANK, features), jnp.bfloat16
        )

    g_up_low = acc_ref[:, features : features + RANK].astype(jnp.bfloat16)
    g_second = acc_ref[:, :features] + product(g_up_low, u_in[...])
    _, normed, inverse = norm_forward(hidden_ref[...], gain[...], 0.0)
    cot = cot_ref[...]
    g_hidden = cot.astype(jnp.float32) + norm_backward(g_second, normed, inverse, gain[...])
    g_branch = g_hidden.astype(jnp.bfloat16)
    g_hidden_ref[...] = g_hidden

    @pl.when(step == 0)
    def _():
        wait_rows(w, 0, features, pl.ds(0, features), sem)

    back = product_transposed(g_branch, w[...])
    g_low = back[:, features : features + RANK].astype(jnp.bfloat16)
    g_mixed = back[:, :features] + product(g_low, a_in[...])
    g_mixed_ref[:, :features] = g_mixed.astype(jnp.bfloat16)
    g_mixed_ref[:, features:] = jnp.zeros((BLOCK, PADDED - features), jnp.bfloat16)
    sums = (
        product_outer(g_up_low, second_ref[...]),
        product_outer(low_ref[...], g_branch),
        product_outer(g_low, mixed_ref[:, :features]),
        product_outer(down_low_ref[...], cot),
    )
    for total, term in zip((g_up_in, g_out_out, g_out_in, g_down_out), sums):
        @pl.when(step == 0)
        def _():
            total[...] = term

        @pl.when(step > 0)
        def _():
            total[...] += term


def out_grad_call(place, acc, hidden, second, cot, mixed, low, down_low, gain, u_in, a_in, a_out, pieces):
    rows, features = hidden.shape
    small = pl.BlockSpec((RANK, features), lambda *_: (0, 0))
    return call(
        out_grad_kernel, "out_grad", (rows // BLOCK,), place,
        [acc, hidden, second, cot, mixed, low, down_low, gain, u_in, a_in, a_out], pieces,
        [row_block(PADDED), row_block(features), row_block(features), row_block(features), row_block(PADDED),
         row_block(RANK), row_block(RANK), whole_of(gain)] + [picked(features)] * 3,
        [out_of((rows, features), jnp.float32), out_of((rows, PADDED), jnp.bfloat16)] + [out_of((RANK, features), jnp.float32)] * 4,
        [row_block(features), row_block(PADDED)] + [small] * 4,
        [pltpu.VMEM((PADDED, features), jnp.bfloat16), pltpu.SemaphoreType.DMA(())],
        rows * features * features,
    )


def down_kernel(place, active_ref, hidden_ref, down_low_ref, bias, a_out, *more):
    pieces, (out_ref, w, acc, hidden, sems, late) = more[:-6], more[-6:]
    rows, features = hidden_ref.shape
    step, steps = pl.program_id(0), pl.num_programs(0)
    copy = pltpu.make_async_copy(hidden_ref, hidden, late)

    @pl.when(step == 0)
    def _():
        fetch_down(pieces, place, w, sems)
        copy.start()
        for block in blocks_of(rows):
            acc[block, :] = product(down_low_ref[block, :], a_out[...]) + bias[...]

    wait_down(step, w, sems)
    weight = w[pl.ds(pl.multiple_of(step * FF_CHUNK, FF_CHUNK), FF_CHUNK), :]
    for block in blocks_of(rows):
        acc[block, :] += product(active_ref[block, :], weight)

    @pl.when(step == steps - 1)
    def _():
        copy.wait()
        for block in blocks_of(rows):
            out_ref[:, block] = (hidden[block, :] + acc[block, :]).astype(jnp.bfloat16).T


def down_call(place, active, hidden, down_low, bias, a_out, pieces):
    rows, features = hidden.shape
    units = active.shape[1]
    return call(
        down_kernel, "down", (units // FF_CHUNK,), place, [active, hidden, down_low, bias, a_out], pieces,
        [column_block(rows, FF_CHUNK), HBM, pl.BlockSpec((rows, RANK), lambda *_: (0, 0)),
         whole_of(bias), picked(features)],
        out_of((features, rows), jnp.bfloat16),
        pl.BlockSpec((features, rows), lambda *_: (0, 0)),
        [pltpu.VMEM((units, features), jnp.bfloat16), pltpu.VMEM((rows, features), jnp.float32), pltpu.VMEM((rows, features), jnp.float32),
         pltpu.SemaphoreType.DMA((SHARDS,)), pltpu.SemaphoreType.DMA(())],
        rows * features * units,
    )


def tokens_grad_kernel(place, x_ref, first_ref, low_ref, g_hidden_ref, gain, a_in, a_out, near_ref, far_ref, *more):
    pieces, (out_ref, g_qkv_out, g_qkv_in, w, acc, x, first, g_hidden, sems, late) = more[:-10], more[-10:]
    rows, features = x_ref.shape
    step, steps = pl.program_id(0), pl.num_programs(0)
    pairs = ((x_ref, x), (first_ref, first), (g_hidden_ref, g_hidden))
    copies = [pltpu.make_async_copy(*pair, late.at[number]) for number, pair in enumerate(pairs)]

    @pl.when(step == 0)
    def _():
        fetch_columns(pieces, place, w, sems, 0)
        for slot in range(2):
            clear_tail(w.at[slot], features)
        acc[...] = jnp.zeros_like(acc)

    @pl.when(step == 1)
    def _():
        for copy in copies:
            copy.start()

    slot = next_columns(pieces, place, w, sems, features)
    w[slot, pl.ds(features, RANK), :] = a_out[...]
    scale = jnp.where(step > 0, 1.0, 0.0)
    qkv_out_sum = jnp.zeros(g_qkv_out.shape, jnp.float32)
    for block in blocks_of(rows):
        g = (near_ref[block, :].astype(jnp.float32) + scale * far_ref[block, :].astype(jnp.float32)).astype(jnp.bfloat16)
        acc[block, :] += product_transposed(g, w[slot])
        qkv_out_sum += product_outer(low_ref[block, :], g)
    g_qkv_out[...] = qkv_out_sum

    @pl.when(step == steps - 1)
    def _():
        for copy in copies:
            copy.wait()
        qkv_in_sum = jnp.zeros((RANK, features), jnp.float32)
        for block in blocks_of(rows):
            g_low = acc[block, pl.ds(features, RANK)].astype(jnp.bfloat16)
            g_first = acc[block, pl.ds(0, features)] + product(g_low, a_in[...])
            _, normed, inverse = norm_forward(x[block, :].astype(jnp.float32), gain[...], 0.0)
            out_ref[:, block] = (g_hidden[block, :] + norm_backward(g_first, normed, inverse, gain[...])).T
            qkv_in_sum += product_outer(g_low, first[block, :])
        g_qkv_in[...] = qkv_in_sum


def tokens_grad_call(place, x, first, low, g_hidden, gain, a_in, a_out, near, far, pieces):
    rows, features = x.shape
    steps = 3
    near_block = pl.BlockSpec((None, rows, PADDED), lambda c, *_: (c, 0, 0))
    far_block = pl.BlockSpec((None, rows, PADDED), lambda c, *_: (jnp.maximum(c - 1, 0), 0, 0))
    return call(
        tokens_grad_kernel, "tokens_grad", (steps,), place, [x, first, low, g_hidden, gain, a_in, a_out, near, far], pieces,
        [HBM, HBM, whole_of(low), HBM, whole_of(gain), picked(features),
         column_block(RANK, PADDED), near_block, far_block],
        [out_of((features, rows), jnp.float32), out_of((RANK, steps * PADDED), jnp.float32), out_of((RANK, features), jnp.float32)],
        [pl.BlockSpec((features, rows), lambda *_: (0, 0)), column_block(RANK, PADDED),
         pl.BlockSpec((RANK, features), lambda *_: (0, 0))],
        [pltpu.VMEM((2, PADDED, PADDED), jnp.bfloat16), pltpu.VMEM((rows, PADDED), jnp.float32),
         pltpu.VMEM((rows, features), jnp.bfloat16), pltpu.VMEM((rows, features), jnp.bfloat16), pltpu.VMEM((rows, features), jnp.float32),
         pltpu.SemaphoreType.DMA((2,)), pltpu.SemaphoreType.DMA((3,))],
        rows * features * steps * PADDED,
    )


def combine_kernel(widths, numbers, *refs):
    parts, totals = refs[: -len(widths)], refs[-len(widths) :]
    sequences, _, part_width = parts[0].shape
    half_width = part_width - 128

    def add(halves):
        start = 0
        for total, spans in zip(totals, widths):
            into = 0
            for width in spans:
                done = 0
                while done < width:
                    half, at = divmod(start + done, half_width)
                    size = min(width - done, half_width - at)
                    for sequence in range(sequences):
                        target = (numbers[sequence], slice(None), pl.ds(into + done, size))
                        total[target] += halves[half][sequence, :, pl.ds(at, size)].astype(jnp.float32)
                    done += size
                into += width
                start += -(-width // 128) * 128

    for total in totals:
        total[...] = jnp.zeros_like(total)
    turned = numbers[sequences]

    @pl.when(turned == 0)
    def _():
        add(parts)

    if len(parts) == 2:
        @pl.when(turned == 1)
        def _():
            add(parts[::-1])


def combine_call(numbers, parts, widths):
    shapes = [(ADAPTERS, RANK, sum(spans)) for spans in widths]
    return pl.pallas_call(
        partial(combine_kernel, widths),
        grid_spec=pltpu.PrefetchScalarGridSpec(
            num_scalar_prefetch=1,
            grid=(1,),
            in_specs=[whole_of(part) for part in parts],
            out_specs=[pl.BlockSpec(shape, lambda *_: (0, 0, 0)) for shape in shapes],
        ),
        out_shape=[out_of(shape, jnp.float32) for shape in shapes],
        compiler_params=pltpu.CompilerParams(vmem_limit_bytes=VMEM_LIMIT),
        cost_estimate=pl.CostEstimate(flops=1 << 30, bytes_accessed=1 << 22, transcendentals=0),
        name="combine",
    )(numbers, *parts)


TILE = 256
REACH_TILES = WINDOW // TILE
SPAN_TILES = REACH_TILES + 1


def split_pair(pair):
    lane = lax.broadcasted_iota(jnp.int32, pair.shape, 1)
    zero = jnp.zeros_like(pair)
    return jnp.concatenate(
        [jnp.where(lane < HEAD_DIM, pair, zero), jnp.where(lane >= HEAD_DIM, pair, zero)], axis=0
    )


def join_pair(stacked):
    lane = lax.broadcasted_iota(jnp.int32, (TILE, 128), 1)
    return jnp.where(lane < HEAD_DIM, stacked[:TILE], stacked[TILE:])


def tile_bias(bounds, query_start, key_start):
    rows = query_start + lax.broadcasted_iota(jnp.int32, (TILE, 1), 0)
    columns = key_start + lax.broadcasted_iota(jnp.int32, (1, TILE), 1)
    row_doc = sum((rows >= bound).astype(jnp.int32) for bound in bounds)
    column_doc = sum((columns >= bound).astype(jnp.int32) for bound in bounds)
    shape = (TILE, TILE)
    distance = jnp.broadcast_to(rows, shape) - jnp.broadcast_to(columns, shape)
    same = jnp.broadcast_to(row_doc, shape) == jnp.broadcast_to(column_doc, shape)
    seen = jnp.broadcast_to(columns, shape) >= 0
    return jnp.where(same & seen & (distance >= 0) & (distance < WINDOW), 0.0, MASKED)


def fill_biases(meta, bias_scr, tiles):
    bounds = [meta[place] for place in range(3)]
    first = meta[3]

    def one(step, carry):
        tile = step // SPAN_TILES
        key_tile = tile + lax.rem(step, SPAN_TILES) - REACH_TILES
        bias_scr[step] = tile_bias(bounds, first + tile * TILE, first + key_tile * TILE)
        return carry

    lax.fori_loop(0, tiles * SPAN_TILES, one, 0)


def key_tile(far_ref, near_ref, tile):
    if tile < REACH_TILES:
        return far_ref[pl.ds(tile * TILE, TILE), :]
    return near_ref[pl.ds((tile - REACH_TILES) * TILE, TILE), :]


def attend_forward_kernel(tiles, meta, q_ref, k_far, v_far, k_near, v_near, *more):
    o_ref, lse_ref, bias_scr, acc_scr = more[-4:]

    @pl.when(pl.program_id(0) == 0)
    def _():
        fill_biases(meta, bias_scr, tiles)

    ones = jnp.ones((TILE, 128), jnp.bfloat16)
    chunk = TILE // 2
    for tile in range(tiles):
        stacked = split_pair(q_ref[pl.ds(tile * TILE, TILE), :] * FACTOR)
        span = range(tile, tile + SPAN_TILES)
        keys = jnp.concatenate([key_tile(k_far, k_near, t) for t in span], axis=0)
        values = jnp.concatenate(
            [jnp.concatenate([key_tile(v_far, v_near, t), ones], axis=1) for t in span], axis=0
        )
        for part in range(2 * TILE // chunk):
            start = part * chunk
            bias_rows = pl.ds(start % TILE, chunk)
            bias = jnp.concatenate(
                [bias_scr[tile * SPAN_TILES + t, bias_rows, :] for t in range(SPAN_TILES)], axis=1
            )
            scores = product_transposed(stacked[start : start + chunk], keys) + bias
            highest = jnp.max(scores, axis=1, keepdims=True)
            mixed = product(jnp.exp(scores - highest).astype(jnp.bfloat16), values)
            summed = mixed[:, 128:]
            acc_scr[pl.ds(start, chunk), :] = mixed[:, :128] / summed
            lse_ref[pl.ds(tile * 2 * TILE + start, chunk), :] = highest + jnp.log(summed)
        o_ref[pl.ds(tile * TILE, TILE), :] = join_pair(acc_scr[...]).astype(jnp.bfloat16)


def pair_columns(rows, offset=0):
    return pl.BlockSpec((rows, 128), lambda j, *_: (0, offset + j))


def attention_cost(products, pairs, rows):
    macs = products * pairs * 2 * rows * SPAN_TILES * TILE * 256
    return pl.CostEstimate(flops=2 * macs, bytes_accessed=1 << 24, transcendentals=0)


def attend_forward(meta, queries, far, near, start, pairs, written=()):
    rows = queries.shape[0]
    tiles = rows // TILE
    return pl.pallas_call(
        partial(attend_forward_kernel, tiles),
        grid_spec=pltpu.PrefetchScalarGridSpec(
            num_scalar_prefetch=1,
            grid=(pairs,),
            in_specs=[
                pair_columns(rows, start), pair_columns(WINDOW, start), pair_columns(WINDOW, PAIRS + start),
                pair_columns(rows, start), pair_columns(rows, PAIRS + start),
            ] + [pl.BlockSpec(memory_space=pl.ANY)] * len(written),
            out_specs=[
                pair_columns(rows, start),
                pl.BlockSpec((None, 2 * rows, 128), lambda j, *_: (start + j, 0, 0)),
            ],
            scratch_shapes=[
                pltpu.VMEM((tiles * SPAN_TILES, TILE, TILE), jnp.float32),
                pltpu.VMEM((2 * TILE, 128), jnp.float32),
            ],
        ),
        out_shape=[
            jax.ShapeDtypeStruct((rows, PADDED), jnp.bfloat16),
            jax.ShapeDtypeStruct((PAIRS, 2 * rows, 128), jnp.float32),
        ],
        input_output_aliases={6 + place: place for place in range(len(written))},
        compiler_params=pltpu.CompilerParams(vmem_limit_bytes=VMEM_LIMIT),
        cost_estimate=attention_cost(2, pairs, rows),
        name="attend_forward",
    )(meta, queries, far, far, near, near, *written)


def attend_backward_kernel(
    tiles, meta, q_ref, k_far, v_far, k_near, v_near, g_ref, o_ref, lse_ref,
    near_ref, far_ref, bias_scr, dq_scr, dkt, dvt,
):
    @pl.when(pl.program_id(0) == 0)
    def _():
        fill_biases(meta, bias_scr, tiles)

    dkt[...] = jnp.zeros_like(dkt)
    dvt[...] = jnp.zeros_like(dvt)
    for tile in range(tiles):
        rows = pl.ds(tile * TILE, TILE)
        queries = split_pair(q_ref[rows, :] * FACTOR)
        grads = split_pair(g_ref[rows, :])
        mixed = o_ref[rows, :].astype(jnp.float32)
        centered = jnp.sum(
            grads.astype(jnp.float32) * jnp.concatenate([mixed, mixed], axis=0), axis=1, keepdims=True
        )
        lse = lse_ref[pl.ds(tile * 2 * TILE, 2 * TILE), :]
        lse = jnp.concatenate([lse, lse], axis=1)
        queries_t = queries.T
        grads_t = grads.T
        dq_scr[...] = jnp.zeros_like(dq_scr)
        for t in range(SPAN_TILES):
            keys = key_tile(k_far, k_near, tile + t)
            bias = bias_scr[tile * SPAN_TILES + t]
            scores = product_transposed(queries, keys)
            chances = jnp.exp(scores + jnp.concatenate([bias, bias], axis=0) - lse)
            grad_chances = product_transposed(grads, key_tile(v_far, v_near, tile + t))
            grad_scores = (chances * (grad_chances - centered)).astype(jnp.bfloat16)
            dvt[tile + t] += product(grads_t, chances.astype(jnp.bfloat16))
            dkt[tile + t] += product(queries_t, grad_scores)
            dq_scr[...] += product(grad_scores, keys)
        near_ref[0, rows, :] = (join_pair(dq_scr[...]) * FACTOR).astype(jnp.bfloat16)
    for t in range(tiles + REACH_TILES):
        target, first = (far_ref, 0) if t < REACH_TILES else (near_ref, 1)
        rows = pl.ds((t if t < REACH_TILES else t - REACH_TILES) * TILE, TILE)
        target[first, rows, :] = dkt[t].T.astype(jnp.bfloat16)
        target[first + 1, rows, :] = dvt[t].T.astype(jnp.bfloat16)


def attend_backward(meta, queries, far, near, grad_mixed, mixed, lse):
    rows = queries.shape[0]
    tiles = rows // TILE
    return pl.pallas_call(
        partial(attend_backward_kernel, tiles),
        grid_spec=pltpu.PrefetchScalarGridSpec(
            num_scalar_prefetch=1,
            grid=(PAIRS,),
            in_specs=[
                pair_columns(rows), pair_columns(WINDOW), pair_columns(WINDOW, PAIRS),
                pair_columns(rows), pair_columns(rows, PAIRS), pair_columns(rows), pair_columns(rows),
                pl.BlockSpec((None, 2 * rows, 128), lambda j, *_: (j, 0, 0)),
            ],
            out_specs=[
                pl.BlockSpec((3, rows, 128), lambda j, *_: (0, 0, j)),
                pl.BlockSpec((2, WINDOW, 128), lambda j, *_: (0, 0, j)),
            ],
            scratch_shapes=[
                pltpu.VMEM((tiles * SPAN_TILES, TILE, TILE), jnp.float32),
                pltpu.VMEM((2 * TILE, 128), jnp.float32),
                pltpu.VMEM((tiles + REACH_TILES, 128, TILE), jnp.float32),
                pltpu.VMEM((tiles + REACH_TILES, 128, TILE), jnp.float32),
            ],
        ),
        out_shape=[
            jax.ShapeDtypeStruct((3, rows, PADDED), jnp.bfloat16),
            jax.ShapeDtypeStruct((2, WINDOW, PADDED), jnp.bfloat16),
        ],
        compiler_params=pltpu.CompilerParams(vmem_limit_bytes=VMEM_LIMIT),
        cost_estimate=attention_cost(5, PAIRS, rows),
        name="attend_backward",
    )(meta, queries, far, far, near, near, grad_mixed, mixed, lse)


def ring_pairs(size):
    return [(i, (i + 1) % size) for i in range(size)]


def plane_pairs(sizes):
    first, second = [], []
    cores = sizes["ctx"]
    for chip in range(sizes["dp"]):
        for core in range(cores):
            steps = (chip ^ 1, chip ^ 2) if core % 2 == 0 else (chip ^ 2, chip ^ 1)
            here = chip * cores + core
            first.append((here, steps[0] * cores + core))
            second.append((here, steps[1] * cores + core))
    return first, second


def swap_pairs(size):
    return [(i, i ^ 1) for i in range(size)]


def shifted(array, size, by):
    pairs = [(i, i + by) for i in range(size) if 0 <= i + by < size]
    return lax.ppermute(array, "ctx", pairs)


def place_of(chosen):
    chip, core, shard = lax.axis_index("dp"), lax.axis_index("ctx") % 2, lax.axis_index("wt")
    places = [(shard - distance) % SHARDS for distance in range(SHARDS)]
    for side in (core, 1 - core):
        near = jnp.where(side == 0, chip ^ 1, chip ^ 2)
        for where in (chip, near, near ^ 3, chip ^ 3):
            places.append(where * 2 + side)
    return jnp.stack([*places, chosen]).astype(jnp.int32)


def after(array, *others):
    return lax.optimization_barrier((array, *others))[0]


def after_all(arrays, *others):
    return lax.optimization_barrier((*arrays, *others))[: len(arrays)]


def own_part(own):
    rows = own.shape[0] // (PARTS * 16) * 16
    chip, core = lax.axis_index("dp"), lax.axis_index("ctx") % 2
    left = own.shape[0] - PARTS * rows
    first = PARTS * rows
    if left > RANK:
        left //= SHARDS
        first += chip * left
    mine = lax.dynamic_slice_in_dim(own, (chip * 2 + core) * rows, rows, 0)
    return jnp.concatenate([mine, lax.dynamic_slice_in_dim(own, first, left, 0)], axis=0)


def eighth(own, moved):
    rows = own.shape[0] // (PARTS * 16) * 16
    return moved if own.shape[0] - PARTS * rows > RANK else moved[:rows]


def ring(sizes, moved):
    steps = []
    for _ in range(SHARDS - 1):
        moved = lax.ppermute(moved, "wt", ring_pairs(sizes["wt"]))
        steps.append(moved)
    return steps


def direct(sizes, moved):
    size = sizes["wt"]
    return [
        lax.ppermute(moved, "wt", [(i, (i + distance) % size) for i in range(size)])
        for distance in range(1, SHARDS)
    ]


def plane_start(sizes, mine):
    first, second = plane_pairs(sizes)
    return [mine, lax.ppermute(mine, ("dp", "ctx"), first), lax.ppermute(mine, ("dp", "ctx"), second)]


def plane_end(sizes, parts):
    _, second = plane_pairs(sizes)
    return [*parts, lax.ppermute(parts[1], ("dp", "ctx"), second)]


def swap_cores(sizes, parts):
    swap = swap_pairs(sizes["ctx"])
    return [*parts, *[lax.ppermute(part, "ctx", swap) for part in parts]]


def pad_thirds(array, features):
    pieces = []
    for third in range(3):
        piece = array[..., third * features : (third + 1) * features]
        pieces.append(jnp.pad(piece, [(0, 0)] * (array.ndim - 1) + [(0, PADDED - features)]))
    return jnp.concatenate(pieces, axis=-1)


def send_adapters(sizes, terms, chosen):
    flat = jnp.concatenate(
        [jnp.pad(term, ((0, 0), (0, -term.shape[1] % 128))) for term in terms], axis=1
    )
    paired = sizes["ctx"] == 2
    if paired:
        half = flat.shape[1] // 2
        core = lax.axis_index("ctx")
        kept = lax.dynamic_slice_in_dim(flat, core * half, half, 1)
        given = lax.dynamic_slice_in_dim(flat, (1 - core) * half, half, 1)
        flat = kept + lax.ppermute(given, "ctx", swap_pairs(2))
    else:
        flat = lax.psum(flat, "ctx")
    ids = jnp.broadcast_to(chosen.astype(jnp.bfloat16), (RANK, 128))
    return jnp.concatenate([flat.astype(jnp.bfloat16), ids], axis=1)


def share_adapters(sent):
    return lax.all_gather(sent, ("dp", "wt"), axis=0)


def sequence_numbers(sizes, everyone):
    numbers = everyone[:, 0, -1].astype(jnp.int32)
    turned = lax.axis_index("ctx") if sizes["ctx"] == 2 else 0
    return jnp.concatenate([numbers, jnp.full((1,), turned, jnp.int32)])


def both_halves(sizes, everyone):
    if sizes["ctx"] != 2:
        return [everyone]
    return [everyone, lax.ppermute(everyone, "ctx", swap_pairs(2))]


def shards(
    sizes,
    tokens,
    cotangent,
    doc_lengths,
    adapter_ids,
    first_gain,
    first_shift,
    qkv_weight,
    qkv_bias,
    out_weight,
    out_bias,
    second_gain,
    second_shift,
    up_weight,
    up_bias,
    down_weight,
    down_bias,
    qkv_adapt_in,
    qkv_adapt_out,
    out_adapt_in,
    out_adapt_out,
    up_adapt_in,
    up_adapt_out,
    down_adapt_in,
    down_adapt_out,
):
    row_count, feature_count = tokens.shape[1:]
    ctx = sizes["ctx"]
    chosen = adapter_ids[0, 0]
    place = place_of(chosen)

    vectors = [first_gain, first_shift, qkv_bias, out_bias, second_gain, second_shift, up_bias, down_bias]
    lengths = [vector.shape[0] for vector in vectors]
    flat = jnp.concatenate(vectors)
    extra_rows = -(-flat.shape[0] // (3 * PADDED))
    flat = jnp.pad(flat, (0, extra_rows * 3 * PADDED - flat.shape[0])).reshape(extra_rows, -1)

    part_qkv = jnp.concatenate([pad_thirds(own_part(qkv_weight), feature_count), flat], axis=0)
    steps_qkv = ring(sizes, part_qkv)
    parts_qkv, before = [], []
    for step in steps_qkv:
        parts = plane_start(sizes, after(eighth(qkv_weight, step), *before))
        before = parts[1:]
        parts_qkv += swap_cores(sizes, plane_end(sizes, parts))
    own_qkv = pad_thirds(after(qkv_weight, steps_qkv[0]), feature_count)
    pieces_qkv = [own_qkv, *steps_qkv, *parts_qkv]
    values, adapter_qkv_out = after_all([tokens[0], qkv_adapt_out], steps_qkv[1])
    upstream = after(cotangent[0], steps_qkv[-1])
    adapter_qkv_out = pad_thirds(
        lax.dynamic_index_in_dim(adapter_qkv_out, chosen, 0, keepdims=False), feature_count
    )

    def stacked(own, steps):
        return jnp.stack([eighth(own, step) for step in steps])

    steps_out = direct(sizes, after(own_part(out_weight), steps_qkv[-1]))
    parts_out = plane_start(sizes, stacked(out_weight, steps_out))
    part_down = own_part(down_weight)
    folded = after(part_down.reshape(4, -1, feature_count), *steps_out)
    turn = partial(lax.ppermute, axis_name="wt", perm=ring_pairs(sizes["wt"]))

    by_distance = jnp.stack([flat] + [step[-extra_rows:] for step in steps_qkv])
    order = (lax.axis_index("wt") - jnp.arange(SHARDS)) % SHARDS
    by_shard = jnp.take(by_distance, order, axis=0).reshape(SHARDS, -1).astype(jnp.float32)
    vectors, start = [], 0
    for length in lengths:
        vectors.append(by_shard[:, start : start + length].reshape(1, -1))
        start += length
    gain_one, shift_one, bias_qkv, bias_out, gain_two, shift_two, bias_up, bias_down = vectors
    bias_qkv = pad_thirds(bias_qkv, feature_count)

    first_query = lax.axis_index("ctx") * row_count
    meta = jnp.concatenate([jnp.cumsum(doc_lengths[0])[:3], first_query[None]]).astype(jnp.int32)
    reach = -(-WINDOW // row_count)

    first_in, qkv_low, near = keys_call(
        place, after(values, upstream, *steps_out), gain_one, shift_one, bias_qkv, qkv_adapt_in, adapter_qkv_out, pieces_qkv
    )
    steps_down = [turn(folded)]
    *parts_out[1:], steps_down[0], near = after_all([*parts_out[1:], steps_down[0], near], near)

    far = jnp.concatenate([shifted(near, ctx, offset) for offset in range(reach, 0, -1)], axis=0)
    every_up = lax.all_gather(after(own_part(up_weight), steps_down[0]), "wt", axis=0)
    parts_out = plane_end(sizes, parts_out)
    steps_down.append(turn(steps_down[0]))
    queries = queries_call(
        place, after(first_in, parts_out[1], steps_down[0]), qkv_low, bias_qkv, adapter_qkv_out, pieces_qkv
    )
    *parts_out[3:], steps_down[1] = after_all([*parts_out[3:], steps_down[1]], queries)

    parts_out = swap_cores(sizes, parts_out)
    steps_down.append(turn(steps_down[1]))
    pairs = PAIRS * 2 // 5
    written = attend_forward(meta, after(queries, parts_out[3], steps_down[1]), far, near, 0, pairs)
    steps_down[2], *parts_out[4:] = after_all([steps_down[2], *parts_out[4:]], written[0])

    steps_down = [step.reshape(part_down.shape) for step in steps_down]
    parts_down = plane_start(sizes, stacked(down_weight, steps_down))
    mixed, logsums = attend_forward(
        meta, after(queries, steps_down[2]), far, near, pairs, PAIRS - pairs, written
    )
    *parts_down[1:], every_up = after_all([*parts_down[1:], every_up], mixed)

    parts_down = plane_end(sizes, parts_down)
    steps_up = [lax.dynamic_index_in_dim(every_up, place[k], 0, keepdims=False) for k in range(1, SHARDS)]
    parts_up = plane_start(sizes, stacked(up_weight, steps_up))
    pieces_out = [out_weight, *steps_out, *parts_out]
    hidden, second_in, out_low, up_low = out_call(
        place, values, after(mixed, *parts_down[1:3], every_up), gain_two, shift_two, bias_out, out_adapt_in,
        out_adapt_out, up_adapt_in, pieces_out,
    )
    parts_down[3] = after(parts_down[3], hidden)

    pieces_down = [down_weight, *steps_down, *swap_cores(sizes, parts_down)]
    written = active_grad_call(
        place, after(upstream, hidden), down_adapt_in, down_adapt_out, pieces_down, 0, 2
    )
    parts_up[1:] = after_all(parts_up[1:], written[0])
    parts_up = plane_end(sizes, parts_up)
    grad_active, grad_down_low = active_grad_call(
        place, after(upstream, *parts_up[1:3]), down_adapt_in, down_adapt_out, pieces_down, 2, 5, written
    )
    parts_up[3] = after(parts_up[3], grad_active)
    pieces_up = [up_weight, every_up, *swap_cores(sizes, parts_up)]
    active, grad_second, down_low, grad_up_out, grad_down_in = up_call(
        place, second_in, up_low, grad_active, grad_down_low, bias_up, up_adapt_out, down_adapt_in, pieces_up
    )
    grad_hidden, grad_mixed, grad_up_in, grad_out_out, grad_out_in, grad_down_out = out_grad_call(
        place, grad_second, hidden, second_in, upstream, mixed, out_low, down_low, gain_two,
        up_adapt_in, out_adapt_in, out_adapt_out, pieces_out,
    )
    terms = [grad_up_out, grad_down_in, grad_up_in, grad_out_out, grad_out_in, grad_down_out]
    widths = [(term.shape[1],) for term in terms]
    sent = send_adapters(sizes, terms, chosen)
    everyone = share_adapters(sent)
    near_grads, far_grads = attend_backward(meta, queries, far, near, after(grad_mixed, sent), mixed, logsums)
    everyone = after(everyone, near_grads)
    moved = 0
    for offset in range(reach, 0, -1):
        first_row = (reach - offset) * row_count
        moved += shifted(far_grads[:, first_row : first_row + row_count], ctx, -offset)
    halves = both_halves(sizes, everyone)
    numbers = sequence_numbers(sizes, everyone)
    grad_input, grad_qkv_out, grad_qkv_in = tokens_grad_call(
        place, values, first_in, qkv_low, grad_hidden, gain_one, qkv_adapt_in, adapter_qkv_out,
        after(near_grads, everyone), moved, pieces_qkv,
    )
    last_sent = send_adapters(sizes, [grad_qkv_out, grad_qkv_in], chosen)
    last_everyone = share_adapters(last_sent)
    numbers, active = after_all([numbers, active], last_sent)
    totals = combine_call(numbers, halves, widths)
    total_up_out, total_down_in, total_up_in, total_out_out, total_out_in, total_down_out = totals
    output = down_call(
        place, after(active, *totals), hidden, down_low, bias_down, down_adapt_out, pieces_down
    )
    last_halves = both_halves(sizes, after(last_everyone, output))
    total_qkv_out, total_qkv_in = combine_call(numbers, last_halves, [(feature_count,) * 3, (feature_count,)])
    return (
        output.T[None],
        grad_input.T[None],
        total_qkv_in,
        total_qkv_out,
        total_out_in,
        total_out_out,
        total_up_in,
        total_up_out,
        total_down_in,
        total_down_out,
    )


def solution(mesh):
    return jax.shard_map(
        partial(shards, dict(mesh.shape)),
        mesh=mesh,
        in_specs=(
            P(("dp", "wt"), "ctx", None),
            P(("dp", "wt"), "ctx", None),
            P(("dp", "wt"), None),
            P(("dp", "wt"), None),
            P("wt"),
            P("wt"),
            P("wt", None),
            P("wt"),
            P("wt", None),
            P("wt"),
            P("wt"),
            P("wt"),
            P("wt", None),
            P("wt"),
            P("wt", None),
            P("wt"),
            P(),
            P(),
            P(),
            P(),
            P(),
            P(),
            P(),
            P(),
        ),
        out_specs=(
            P(("dp", "wt"), "ctx", None),
            P(("dp", "wt"), "ctx", None),
            P(),
            P(),
            P(),
            P(),
            P(),
            P(),
            P(),
            P(),
        ),
        check_vma=False,
    )
```

```python
from functools import partial

import jax
import jax.numpy as jnp
from jax import lax
from jax.experimental import pallas as pl
from jax.experimental.pallas import tpu as pltpu
from jax.sharding import PartitionSpec as P

HEADS = 25
HEAD_DIM = 64
ADAPTERS = 8
WINDOW = 1024
RANK = 16
EPSILON = 1e-05
MASKED = -1e30

PAIRS = (HEADS + 1) // 2
PADDED = PAIRS * 128
FACTOR = HEAD_DIM ** (-0.5)
SHARDS = 4
PARTS = 8
BLOCK = 256
FF_CHUNK = 1280
VMEM_LIMIT = 60 << 20

def product(left_side, right_side):
    return lax.dot_general(left_side, right_side, (((1,), (0,)), ((), ())), preferred_element_type=jnp.float32)


def product_transposed(left_side, right_side):
    return lax.dot_general(left_side, right_side, (((1,), (1,)), ((), ())), preferred_element_type=jnp.float32)


def product_outer(left_side, right_side):
    return lax.dot_general(left_side, right_side, (((0,), (0,)), ((), ())), preferred_element_type=jnp.float32)


def norm_forward(values, norm_gain, norm_shift):
    center = values - jnp.mean(values, axis=-1, keepdims=True)
    inverse = lax.rsqrt(jnp.mean(center * center, axis=-1, keepdims=True) + EPSILON)
    normed = center * inverse
    return (normed * norm_gain + norm_shift, normed, inverse)


def norm_backward(upstream, normed, inverse, norm_gain):
    scaled = upstream * norm_gain
    return inverse * (
        scaled
        - jnp.mean(scaled, axis=-1, keepdims=True)
        - normed * jnp.mean(scaled * normed, axis=-1, keepdims=True)
    )


def copy_piece(source, target, row, columns, sem):
    start = pl.multiple_of(row, 16)
    pltpu.make_async_copy(source, target.at[pl.ds(start, source.shape[0]), columns], sem).start()


def start_shard(pieces, place, distance, target, source_columns, columns, sem):
    own, steps = pieces[0], pieces[1:SHARDS]
    together = len(steps[0].shape) == 3
    parts = pieces[2:] if together else pieces[SHARDS:]
    base = place[distance] * own.shape[0]
    if distance == 0:
        copy_piece(own.at[:, source_columns], target, base, columns, sem)
        return
    part_rows = own.shape[0] // (PARTS * 16) * 16
    for source in range(PARTS):
        if len(parts) == PARTS:
            part = parts[source].at[distance - 1, pl.ds(0, part_rows), source_columns]
        else:
            part = parts[(distance - 1) * PARTS + source].at[:, source_columns]
        row = base + place[SHARDS + source] * part_rows
        copy_piece(part, target, row, columns, sem)
    left = own.shape[0] - PARTS * part_rows
    base += PARTS * part_rows
    if left > RANK:
        left //= SHARDS
        for source in range(SHARDS):
            rest = parts[source].at[distance - 1, pl.ds(part_rows, left), source_columns]
            copy_piece(rest, target, base + place[SHARDS + source] // 2 * left, columns, sem)
        return
    step = steps[0].at[place[distance]] if together else steps[distance - 1]
    copy_piece(step.at[pl.ds(part_rows, left), source_columns], target, base, columns, sem)


def start_columns(pieces, place, target, source_columns, columns, sem):
    for distance in range(SHARDS):
        start_shard(pieces, place, distance, target, source_columns, columns, sem)


def wait_rows(target, start, rows, columns, sem):
    whole = target.at[pl.ds(start, rows), columns]
    pltpu.make_async_copy(whole, whole, sem).wait()


def widen(wide, low):
    rows = wide.shape[0]
    fill = jnp.zeros((rows, PADDED - wide.shape[1] - low.shape[1]), jnp.bfloat16)
    return jnp.concatenate([wide, low, fill], axis=1)


def blocks_of(rows):
    return [pl.ds(start, BLOCK) for start in range(0, rows, BLOCK)]


HBM = pl.BlockSpec(memory_space=pl.ANY)


def whole_of(array):
    shape = array.shape
    return pl.BlockSpec(shape, lambda *_: (0,) * len(shape))


def call(kernel, name, grid, place, inputs, pieces, in_specs, outs, out_specs, scratch, macs, aliases={}):
    return pl.pallas_call(
        kernel,
        grid_spec=pltpu.PrefetchScalarGridSpec(
            num_scalar_prefetch=1,
            grid=grid,
            in_specs=in_specs + [HBM] * len(pieces),
            out_specs=out_specs,
            scratch_shapes=scratch,
        ),
        out_shape=outs,
        input_output_aliases=aliases,
        compiler_params=pltpu.CompilerParams(vmem_limit_bytes=VMEM_LIMIT),
        cost_estimate=pl.CostEstimate(flops=2 * macs, bytes_accessed=1 << 22, transcendentals=0),
        name=name,
    )(place, *inputs, *pieces)


def out_of(shape, kind):
    return jax.ShapeDtypeStruct(shape, kind)


def picked(width, column=lambda *grid: 0):
    return pl.BlockSpec((None, RANK, width), lambda c, place: (place[SHARDS + PARTS], 0, column(c)))


def column_block(rows, width):
    return pl.BlockSpec((rows, width), lambda c, *_: (0, c))


def row_block(width):
    return pl.BlockSpec((BLOCK, width), lambda r, *_: (r, 0))


def keys_kernel(place, x_ref, gain, shift, bias, a_in, a_out, *more):
    pieces, (first_ref, low_ref, kv_ref, w, wide, sems) = more[:-6], more[-6:]
    rows, features = x_ref.shape

    @pl.when(pl.program_id(0) == 0)
    def _():
        fetch_columns(pieces, place, w, sems, 0, 1)
        for slot in range(2):
            clear_tail(w.at[slot], features)
        for block in blocks_of(rows):
            normed_in, _, _ = norm_forward(x_ref[block, :].astype(jnp.float32), gain[...], shift[...])
            first = normed_in.astype(jnp.bfloat16)
            low = product_transposed(first, a_in[...]).astype(jnp.bfloat16)
            first_ref[block, :] = first
            low_ref[block, :] = low
            wide[block, :] = widen(first, low)

    slot = next_columns(pieces, place, w, sems, features, 1)
    w[slot, pl.ds(features, RANK), :] = a_out[...]
    for block in blocks_of(rows):
        kv_ref[block, :] = (product(wide[block, :], w[slot]) + bias[...]).astype(jnp.bfloat16)


def fetch_columns(pieces, place, w, sems, c, offset=0):
    width = w.shape[2]
    columns = pl.ds(pl.multiple_of((c + offset) * width, 128), width)
    start_columns(pieces, place, w.at[c % 2], columns, pl.ds(0, width), sems.at[c % 2])


def next_columns(pieces, place, w, sems, features, offset=0):
    step, steps = pl.program_id(0), pl.num_programs(0)

    @pl.when(step + 1 < steps)
    def _():
        fetch_columns(pieces, place, w, sems, step + 1, offset)

    slot = lax.rem(step, 2)
    wait_rows(w.at[slot], 0, features, pl.ds(0, w.shape[2]), sems.at[slot])
    return slot


def clear_tail(w, features):
    count = w.shape[0] - features - RANK
    w[pl.ds(features + RANK, count), :] = jnp.zeros((count, w.shape[1]), jnp.bfloat16)


def keys_call(place, x, gain, shift, bias, a_in, a_out, pieces):
    rows, features = x.shape
    width = PADDED
    third = lambda height: pl.BlockSpec((height, width), lambda c, *_: (0, c + 1))
    return call(
        keys_kernel, "keys", (2,), place, [x, gain, shift, bias, a_in, a_out], pieces,
        [whole_of(x), whole_of(gain), whole_of(shift), third(1), picked(features), third(RANK)],
        [out_of((rows, features), jnp.bfloat16), out_of((rows, RANK), jnp.bfloat16), out_of((rows, 2 * width), jnp.bfloat16)],
        [whole_of(x), pl.BlockSpec((rows, RANK), lambda *_: (0, 0)), column_block(rows, width)],
        [pltpu.VMEM((2, PADDED, width), jnp.bfloat16), pltpu.VMEM((rows, PADDED), jnp.bfloat16), pltpu.SemaphoreType.DMA((2,))],
        rows * features * 2 * width,
    )


def queries_kernel(place, first_ref, low_ref, bias, a_out, *more):
    pieces, (q_ref, w, sems) = more[:-3], more[-3:]
    rows, features = first_ref.shape
    width = w.shape[1]
    halves = [pl.ds(0, width // 256 * 128), pl.ds(width // 256 * 128, width - width // 256 * 128)]
    for half, columns in enumerate(halves):
        start_columns(pieces, place, w, columns, columns, sems.at[half])
    clear_tail(w, features)
    w[pl.ds(features, RANK), :] = a_out[...]
    for half, columns in enumerate(halves):
        wait_rows(w, 0, features, columns, sems.at[half])
        for block in blocks_of(rows):
            wide = widen(first_ref[block, :], low_ref[block, :])
            q_ref[block, columns] = (product(wide, w[:, columns]) + bias[:, columns]).astype(jnp.bfloat16)


def queries_call(place, first, low, bias, a_out, pieces):
    rows, features = first.shape
    width = PADDED
    return call(
        queries_kernel, "queries", (1,), place, [first, low, bias, a_out], pieces,
        [whole_of(first), whole_of(low), column_block(1, width), column_block(RANK, width)],
        out_of((rows, width), jnp.bfloat16),
        column_block(rows, width),
        [pltpu.VMEM((PADDED, width), jnp.bfloat16), pltpu.SemaphoreType.DMA((2,))],
        rows * features * width,
    )


def out_kernel(place, x_ref, mixed_ref, gain, shift, bias, a_in, a_out, u_in, *more):
    pieces, (hidden_ref, second_ref, low_ref, up_low_ref, w, sem) = more[:-6], more[-6:]
    features = x_ref.shape[1]

    @pl.when(pl.program_id(0) == 0)
    def _():
        start_columns(pieces, place, w, pl.ds(0, features), pl.ds(0, features), sem)
        w[pl.ds(features, RANK), :] = a_out[...]
        w[pl.ds(features + RANK, PADDED - features - RANK), :] = jnp.zeros(
            (PADDED - features - RANK, features), jnp.bfloat16
        )
        wait_rows(w, 0, features, pl.ds(0, features), sem)

    mixed = mixed_ref[:, :features]
    low = product_transposed(mixed, a_in[...]).astype(jnp.bfloat16)
    hidden = x_ref[...].astype(jnp.float32) + (product(widen(mixed, low), w[...]) + bias[...])
    normed_mid, _, _ = norm_forward(hidden, gain[...], shift[...])
    second = normed_mid.astype(jnp.bfloat16)
    hidden_ref[...] = hidden
    second_ref[...] = second
    low_ref[...] = low
    up_low_ref[...] = product_transposed(second, u_in[...]).astype(jnp.bfloat16)


def out_call(place, x, mixed, gain, shift, bias, a_in, a_out, u_in, pieces):
    rows, features = x.shape
    return call(
        out_kernel, "out", (rows // BLOCK,), place, [x, mixed, gain, shift, bias, a_in, a_out, u_in], pieces,
        [row_block(features), row_block(PADDED)] + [whole_of(a) for a in (gain, shift, bias)] + [picked(features)] * 3,
        [out_of((rows, features), jnp.float32), out_of((rows, features), jnp.bfloat16), out_of((rows, RANK), jnp.bfloat16), out_of((rows, RANK), jnp.bfloat16)],
        [row_block(features), row_block(features), row_block(RANK), row_block(RANK)],
        [pltpu.VMEM((PADDED, features), jnp.bfloat16), pltpu.SemaphoreType.DMA(())],
        rows * features * features,
    )


def fetch_down(pieces, place, w, sems, first=0, last=None):
    width = w.shape[1]
    shard_rows = w.shape[0] // SHARDS
    last = w.shape[0] // FF_CHUNK if last is None else last
    for shard in range(SHARDS):
        if shard * shard_rows >= last * FF_CHUNK or (shard + 1) * shard_rows <= first * FF_CHUNK:
            continue
        for distance in range(SHARDS):
            @pl.when(place[distance] == shard)
            def _():
                start_shard(pieces, place, distance, w, pl.ds(0, width), pl.ds(0, width), sems.at[shard])


def wait_down(step, w, sems, first=0, last=None):
    shard_rows = w.shape[0] // SHARDS
    last = w.shape[0] // FF_CHUNK if last is None else last
    for shard in range(SHARDS):
        if shard * shard_rows >= last * FF_CHUNK or (shard + 1) * shard_rows <= first * FF_CHUNK:
            continue
        first_step = max(first, -(-(shard * shard_rows - FF_CHUNK + 1) // FF_CHUNK))

        @pl.when(step == first_step)
        def _():
            wait_rows(w, shard * shard_rows, shard_rows, pl.ds(0, w.shape[1]), sems.at[shard])


def active_grad_kernel(first, last, place, cot_ref, a_in, a_out, *more):
    pieces, (g_ref, low_ref, w, sems) = more[:-4], more[-4:]
    pieces = pieces[: len(pieces) - (2 if first else 0)]
    rows, features = cot_ref.shape
    step = pl.program_id(0) + first

    @pl.when(step == first)
    def _():
        fetch_down(pieces, place, w, sems, first, last)
        for block in blocks_of(rows):
            low_ref[block, :] = product_transposed(cot_ref[block, :], a_out[...]).astype(jnp.bfloat16)

    wait_down(step, w, sems, first, last)
    weight = w[pl.ds(pl.multiple_of(step * FF_CHUNK, FF_CHUNK), FF_CHUNK), :]
    for block in blocks_of(rows):
        g_ref[block, :] = (
            product_transposed(cot_ref[block, :], weight) + product(low_ref[block, :], a_in[...])
        ).astype(jnp.bfloat16)


def active_grad_call(place, cot, a_in, a_out, pieces, first, last, written=()):
    rows, features = cot.shape
    units = a_in.shape[2]
    chunk = lambda height: pl.BlockSpec((height, FF_CHUNK), lambda c, *_: (0, c + first))
    return call(
        partial(active_grad_kernel, first, last), "active_grad", (last - first,), place, [cot, a_in, a_out],
        [*pieces, *written],
        [whole_of(cot), picked(FF_CHUNK, lambda c: c + first), picked(features)],
        [out_of((rows, units), jnp.bfloat16), out_of((rows, RANK), jnp.bfloat16)],
        [chunk(rows), pl.BlockSpec((rows, RANK), lambda *_: (0, 0))],
        [pltpu.VMEM((units, features), jnp.bfloat16), pltpu.SemaphoreType.DMA((SHARDS,))],
        rows * features * FF_CHUNK * (last - first),
        {4 + len(pieces) + place: place for place in range(len(written))},
    )


GELU_A = 0.7978845608
GELU_B = 0.044715


def up_kernel(place, second_ref, up_low_ref, g_active_ref, g_low_ref, bias, u_out, d_in, *more):
    pieces, (active_ref, acc_ref, down_low_ref, g_up_out_ref, g_down_in_ref, w, wide, low_scr, g_scr, sems) = more[:-10], more[-10:]
    rows, features = second_ref.shape
    step, steps = pl.program_id(0), pl.num_programs(0)
    width = w.shape[2]

    def fetch(c):
        columns = pl.ds(pl.multiple_of(c * width, 128), width)
        start_columns(pieces, place, w.at[c % 2], columns, pl.ds(0, width), sems.at[c % 2])

    @pl.when(step == 0)
    def _():
        fetch(0)
        for slot in range(2):
            w[slot, pl.ds(features + RANK, PADDED - features - RANK), :] = jnp.zeros(
                (PADDED - features - RANK, width), jnp.bfloat16
            )
        acc_ref[...] = jnp.zeros_like(acc_ref)
        low_scr[...] = jnp.zeros_like(low_scr)
        for block in blocks_of(rows):
            wide[block, :] = widen(second_ref[block, :], up_low_ref[block, :])

    @pl.when(step + 1 < steps)
    def _():
        fetch(step + 1)

    slot = lax.rem(step, 2)
    wait_rows(w.at[slot], 0, features, pl.ds(0, width), sems.at[slot])
    w[slot, pl.ds(features, RANK), :] = u_out[...]
    blocks = blocks_of(rows)
    ahead = product(wide[blocks[0], :], w[slot])
    for number, block in enumerate(blocks):
        upper = ahead + bias[...]
        if number + 1 < len(blocks):
            ahead = product(wide[blocks[number + 1], :], w[slot])
        square = upper * upper
        inner = jnp.tanh(upper * (GELU_A + (GELU_A * GELU_B) * square))
        half = 0.5 + 0.5 * inner
        active = (upper * half).astype(jnp.bfloat16)
        slope = half + upper * (1.0 - inner * inner) * (0.5 * GELU_A + (1.5 * GELU_A * GELU_B) * square)
        g_upper = (g_active_ref[block, :].astype(jnp.float32) * slope).astype(jnp.bfloat16)
        active_ref[block, :] = active
        g_scr[block, :] = g_upper
        acc_ref[block, :] += product_transposed(g_upper, w[slot])
        low_scr[block, :] += product_transposed(active, d_in[...])
    g_up_out_ref[...] = product_outer(up_low_ref[...], g_scr[...])
    g_down_in_ref[...] = product_outer(g_low_ref[...], active_ref[...])

    @pl.when(step == steps - 1)
    def _():
        down_low_ref[...] = low_scr[...].astype(jnp.bfloat16)


def up_call(place, second, up_low, g_active, g_low, bias, u_out, d_in, pieces):
    rows, features = second.shape
    units = bias.shape[1]
    low_block = pl.BlockSpec((rows, RANK), lambda *_: (0, 0))
    return call(
        up_kernel, "up", (units // FF_CHUNK,), place, [second, up_low, g_active, g_low, bias, u_out, d_in], pieces,
        [whole_of(second), low_block, column_block(rows, FF_CHUNK), low_block,
         column_block(1, FF_CHUNK), picked(FF_CHUNK, lambda c: c), picked(FF_CHUNK, lambda c: c)],
        [out_of((rows, units), jnp.bfloat16), out_of((rows, PADDED), jnp.float32), out_of((rows, RANK), jnp.bfloat16),
         out_of((RANK, units), jnp.float32), out_of((RANK, units), jnp.float32)],
        [column_block(rows, FF_CHUNK), pl.BlockSpec((rows, PADDED), lambda *_: (0, 0)), low_block,
         column_block(RANK, FF_CHUNK), column_block(RANK, FF_CHUNK)],
        [pltpu.VMEM((2, PADDED, FF_CHUNK), jnp.bfloat16), pltpu.VMEM((rows, PADDED), jnp.bfloat16), pltpu.VMEM((rows, RANK), jnp.float32),
         pltpu.VMEM((rows, FF_CHUNK), jnp.bfloat16), pltpu.SemaphoreType.DMA((2,))],
        2 * rows * features * units,
    )


def out_grad_kernel(place, acc_ref, hidden_ref, second_ref, cot_ref, mixed_ref, low_ref, down_low_ref, gain, u_in, a_in, a_out, *more):
    pieces, (g_hidden_ref, g_mixed_ref, g_up_in, g_out_out, g_out_in, g_down_out, w, sem) = more[:-8], more[-8:]
    features = hidden_ref.shape[1]
    step = pl.program_id(0)

    @pl.when(step == 0)
    def _():
        start_columns(pieces, place, w, pl.ds(0, features), pl.ds(0, features), sem)
        w[pl.ds(features, RANK), :] = a_out[...]
        w[pl.ds(features + RANK, PADDED - features - RANK), :] = jnp.zeros(
            (PADDED - features - RANK, features), jnp.bfloat16
        )

    g_up_low = acc_ref[:, features : features + RANK].astype(jnp.bfloat16)
    g_second = acc_ref[:, :features] + product(g_up_low, u_in[...])
    _, normed, inverse = norm_forward(hidden_ref[...], gain[...], 0.0)
    cot = cot_ref[...]
    g_hidden = cot.astype(jnp.float32) + norm_backward(g_second, normed, inverse, gain[...])
    g_branch = g_hidden.astype(jnp.bfloat16)
    g_hidden_ref[...] = g_hidden

    @pl.when(step == 0)
    def _():
        wait_rows(w, 0, features, pl.ds(0, features), sem)

    back = product_transposed(g_branch, w[...])
    g_low = back[:, features : features + RANK].astype(jnp.bfloat16)
    g_mixed = back[:, :features] + product(g_low, a_in[...])
    g_mixed_ref[:, :features] = g_mixed.astype(jnp.bfloat16)
    g_mixed_ref[:, features:] = jnp.zeros((BLOCK, PADDED - features), jnp.bfloat16)
    sums = (
        product_outer(g_up_low, second_ref[...]),
        product_outer(low_ref[...], g_branch),
        product_outer(g_low, mixed_ref[:, :features]),
        product_outer(down_low_ref[...], cot),
    )
    for total, term in zip((g_up_in, g_out_out, g_out_in, g_down_out), sums):
        @pl.when(step == 0)
        def _():
            total[...] = term

        @pl.when(step > 0)
        def _():
            total[...] += term


def out_grad_call(place, acc, hidden, second, cot, mixed, low, down_low, gain, u_in, a_in, a_out, pieces):
    rows, features = hidden.shape
    small = pl.BlockSpec((RANK, features), lambda *_: (0, 0))
    return call(
        out_grad_kernel, "out_grad", (rows // BLOCK,), place,
        [acc, hidden, second, cot, mixed, low, down_low, gain, u_in, a_in, a_out], pieces,
        [row_block(PADDED), row_block(features), row_block(features), row_block(features), row_block(PADDED),
         row_block(RANK), row_block(RANK), whole_of(gain)] + [picked(features)] * 3,
        [out_of((rows, features), jnp.float32), out_of((rows, PADDED), jnp.bfloat16)] + [out_of((RANK, features), jnp.float32)] * 4,
        [row_block(features), row_block(PADDED)] + [small] * 4,
        [pltpu.VMEM((PADDED, features), jnp.bfloat16), pltpu.SemaphoreType.DMA(())],
        rows * features * features,
    )


def down_kernel(place, active_ref, hidden_ref, down_low_ref, bias, a_out, *more):
    pieces, (out_ref, w, acc, hidden, sems, late) = more[:-6], more[-6:]
    rows, features = hidden_ref.shape
    step, steps = pl.program_id(0), pl.num_programs(0)
    copy = pltpu.make_async_copy(hidden_ref, hidden, late)

    @pl.when(step == 0)
    def _():
        fetch_down(pieces, place, w, sems)
        copy.start()
        for block in blocks_of(rows):
            acc[block, :] = product(down_low_ref[block, :], a_out[...]) + bias[...]

    wait_down(step, w, sems)
    weight = w[pl.ds(pl.multiple_of(step * FF_CHUNK, FF_CHUNK), FF_CHUNK), :]
    for block in blocks_of(rows):
        acc[block, :] += product(active_ref[block, :], weight)

    @pl.when(step == steps - 1)
    def _():
        copy.wait()
        for block in blocks_of(rows):
            out_ref[:, block] = (hidden[block, :] + acc[block, :]).astype(jnp.bfloat16).T


def down_call(place, active, hidden, down_low, bias, a_out, pieces):
    rows, features = hidden.shape
    units = active.shape[1]
    return call(
        down_kernel, "down", (units // FF_CHUNK,), place, [active, hidden, down_low, bias, a_out], pieces,
        [column_block(rows, FF_CHUNK), HBM, pl.BlockSpec((rows, RANK), lambda *_: (0, 0)),
         whole_of(bias), picked(features)],
        out_of((features, rows), jnp.bfloat16),
        pl.BlockSpec((features, rows), lambda *_: (0, 0)),
        [pltpu.VMEM((units, features), jnp.bfloat16), pltpu.VMEM((rows, features), jnp.float32), pltpu.VMEM((rows, features), jnp.float32),
         pltpu.SemaphoreType.DMA((SHARDS,)), pltpu.SemaphoreType.DMA(())],
        rows * features * units,
    )


def qkv_out_kernel(place, low_ref, near_ref, far_ref, out_ref):
    scale = jnp.where(pl.program_id(0) > 0, 1.0, 0.0)
    g = (near_ref[...].astype(jnp.float32) + scale * far_ref[...].astype(jnp.float32)).astype(jnp.bfloat16)
    out_ref[...] = product_outer(low_ref[...], g)


def qkv_out_call(place, low, near, far):
    rows = low.shape[0]
    near_block = pl.BlockSpec((None, rows, PADDED), lambda c, *_: (c, 0, 0))
    far_block = pl.BlockSpec((None, rows, PADDED), lambda c, *_: (jnp.maximum(c - 1, 0), 0, 0))
    return call(
        qkv_out_kernel, "qkv_out", (3,), place, [low, near, far], [],
        [whole_of(low), near_block, far_block],
        out_of((RANK, 3 * PADDED), jnp.float32),
        column_block(RANK, PADDED),
        [],
        3 * rows * PADDED * RANK,
    )


def tokens_grad_kernel(place, x_ref, first_ref, g_hidden_ref, gain, a_in, a_out, near_ref, far_ref, *more):
    pieces, (out_ref, g_qkv_in, w, acc, x, first, g_hidden, sems, late) = more[:-9], more[-9:]
    rows, features = x_ref.shape
    step, steps = pl.program_id(0), pl.num_programs(0)
    pairs = ((x_ref, x), (first_ref, first), (g_hidden_ref, g_hidden))
    copies = [pltpu.make_async_copy(*pair, late.at[number]) for number, pair in enumerate(pairs)]

    @pl.when(step == 0)
    def _():
        fetch_columns(pieces, place, w, sems, 0)
        for slot in range(2):
            clear_tail(w.at[slot], features)
        acc[...] = jnp.zeros_like(acc)

    @pl.when(step == 1)
    def _():
        for copy in copies:
            copy.start()

    slot = next_columns(pieces, place, w, sems, features)
    w[slot, pl.ds(features, RANK), :] = a_out[...]
    scale = jnp.where(step > 0, 1.0, 0.0)
    for block in blocks_of(rows):
        g = (near_ref[block, :].astype(jnp.float32) + scale * far_ref[block, :].astype(jnp.float32)).astype(jnp.bfloat16)
        acc[block, :] += product_transposed(g, w[slot])

    @pl.when(step == steps - 1)
    def _():
        for copy in copies:
            copy.wait()
        qkv_in_sum = jnp.zeros((RANK, features), jnp.float32)
        for block in blocks_of(rows):
            g_low = acc[block, pl.ds(features, RANK)].astype(jnp.bfloat16)
            g_first = acc[block, pl.ds(0, features)] + product(g_low, a_in[...])
            _, normed, inverse = norm_forward(x[block, :].astype(jnp.float32), gain[...], 0.0)
            out_ref[:, block] = (g_hidden[block, :] + norm_backward(g_first, normed, inverse, gain[...])).T
            qkv_in_sum += product_outer(g_low, first[block, :])
        g_qkv_in[...] = qkv_in_sum


def tokens_grad_call(place, x, first, g_hidden, gain, a_in, a_out, near, far, pieces):
    rows, features = x.shape
    steps = 3
    near_block = pl.BlockSpec((None, rows, PADDED), lambda c, *_: (c, 0, 0))
    far_block = pl.BlockSpec((None, rows, PADDED), lambda c, *_: (jnp.maximum(c - 1, 0), 0, 0))
    return call(
        tokens_grad_kernel, "tokens_grad", (steps,), place, [x, first, g_hidden, gain, a_in, a_out, near, far], pieces,
        [HBM, HBM, HBM, whole_of(gain), picked(features),
         column_block(RANK, PADDED), near_block, far_block],
        [out_of((features, rows), jnp.float32), out_of((RANK, features), jnp.float32)],
        [pl.BlockSpec((features, rows), lambda *_: (0, 0)),
         pl.BlockSpec((RANK, features), lambda *_: (0, 0))],
        [pltpu.VMEM((2, PADDED, PADDED), jnp.bfloat16), pltpu.VMEM((rows, PADDED), jnp.float32),
         pltpu.VMEM((rows, features), jnp.bfloat16), pltpu.VMEM((rows, features), jnp.bfloat16), pltpu.VMEM((rows, features), jnp.float32),
         pltpu.SemaphoreType.DMA((2,)), pltpu.SemaphoreType.DMA((3,))],
        rows * features * steps * PADDED,
    )


def combine_kernel(widths, numbers, *refs):
    parts, totals = refs[: -len(widths)], refs[-len(widths) :]
    sequences, _, part_width = parts[0].shape
    half_width = part_width - 128

    def add(halves):
        start = 0
        for total, spans in zip(totals, widths):
            into = 0
            for width in spans:
                done = 0
                while done < width:
                    half, at = divmod(start + done, half_width)
                    size = min(width - done, half_width - at)
                    for sequence in range(sequences):
                        target = (numbers[sequence], slice(None), pl.ds(into + done, size))
                        total[target] += halves[half][sequence, :, pl.ds(at, size)].astype(jnp.float32)
                    done += size
                into += width
                start += -(-width // 128) * 128

    for total in totals:
        total[...] = jnp.zeros_like(total)
    turned = numbers[sequences]

    @pl.when(turned == 0)
    def _():
        add(parts)

    if len(parts) == 2:
        @pl.when(turned == 1)
        def _():
            add(parts[::-1])


def combine_call(numbers, parts, widths):
    shapes = [(ADAPTERS, RANK, sum(spans)) for spans in widths]
    return pl.pallas_call(
        partial(combine_kernel, widths),
        grid_spec=pltpu.PrefetchScalarGridSpec(
            num_scalar_prefetch=1,
            grid=(1,),
            in_specs=[whole_of(part) for part in parts],
            out_specs=[pl.BlockSpec(shape, lambda *_: (0, 0, 0)) for shape in shapes],
        ),
        out_shape=[out_of(shape, jnp.float32) for shape in shapes],
        compiler_params=pltpu.CompilerParams(vmem_limit_bytes=VMEM_LIMIT),
        cost_estimate=pl.CostEstimate(flops=1 << 30, bytes_accessed=1 << 22, transcendentals=0),
        name="combine",
    )(numbers, *parts)


TILE = 256
REACH_TILES = WINDOW // TILE
SPAN_TILES = REACH_TILES + 1


def split_pair(pair):
    lane = lax.broadcasted_iota(jnp.int32, pair.shape, 1)
    zero = jnp.zeros_like(pair)
    return jnp.concatenate(
        [jnp.where(lane < HEAD_DIM, pair, zero), jnp.where(lane >= HEAD_DIM, pair, zero)], axis=0
    )


def join_pair(stacked):
    lane = lax.broadcasted_iota(jnp.int32, (TILE, 128), 1)
    return jnp.where(lane < HEAD_DIM, stacked[:TILE], stacked[TILE:])


def tile_bias(bounds, query_start, key_start):
    rows = query_start + lax.broadcasted_iota(jnp.int32, (TILE, 1), 0)
    columns = key_start + lax.broadcasted_iota(jnp.int32, (1, TILE), 1)
    row_doc = sum((rows >= bound).astype(jnp.int32) for bound in bounds)
    column_doc = sum((columns >= bound).astype(jnp.int32) for bound in bounds)
    shape = (TILE, TILE)
    distance = jnp.broadcast_to(rows, shape) - jnp.broadcast_to(columns, shape)
    same = jnp.broadcast_to(row_doc, shape) == jnp.broadcast_to(column_doc, shape)
    seen = jnp.broadcast_to(columns, shape) >= 0
    return jnp.where(same & seen & (distance >= 0) & (distance < WINDOW), 0.0, MASKED)


def fill_biases(meta, bias_scr, tiles):
    bounds = [meta[place] for place in range(3)]
    first = meta[3]

    def one(step, carry):
        tile = step // SPAN_TILES
        key_tile = tile + lax.rem(step, SPAN_TILES) - REACH_TILES
        bias_scr[step] = tile_bias(bounds, first + tile * TILE, first + key_tile * TILE)
        return carry

    lax.fori_loop(0, tiles * SPAN_TILES, one, 0)


def key_tile(far_ref, near_ref, tile):
    if tile < REACH_TILES:
        return far_ref[pl.ds(tile * TILE, TILE), :]
    return near_ref[pl.ds((tile - REACH_TILES) * TILE, TILE), :]


def attend_forward_kernel(tiles, meta, q_ref, k_far, v_far, k_near, v_near, *more):
    o_ref, lse_ref, bias_scr, acc_scr = more[-4:]

    @pl.when(pl.program_id(0) == 0)
    def _():
        fill_biases(meta, bias_scr, tiles)

    ones = jnp.ones((TILE, 128), jnp.bfloat16)
    chunk = TILE // 2
    for tile in range(tiles):
        stacked = split_pair(q_ref[pl.ds(tile * TILE, TILE), :] * FACTOR)
        span = range(tile, tile + SPAN_TILES)
        keys = jnp.concatenate([key_tile(k_far, k_near, t) for t in span], axis=0)
        values = jnp.concatenate(
            [jnp.concatenate([key_tile(v_far, v_near, t), ones], axis=1) for t in span], axis=0
        )
        for part in range(2 * TILE // chunk):
            start = part * chunk
            bias_rows = pl.ds(start % TILE, chunk)
            bias = jnp.concatenate(
                [bias_scr[tile * SPAN_TILES + t, bias_rows, :] for t in range(SPAN_TILES)], axis=1
            )
            scores = product_transposed(stacked[start : start + chunk], keys) + bias
            highest = jnp.max(scores, axis=1, keepdims=True)
            mixed = product(jnp.exp(scores - highest).astype(jnp.bfloat16), values)
            summed = mixed[:, 128:]
            acc_scr[pl.ds(start, chunk), :] = mixed[:, :128] / summed
            lse_ref[pl.ds(tile * 2 * TILE + start, chunk), :] = highest + jnp.log(summed)
        o_ref[pl.ds(tile * TILE, TILE), :] = join_pair(acc_scr[...]).astype(jnp.bfloat16)


def pair_columns(rows, offset=0):
    return pl.BlockSpec((rows, 128), lambda j, *_: (0, offset + j))


def attention_cost(products, pairs, rows):
    macs = products * pairs * 2 * rows * SPAN_TILES * TILE * 256
    return pl.CostEstimate(flops=2 * macs, bytes_accessed=1 << 24, transcendentals=0)


def attend_forward(meta, queries, far, near, start, pairs, written=()):
    rows = queries.shape[0]
    tiles = rows // TILE
    return pl.pallas_call(
        partial(attend_forward_kernel, tiles),
        grid_spec=pltpu.PrefetchScalarGridSpec(
            num_scalar_prefetch=1,
            grid=(pairs,),
            in_specs=[
                pair_columns(rows, start), pair_columns(WINDOW, start), pair_columns(WINDOW, PAIRS + start),
                pair_columns(rows, start), pair_columns(rows, PAIRS + start),
            ] + [pl.BlockSpec(memory_space=pl.ANY)] * len(written),
            out_specs=[
                pair_columns(rows, start),
                pl.BlockSpec((None, 2 * rows, 128), lambda j, *_: (start + j, 0, 0)),
            ],
            scratch_shapes=[
                pltpu.VMEM((tiles * SPAN_TILES, TILE, TILE), jnp.float32),
                pltpu.VMEM((2 * TILE, 128), jnp.float32),
            ],
        ),
        out_shape=[
            jax.ShapeDtypeStruct((rows, PADDED), jnp.bfloat16),
            jax.ShapeDtypeStruct((PAIRS, 2 * rows, 128), jnp.float32),
        ],
        input_output_aliases={6 + place: place for place in range(len(written))},
        compiler_params=pltpu.CompilerParams(vmem_limit_bytes=VMEM_LIMIT),
        cost_estimate=attention_cost(2, pairs, rows),
        name="attend_forward",
    )(meta, queries, far, far, near, near, *written)


def attend_backward_kernel(
    tiles, meta, q_ref, k_far, v_far, k_near, v_near, g_ref, o_ref, lse_ref,
    near_ref, far_ref, bias_scr, dq_scr, dkt, dvt,
):
    @pl.when(pl.program_id(0) == 0)
    def _():
        fill_biases(meta, bias_scr, tiles)

    dkt[...] = jnp.zeros_like(dkt)
    dvt[...] = jnp.zeros_like(dvt)
    for tile in range(tiles):
        rows = pl.ds(tile * TILE, TILE)
        queries = split_pair(q_ref[rows, :] * FACTOR)
        grads = split_pair(g_ref[rows, :])
        mixed = o_ref[rows, :].astype(jnp.float32)
        centered = jnp.sum(
            grads.astype(jnp.float32) * jnp.concatenate([mixed, mixed], axis=0), axis=1, keepdims=True
        )
        lse = lse_ref[pl.ds(tile * 2 * TILE, 2 * TILE), :]
        lse = jnp.concatenate([lse, lse], axis=1)
        queries_t = queries.T
        grads_t = grads.T
        dq_scr[...] = jnp.zeros_like(dq_scr)
        for t in range(SPAN_TILES):
            keys = key_tile(k_far, k_near, tile + t)
            bias = bias_scr[tile * SPAN_TILES + t]
            scores = product_transposed(queries, keys)
            chances = jnp.exp(scores + jnp.concatenate([bias, bias], axis=0) - lse)
            grad_chances = product_transposed(grads, key_tile(v_far, v_near, tile + t))
            grad_scores = (chances * (grad_chances - centered)).astype(jnp.bfloat16)
            dvt[tile + t] += product(grads_t, chances.astype(jnp.bfloat16))
            dkt[tile + t] += product(queries_t, grad_scores)
            dq_scr[...] += product(grad_scores, keys)
        near_ref[0, rows, :] = (join_pair(dq_scr[...]) * FACTOR).astype(jnp.bfloat16)
    for t in range(tiles + REACH_TILES):
        target, first = (far_ref, 0) if t < REACH_TILES else (near_ref, 1)
        rows = pl.ds((t if t < REACH_TILES else t - REACH_TILES) * TILE, TILE)
        target[first, rows, :] = dkt[t].T.astype(jnp.bfloat16)
        target[first + 1, rows, :] = dvt[t].T.astype(jnp.bfloat16)


def attend_backward(meta, queries, far, near, grad_mixed, mixed, lse):
    rows = queries.shape[0]
    tiles = rows // TILE
    return pl.pallas_call(
        partial(attend_backward_kernel, tiles),
        grid_spec=pltpu.PrefetchScalarGridSpec(
            num_scalar_prefetch=1,
            grid=(PAIRS,),
            in_specs=[
                pair_columns(rows), pair_columns(WINDOW), pair_columns(WINDOW, PAIRS),
                pair_columns(rows), pair_columns(rows, PAIRS), pair_columns(rows), pair_columns(rows),
                pl.BlockSpec((None, 2 * rows, 128), lambda j, *_: (j, 0, 0)),
            ],
            out_specs=[
                pl.BlockSpec((3, rows, 128), lambda j, *_: (0, 0, j)),
                pl.BlockSpec((2, WINDOW, 128), lambda j, *_: (0, 0, j)),
            ],
            scratch_shapes=[
                pltpu.VMEM((tiles * SPAN_TILES, TILE, TILE), jnp.float32),
                pltpu.VMEM((2 * TILE, 128), jnp.float32),
                pltpu.VMEM((tiles + REACH_TILES, 128, TILE), jnp.float32),
                pltpu.VMEM((tiles + REACH_TILES, 128, TILE), jnp.float32),
            ],
        ),
        out_shape=[
            jax.ShapeDtypeStruct((3, rows, PADDED), jnp.bfloat16),
            jax.ShapeDtypeStruct((2, WINDOW, PADDED), jnp.bfloat16),
        ],
        compiler_params=pltpu.CompilerParams(vmem_limit_bytes=VMEM_LIMIT),
        cost_estimate=attention_cost(5, PAIRS, rows),
        name="attend_backward",
    )(meta, queries, far, far, near, near, grad_mixed, mixed, lse)


def ring_pairs(size):
    return [(i, (i + 1) % size) for i in range(size)]


def plane_pairs(sizes):
    first, second = [], []
    cores = sizes["ctx"]
    for chip in range(sizes["dp"]):
        for core in range(cores):
            steps = (chip ^ 1, chip ^ 2) if core % 2 == 0 else (chip ^ 2, chip ^ 1)
            here = chip * cores + core
            first.append((here, steps[0] * cores + core))
            second.append((here, steps[1] * cores + core))
    return first, second


def swap_pairs(size):
    return [(i, i ^ 1) for i in range(size)]


def shifted(array, size, by):
    pairs = [(i, i + by) for i in range(size) if 0 <= i + by < size]
    return lax.ppermute(array, "ctx", pairs)


def place_of(chosen):
    chip, core, shard = lax.axis_index("dp"), lax.axis_index("ctx") % 2, lax.axis_index("wt")
    places = [(shard - distance) % SHARDS for distance in range(SHARDS)]
    for side in (core, 1 - core):
        near = jnp.where(side == 0, chip ^ 1, chip ^ 2)
        for where in (chip, near, near ^ 3, chip ^ 3):
            places.append(where * 2 + side)
    return jnp.stack([*places, chosen]).astype(jnp.int32)


def after(array, *others):
    return lax.optimization_barrier((array, *others))[0]


def after_all(arrays, *others):
    return lax.optimization_barrier((*arrays, *others))[: len(arrays)]


def own_part(own):
    rows = own.shape[0] // (PARTS * 16) * 16
    chip, core = lax.axis_index("dp"), lax.axis_index("ctx") % 2
    left = own.shape[0] - PARTS * rows
    first = PARTS * rows
    if left > RANK:
        left //= SHARDS
        first += chip * left
    mine = lax.dynamic_slice_in_dim(own, (chip * 2 + core) * rows, rows, 0)
    return jnp.concatenate([mine, lax.dynamic_slice_in_dim(own, first, left, 0)], axis=0)


def eighth(own, moved):
    rows = own.shape[0] // (PARTS * 16) * 16
    return moved if own.shape[0] - PARTS * rows > RANK else moved[:rows]


def ring(sizes, moved):
    steps = []
    for _ in range(SHARDS - 1):
        moved = lax.ppermute(moved, "wt", ring_pairs(sizes["wt"]))
        steps.append(moved)
    return steps


def direct(sizes, moved):
    size = sizes["wt"]
    return [
        lax.ppermute(moved, "wt", [(i, (i + distance) % size) for i in range(size)])
        for distance in range(1, SHARDS)
    ]


def plane_start(sizes, mine):
    first, second = plane_pairs(sizes)
    return [mine, lax.ppermute(mine, ("dp", "ctx"), first), lax.ppermute(mine, ("dp", "ctx"), second)]


def plane_end(sizes, parts):
    _, second = plane_pairs(sizes)
    return [*parts, lax.ppermute(parts[1], ("dp", "ctx"), second)]


def swap_cores(sizes, parts):
    swap = swap_pairs(sizes["ctx"])
    return [*parts, *[lax.ppermute(part, "ctx", swap) for part in parts]]


def pad_thirds(array, features):
    pieces = []
    for third in range(3):
        piece = array[..., third * features : (third + 1) * features]
        pieces.append(jnp.pad(piece, [(0, 0)] * (array.ndim - 1) + [(0, PADDED - features)]))
    return jnp.concatenate(pieces, axis=-1)


def send_adapters(sizes, terms, chosen):
    flat = jnp.concatenate(
        [jnp.pad(term, ((0, 0), (0, -term.shape[1] % 128))) for term in terms], axis=1
    )
    flat = jnp.pad(flat, ((0, 0), (0, -flat.shape[1] % 256)))
    paired = sizes["ctx"] == 2
    if paired:
        half = flat.shape[1] // 2
        core = lax.axis_index("ctx")
        kept = lax.dynamic_slice_in_dim(flat, core * half, half, 1)
        given = lax.dynamic_slice_in_dim(flat, (1 - core) * half, half, 1)
        flat = kept + lax.ppermute(given, "ctx", swap_pairs(2))
    else:
        flat = lax.psum(flat, "ctx")
    ids = jnp.broadcast_to(chosen.astype(jnp.bfloat16), (RANK, 128))
    return jnp.concatenate([flat.astype(jnp.bfloat16), ids], axis=1)


def share_adapters(sent):
    return lax.all_gather(sent, ("dp", "wt"), axis=0)


def sequence_numbers(sizes, everyone):
    numbers = everyone[:, 0, -1].astype(jnp.int32)
    turned = lax.axis_index("ctx") if sizes["ctx"] == 2 else 0
    return jnp.concatenate([numbers, jnp.full((1,), turned, jnp.int32)])


def both_halves(sizes, everyone):
    if sizes["ctx"] != 2:
        return [everyone]
    return [everyone, lax.ppermute(everyone, "ctx", swap_pairs(2))]


def shards(
    sizes,
    tokens,
    cotangent,
    doc_lengths,
    adapter_ids,
    first_gain,
    first_shift,
    qkv_weight,
    qkv_bias,
    out_weight,
    out_bias,
    second_gain,
    second_shift,
    up_weight,
    up_bias,
    down_weight,
    down_bias,
    qkv_adapt_in,
    qkv_adapt_out,
    out_adapt_in,
    out_adapt_out,
    up_adapt_in,
    up_adapt_out,
    down_adapt_in,
    down_adapt_out,
):
    row_count, feature_count = tokens.shape[1:]
    ctx = sizes["ctx"]
    chosen = adapter_ids[0, 0]
    place = place_of(chosen)

    vectors = [first_gain, first_shift, qkv_bias, out_bias, second_gain, second_shift, up_bias, down_bias]
    lengths = [vector.shape[0] for vector in vectors]
    flat = jnp.concatenate(vectors)
    extra_rows = -(-flat.shape[0] // (3 * PADDED))
    flat = jnp.pad(flat, (0, extra_rows * 3 * PADDED - flat.shape[0])).reshape(extra_rows, -1)

    part_qkv = jnp.concatenate([pad_thirds(own_part(qkv_weight), feature_count), flat], axis=0)
    steps_qkv = ring(sizes, part_qkv)
    parts_qkv = []
    for step in steps_qkv:
        parts_qkv += swap_cores(sizes, plane_end(sizes, plane_start(sizes, eighth(qkv_weight, step))))
    own_qkv = pad_thirds(after(qkv_weight, steps_qkv[0]), feature_count)
    pieces_qkv = [own_qkv, *steps_qkv, *parts_qkv]
    values, adapter_qkv_out = after_all([tokens[0], qkv_adapt_out], steps_qkv[1])
    upstream = after(cotangent[0], steps_qkv[-1])
    adapter_qkv_out = pad_thirds(
        lax.dynamic_index_in_dim(adapter_qkv_out, chosen, 0, keepdims=False), feature_count
    )

    def stacked(own, steps):
        return jnp.stack([eighth(own, step) for step in steps])

    steps_out = direct(sizes, after(own_part(out_weight), steps_qkv[-1]))
    parts_out = plane_start(sizes, stacked(out_weight, steps_out))
    part_down = own_part(down_weight)
    folded = after(part_down.reshape(4, -1, feature_count), *steps_out)
    turn = partial(lax.ppermute, axis_name="wt", perm=ring_pairs(sizes["wt"]))

    by_distance = jnp.stack([flat] + [step[-extra_rows:] for step in steps_qkv])
    order = (lax.axis_index("wt") - jnp.arange(SHARDS)) % SHARDS
    by_shard = jnp.take(by_distance, order, axis=0).reshape(SHARDS, -1).astype(jnp.float32)
    vectors, start = [], 0
    for length in lengths:
        vectors.append(by_shard[:, start : start + length].reshape(1, -1))
        start += length
    gain_one, shift_one, bias_qkv, bias_out, gain_two, shift_two, bias_up, bias_down = vectors
    bias_qkv = pad_thirds(bias_qkv, feature_count)

    first_query = lax.axis_index("ctx") * row_count
    meta = jnp.concatenate([jnp.cumsum(doc_lengths[0])[:3], first_query[None]]).astype(jnp.int32)
    reach = -(-WINDOW // row_count)

    first_in, qkv_low, near = keys_call(
        place, after(values, upstream, *steps_out), gain_one, shift_one, bias_qkv, qkv_adapt_in, adapter_qkv_out, pieces_qkv
    )
    steps_down = [turn(folded)]
    *parts_out[1:], steps_down[0], near = after_all([*parts_out[1:], steps_down[0], near], near)

    far = jnp.concatenate([shifted(near, ctx, offset) for offset in range(reach, 0, -1)], axis=0)
    every_up = lax.all_gather(after(own_part(up_weight), steps_down[0]), "wt", axis=0)
    parts_out = plane_end(sizes, parts_out)
    steps_down.append(turn(steps_down[0]))
    queries = queries_call(
        place, after(first_in, parts_out[1], steps_down[0]), qkv_low, bias_qkv, adapter_qkv_out, pieces_qkv
    )
    *parts_out[3:], steps_down[1] = after_all([*parts_out[3:], steps_down[1]], queries)

    parts_out = swap_cores(sizes, parts_out)
    steps_down.append(turn(steps_down[1]))
    pairs = PAIRS // 2 + 1
    written = attend_forward(meta, after(queries, parts_out[3], steps_down[1]), far, near, 0, pairs)
    steps_down[2], *parts_out[4:] = after_all([steps_down[2], *parts_out[4:]], written[0])

    steps_down = [step.reshape(part_down.shape) for step in steps_down]
    parts_down = plane_start(sizes, stacked(down_weight, steps_down))
    mixed, logsums = attend_forward(
        meta, after(queries, steps_down[2]), far, near, pairs, PAIRS - pairs, written
    )
    *parts_down[1:], every_up = after_all([*parts_down[1:], every_up], mixed)

    parts_down = plane_end(sizes, parts_down)
    steps_up = [lax.dynamic_index_in_dim(every_up, place[k], 0, keepdims=False) for k in range(1, SHARDS)]
    parts_up = plane_start(sizes, stacked(up_weight, steps_up))
    pieces_out = [out_weight, *steps_out, *parts_out]
    hidden, second_in, out_low, up_low = out_call(
        place, values, after(mixed, *parts_down[1:3], every_up), gain_two, shift_two, bias_out, out_adapt_in,
        out_adapt_out, up_adapt_in, pieces_out,
    )
    parts_down[3] = after(parts_down[3], hidden)

    pieces_down = [down_weight, *steps_down, *swap_cores(sizes, parts_down)]
    written = active_grad_call(
        place, after(upstream, hidden), down_adapt_in, down_adapt_out, pieces_down, 0, 2
    )
    parts_up[1:] = after_all(parts_up[1:], written[0])
    parts_up = plane_end(sizes, parts_up)
    grad_active, grad_down_low = active_grad_call(
        place, after(upstream, *parts_up[1:3]), down_adapt_in, down_adapt_out, pieces_down, 2, 5, written
    )
    parts_up[3] = after(parts_up[3], grad_active)
    pieces_up = [up_weight, every_up, *swap_cores(sizes, parts_up)]
    active, grad_second, down_low, grad_up_out, grad_down_in = up_call(
        place, second_in, up_low, grad_active, grad_down_low, bias_up, up_adapt_out, down_adapt_in, pieces_up
    )
    grad_hidden, grad_mixed, grad_up_in, grad_out_out, grad_out_in, grad_down_out = out_grad_call(
        place, grad_second, hidden, second_in, upstream, mixed, out_low, down_low, gain_two,
        up_adapt_in, out_adapt_in, out_adapt_out, pieces_out,
    )
    terms = [grad_up_out, grad_down_in, grad_up_in, grad_out_out, grad_out_in, grad_down_out]
    widths = [(term.shape[1],) for term in terms]
    sent = send_adapters(sizes, terms, chosen)
    everyone = share_adapters(sent)
    near_grads, far_grads = attend_backward(meta, queries, far, near, after(grad_mixed, sent), mixed, logsums)
    everyone = after(everyone, near_grads)
    moved = 0
    for offset in range(reach, 0, -1):
        first_row = (reach - offset) * row_count
        moved += shifted(far_grads[:, first_row : first_row + row_count], ctx, -offset)
    halves = both_halves(sizes, everyone)
    numbers = sequence_numbers(sizes, everyone)
    grad_qkv_out = qkv_out_call(place, qkv_low, near_grads, moved)
    out_sent = send_adapters(sizes, [grad_qkv_out], chosen)
    out_everyone = share_adapters(out_sent)
    grad_input, grad_qkv_in = tokens_grad_call(
        place, values, first_in, grad_hidden, gain_one, qkv_adapt_in, adapter_qkv_out,
        after(near_grads, everyone, out_sent), moved, pieces_qkv,
    )
    in_sent = send_adapters(sizes, [grad_qkv_in], chosen)
    in_everyone = share_adapters(in_sent)
    numbers, active = after_all([numbers, active], in_sent)
    totals = combine_call(numbers, halves, widths)
    total_up_out, total_down_in, total_up_in, total_out_out, total_out_in, total_down_out = totals
    output = down_call(
        place, after(active, *totals), hidden, down_low, bias_down, down_adapt_out, pieces_down
    )
    out_halves = both_halves(sizes, after(out_everyone, output))
    in_halves = both_halves(sizes, after(in_everyone, output))
    total_qkv_out, = combine_call(numbers, out_halves, [(feature_count,) * 3])
    total_qkv_in, = combine_call(numbers, in_halves, [(feature_count,)])
    return (
        output.T[None],
        grad_input.T[None],
        total_qkv_in,
        total_qkv_out,
        total_out_in,
        total_out_out,
        total_up_in,
        total_up_out,
        total_down_in,
        total_down_out,
    )


def solution(mesh):
    return jax.shard_map(
        partial(shards, dict(mesh.shape)),
        mesh=mesh,
        in_specs=(
            P(("dp", "wt"), "ctx", None),
            P(("dp", "wt"), "ctx", None),
            P(("dp", "wt"), None),
            P(("dp", "wt"), None),
            P("wt"),
            P("wt"),
            P("wt", None),
            P("wt"),
            P("wt", None),
            P("wt"),
            P("wt"),
            P("wt"),
            P("wt", None),
            P("wt"),
            P("wt", None),
            P("wt"),
            P(),
            P(),
            P(),
            P(),
            P(),
            P(),
            P(),
            P(),
        ),
        out_specs=(
            P(("dp", "wt"), "ctx", None),
            P(("dp", "wt"), "ctx", None),
            P(),
            P(),
            P(),
            P(),
            P(),
            P(),
            P(),
            P(),
        ),
        check_vma=False,
    )
```
